32 devices in a mesh: dp: 8 (over z, x), tensor: 4 (over y, core).
Axes of the slice: x: 2, y: 2, z: 4, core: 2. Of those that a mesh axis runs over, the one named last changes fastest.
Arguments:
- tokens: bfloat16 [16384, 768], P(('dp', 'tensor')), may hold values from -6 to 6
- segment: int32 [16384], P(('dp', 'tensor')), may hold values from 0 to 512, as said below
- live: int32 [16384], P(('dp', 'tensor')), may hold values from 0 to 1, as said below
- mix_weight: bfloat16 [3, 768, 768], replicated, may hold values from -0.21875 to 0.21875
- out_weight: bfloat16 [768, 768], replicated, may hold values from -0.875 to 0.875
- position_table: bfloat16 [512, 768], replicated, may hold values from -6 to 6
- norm_gain: float32 [2, 768], replicated, may hold values from 0.5 to 1.5
- norm_bias: float32 [2, 768], replicated, may hold values from -1.5 to 1.5
- mix_left: bfloat16 [4, 768, 12], replicated, may hold values from -0.21875 to 0.21875
- mix_scale: float32 [4, 12], replicated, may hold values from -3 to 3
- mix_right: bfloat16 [4, 12, 768], replicated, may hold values from -1.75 to 1.75
- expand_weight: bfloat16 [768, 3072], P(None, 'tensor'), may hold values from -0.21875 to 0.21875
- expand_left: bfloat16 [768, 12], replicated, may hold values from -0.21875 to 0.21875
- expand_right: bfloat16 [12, 3072], P(None, 'tensor'), may hold values from -1.75 to 1.75
- shrink_weight: bfloat16 [3072, 768], P('tensor'), may hold values from -0.21875 to 0.21875
- shrink_left: bfloat16 [3072, 12], P('tensor'), may hold values from -0.21875 to 0.21875
- feed_scale: float32 [2, 12], replicated, may hold values from -3 to 3
- shrink_right: bfloat16 [12, 768], replicated, may hold values from -1.75 to 1.75
- cotangent: bfloat16 [16384, 768], P(('dp', 'tensor'))
Outputs:
- layer_out: bfloat16 [16384, 768], P(('dp', 'tensor'))
- grad_tokens: float32 [16384, 768], P(('dp', 'tensor'))
- grad_mix_left: float32 [4, 768, 12], replicated
- grad_mix_scale: float32 [4, 12], replicated
- grad_mix_right: float32 [4, 12, 768], replicated
- grad_expand_left: float32 [768, 12], replicated
- grad_expand_right: float32 [12, 3072], P(None, 'tensor')
- grad_shrink_left: float32 [3072, 12], P('tensor')
- grad_feed_scale: float32 [2, 12], replicated
- grad_shrink_right: float32 [12, 768], replicated
The draws below stay inside these ranges and needn't reach their ends.
Inputs may be any that keep to these rules, and one draw needn't show every extreme that they name: `segment`: within each aligned block of 512 slots (one device's slots) the live slots come first and their sequence numbers start at 0 and never fall; padding slots carry 512; some block holds a single sequence of 512 tokens. In each aligned block of 512 slots the live ones come first, at least 256 of them; some block is fully live.
All inputs are finite; a program needn't handle non-finite values.
Results may differ from the reference program's by a relative error of at most 0.023.
Values may be sent and summed in bfloat16 or wider, within the bound.
A program may use at most 192 MiB of HBM per device.

```python
import math
from functools import partial
import jax
import jax.numpy as jnp
from jax import lax

D = 768
HEADS = 12
HEAD_DIM = 64
FF = 3072
SPAN = 256
RANK = 12
ROWS_DEV = 512
TOKENS = 16384


def layout_rows(key):
    base_key = jax.random.fold_in(key, 7)
    key_lengths, key_counts, key_long, key_pick = jax.random.split(base_key, 4)
    blocks = TOKENS // ROWS_DEV
    lengths = jax.random.randint(key_lengths, (blocks, ROWS_DEV), 1, 64)
    bounds = jnp.cumsum(lengths, axis=1)
    places = jnp.arange(ROWS_DEV, dtype=jnp.int32)
    numbers = jnp.sum((bounds[:, None, :] <= places[None, :, None]).astype(jnp.int32), axis=2)
    live_counts = jax.random.randint(key_counts, (blocks,), ROWS_DEV // 2, ROWS_DEV + 1)
    block_ids = jnp.arange(blocks, dtype=jnp.int32)
    chosen = jax.random.randint(key_pick, (), 0, blocks)
    short_block = block_ids == (chosen + 1) % blocks
    long_block = ((jax.random.randint(key_long, (blocks,), 0, 4) == 0) | (block_ids == chosen)) & ~short_block
    live_counts = jnp.where(long_block, ROWS_DEV, jnp.where(short_block, ROWS_DEV // 2, live_counts))
    numbers = jnp.where(long_block[:, None], 0, numbers)
    alive = places[None, :] < live_counts[:, None]
    numbers = jnp.where(alive, numbers, ROWS_DEV)
    return (numbers.reshape(-1).astype(jnp.int32), alive.astype(jnp.int32).reshape(-1))


def draw_segment(key, part):
    return layout_rows(key)[0]


def draw_live(key, part):
    return layout_rows(key)[1]


def draw_cotangent(key, part):
    places = jnp.arange(TOKENS, dtype=jnp.float32)
    rising = 1.0 + 2.0 * places / (TOKENS - 1)
    base_values = jnp.clip(jax.random.normal(key, (TOKENS, D), jnp.float32), -4.0, 4.0)
    return (base_values * rising[:, None]).astype(jnp.bfloat16)


def steps_of(own_key, dims, cuts, least, largest):
    def one(dim, blocks):
        draws = jax.random.uniform(jax.random.fold_in(jax.random.fold_in(own_key, 6), dim), (blocks,), jnp.float32, least / len(cuts), largest / len(cuts))
        return jnp.repeat(jnp.exp(draws), dims[dim] // blocks).reshape((-1,) + (1,) * (len(dims) - dim - 1))

    loudness = one(*cuts[0])
    for cut in cuts[1:]:
        loudness = loudness * one(*cut)
    return loudness


def scatter_about(rng, dims, scale, limit, pieces=(), kind=jnp.bfloat16):
    drawn = scale * jax.random.normal(rng, dims, jnp.float32)
    if pieces:
        drawn = drawn * steps_of(rng, dims, pieces, -0.22, 0.18)
    return jnp.clip(drawn, -limit, limit).astype(kind)


def setup_inputs(seed: int = 0) -> dict:
    splits = jax.random.split(jax.random.key(seed), 20)
    tokens = scatter_about(splits[0], (TOKENS, D), 1.0, 6.0, ((0, 32),))
    segment = draw_segment(jax.random.fold_in(splits[19], 71), 0)
    live = draw_live(jax.random.fold_in(splits[19], 71), 0)
    mix_weight = scatter_about(splits[3], (3, D, D), D ** -0.5, 0.21875)
    out_weight = scatter_about(splits[4], (D, D), (D // 16) ** -0.5, 0.875)
    position_table = scatter_about(splits[5], (2 * SPAN, D), 1.0, 6.0)
    norm_gain = jnp.clip(1.0 + 0.1 * jax.random.normal(splits[6], (2, D), jnp.float32), 0.5, 1.5)
    norm_bias = scatter_about(splits[7], (2, D), 0.3, 1.5, (), jnp.float32)
    mix_left = scatter_about(splits[8], (4, D, RANK), D ** -0.5, 0.21875)
    mix_scale = scatter_about(splits[9], (4, RANK), 0.6, 3.0, (), jnp.float32)
    mix_right = scatter_about(splits[10], (4, RANK, D), RANK ** -0.5, 1.75)
    expand_weight = scatter_about(splits[11], (D, FF), D ** -0.5, 0.21875, ((1, 4),))
    expand_left = scatter_about(splits[12], (D, RANK), D ** -0.5, 0.21875)
    expand_right = scatter_about(splits[13], (RANK, FF), RANK ** -0.5, 1.75, ((1, 4),))
    shrink_weight = scatter_about(splits[14], (FF, D), (FF // 4) ** -0.5, 0.21875, ((0, 4),))
    shrink_left = scatter_about(splits[15], (FF, RANK), (FF // 4) ** -0.5, 0.21875, ((0, 4),))
    feed_scale = scatter_about(splits[16], (2, RANK), 0.6, 3.0, (), jnp.float32)
    shrink_right = scatter_about(splits[17], (RANK, D), RANK ** -0.5, 1.75)
    cotangent = draw_cotangent(jax.random.fold_in(splits[19], 71), 0)
    return {"tokens": tokens, "segment": segment, "live": live, "mix_weight": mix_weight, "out_weight": out_weight, "position_table": position_table, "norm_gain": norm_gain, "norm_bias": norm_bias, "mix_left": mix_left, "mix_scale": mix_scale, "mix_right": mix_right, "expand_weight": expand_weight, "expand_left": expand_left, "expand_right": expand_right, "shrink_weight": shrink_weight, "shrink_left": shrink_left, "feed_scale": feed_scale, "shrink_right": shrink_right, "cotangent": cotangent}


@jax.custom_vjp
def low(v):
    return lax.optimization_barrier(v.astype(jnp.bfloat16)).astype(jnp.float32)

@jax.custom_vjp
def low_back(v):
    return v

def low_keep(v):
    return (low(v), None)

def low_pass(kept, grad):
    return (grad,)

def back_keep(v):
    return (v, None)

def back_low(kept, grad):
    return (low(grad),)
low.defvjp(low_keep, low_pass)
low_back.defvjp(back_keep, back_low)
norm_eps = 1e-07
masked_fill = -1e+30

def product(left, right):
    return jnp.dot(left, right, precision=lax.Precision.HIGHEST, preferred_element_type=jnp.float32)

def adapted(inputs, weight, left_factor, scale_vector, right_factor):
    rank_values = low_back(product(inputs, left_factor))
    rank_low = low(rank_values * scale_vector)
    return product(inputs, weight) + product(rank_low, right_factor)

def layer_norm(values, gain, shift):
    center = values - lax.optimization_barrier(jnp.mean(values, axis=-1, keepdims=True))
    spread = lax.optimization_barrier(jnp.mean(center * center, axis=-1, keepdims=True))
    return center * lax.rsqrt(spread + norm_eps) * gain + shift

def relative_index(length):
    places = jnp.arange(length, dtype=jnp.int32)
    return (jnp.clip(places[:, None] - places[None, :], -SPAN, SPAN - 1) + SPAN).astype(jnp.int32)

def attend_block(pos_queries, pos_keys, block):
    queries, key_rows, values, segment, live = block
    length = queries.shape[0]
    places = jnp.arange(length, dtype=jnp.int32)
    offsets = jnp.broadcast_to(relative_index(length)[None], (HEADS, length, length))
    allowed = (segment[:, None] == segment[None, :]) & ((live[None, :] == 1) | (places[:, None] == places[None, :]))
    precision_setting = lax.Precision.HIGHEST
    per_head_queries = queries.reshape(length, HEADS, HEAD_DIM)
    per_head_keys = key_rows.reshape(length, HEADS, HEAD_DIM)
    head_values = values.reshape(length, HEADS, HEAD_DIM)
    position_query_rows = pos_queries.reshape(2 * SPAN, HEADS, HEAD_DIM)
    position_key_rows = pos_keys.reshape(2 * SPAN, HEADS, HEAD_DIM)
    content = jnp.einsum('ihd,jhd->hij', per_head_queries, per_head_keys, precision=precision_setting)
    query_position_scores = low_back(jnp.einsum('sbn,ybn->bsy', per_head_queries, position_key_rows, precision=precision_setting))
    key_position_scores = low_back(jnp.einsum('ysv,psv->syp', per_head_keys, position_query_rows, precision=precision_setting))
    along = jnp.take_along_axis(query_position_scores, offsets, axis=2)
    across = jnp.swapaxes(jnp.take_along_axis(key_position_scores, offsets, axis=2), 1, 2)
    logits = low_back((content + along + across) * (1.0 / math.sqrt(3.0 * HEAD_DIM)))
    logits = jnp.where(allowed[None], logits, masked_fill)
    peaks = lax.optimization_barrier(jnp.max(logits, axis=-1, keepdims=True))
    weights = jnp.exp(logits - peaks)
    shares = weights / lax.optimization_barrier(jnp.sum(weights, axis=-1, keepdims=True))
    context = jnp.einsum('hij,jhd->ihd', low(shares), head_values, precision=precision_setting)
    return context.reshape(length, HEADS * HEAD_DIM)

def forward(tokens, mix_left, mix_scale, mix_right, expand_left, expand_right, shrink_left, feed_scale, shrink_right, frozen):
    segment, live, mix_weight, out_weight, position_table, norm_gain, norm_bias, expand_weight, shrink_weight = frozen

    def project(inputs, which, weight):
        return adapted(inputs, weight, mix_left[which], mix_scale[which], mix_right[which])
    queries = low(low_back(project(tokens, 0, mix_weight[0])))
    key_rows = low(low_back(project(tokens, 1, mix_weight[1])))
    values = low(low_back(project(tokens, 2, mix_weight[2])))
    pos_queries = low(low_back(project(position_table, 0, mix_weight[0])))
    pos_keys = low(low_back(project(position_table, 1, mix_weight[1])))
    blocks = tokens.shape[0] // ROWS_DEV
    shaped = (queries.reshape(blocks, ROWS_DEV, D), key_rows.reshape(blocks, ROWS_DEV, D), values.reshape(blocks, ROWS_DEV, D), segment.reshape(blocks, ROWS_DEV), live.reshape(blocks, ROWS_DEV))
    context = lax.map(jax.checkpoint(partial(attend_block, pos_queries, pos_keys)), shaped)
    context = low(low_back(context.reshape(blocks * ROWS_DEV, D)))
    attended = low_back(project(context, 3, out_weight))
    normed = layer_norm(tokens + attended, norm_gain[0], norm_bias[0])
    hidden = low(normed)
    pre_act = low_back(adapted(hidden, expand_weight, expand_left, feed_scale[0], expand_right))
    active = low(jax.nn.gelu(pre_act, approximate=False))
    branch = low_back(adapted(active, shrink_weight, shrink_left, feed_scale[1], shrink_right))
    return layer_norm(normed + branch, norm_gain[1], norm_bias[1])

def widen(values):
    return values.astype(jnp.float32)

def reference(tokens, segment, live, mix_weight, out_weight, position_table, norm_gain, norm_bias, mix_left, mix_scale, mix_right, expand_weight, expand_left, expand_right, shrink_weight, shrink_left, feed_scale, shrink_right, cotangent):
    frozen = (segment, live, widen(mix_weight), widen(out_weight), widen(position_table), widen(norm_gain), widen(norm_bias), widen(expand_weight), widen(shrink_weight))
    trained = tuple((widen(element) for element in (tokens, mix_left, mix_scale, mix_right, expand_left, expand_right, shrink_left, feed_scale, shrink_right)))
    layer_out, pullback = jax.vjp(lambda *params: forward(*params, frozen), *trained)
    gradients = pullback(widen(cotangent))
    return (layer_out.astype(jnp.bfloat16), gradients[0], gradients[1], gradients[2], gradients[3], gradients[4], gradients[5], gradients[6], gradients[7], gradients[8])
```

```python
import math

import jax
import jax.numpy as jnp
from jax import lax
from jax.experimental import pallas as pl
from jax.experimental.pallas import tpu as pltpu
from jax.sharding import PartitionSpec as P

PAIRS = 6
LANES = 128
ROWS = 512
WIDTH = 768
RANK = 12
BLOCKS = ROWS // LANES

norm_eps = 1e-07
masked_fill = -1e30
score_scale = 1.0 / math.sqrt(192.0)
inverse_root_two = 1.0 / math.sqrt(2.0)
inverse_root_tau = 1.0 / math.sqrt(2.0 * math.pi)

f32 = jnp.float32
bf16 = jnp.bfloat16


def dot_nn(left, right):
    return jnp.dot(left, right, preferred_element_type=f32)


def dot_nt(left, right):
    return lax.dot_general(left, right, (((1,), (1,)), ((), ())), preferred_element_type=f32)


def dot_tn(left, right):
    return lax.dot_general(left, right, (((0,), (0,)), ((), ())), preferred_element_type=f32)


def column_of(row):
    n = row.shape[1]
    eye = lax.broadcasted_iota(jnp.int32, (n, n), 0) == lax.broadcasted_iota(jnp.int32, (n, n), 1)
    return jnp.sum(jnp.where(eye, row, 0.0), axis=1, keepdims=True)


def block_iotas():
    shape = (LANES, LANES)
    return lax.broadcasted_iota(jnp.int32, shape, 0), lax.broadcasted_iota(jnp.int32, shape, 1)


def head_mask(which):
    lane = lax.broadcasted_iota(jnp.int32, (1, LANES), 1)
    return ((lane >= 64) if which else (lane < 64)).astype(bf16)


def pick_tiles(scores, block, below):
    first = scores[:, :1]
    last = scores[:, ROWS - 1 :]
    rolled = pltpu.roll(scores, 1, 1, stride=1, stride_axis=0)
    tiles = []
    for other in range(BLOCKS):
        v = other - block + 2
        if v < 0:
            tile = jnp.broadcast_to(first, (LANES, LANES))
        elif v == 0:
            tile = jnp.where(below, first, rolled[:, :LANES])
        elif v < 4:
            tile = rolled[:, v * LANES : (v + 1) * LANES]
        elif v == 4:
            tile = jnp.where(below, rolled[:, :LANES], last)
        else:
            tile = jnp.broadcast_to(last, (LANES, LANES))
        tiles.append(tile)
    return tiles


def fold_rows(grads, block, below_rev, lane_first, lane_last):
    zero = jnp.zeros((LANES, LANES), f32)
    tile = [grads[:, b * LANES : (b + 1) * LANES] for b in range(BLOCKS)]
    placed = [zero, zero, zero, zero]
    low = None
    high = None
    for other in range(BLOCKS):
        v = other - block + 2
        if v < 0:
            low = tile[other] if low is None else low + tile[other]
        elif v == 0:
            placed[0] = jnp.where(below_rev, 0.0, tile[other])
            part = jnp.where(below_rev, tile[other], 0.0)
            low = part if low is None else low + part
        elif v < 4:
            placed[v] = tile[other]
        elif v == 4:
            placed[0] = jnp.where(below_rev, tile[other], 0.0)
            part = jnp.where(below_rev, 0.0, tile[other])
            high = part if high is None else high + part
        else:
            high = tile[other] if high is None else high + tile[other]
    rolled = pltpu.roll(
        jnp.concatenate(placed, axis=1), ROWS - LANES, 1, stride=1, stride_axis=0
    )
    out = [rolled[:, b * LANES : (b + 1) * LANES] for b in range(BLOCKS)]
    if low is not None:
        out[0] = out[0] + jnp.where(lane_first, jnp.sum(low, axis=1, keepdims=True), 0.0)
    if high is not None:
        out[3] = out[3] + jnp.where(lane_last, jnp.sum(high, axis=1, keepdims=True), 0.0)
    return jnp.concatenate(out, axis=1)


def attend_kernel(
    segment,
    live,
    tokens,
    table,
    mix_weight,
    left_t,
    right,
    scale,
    shares_out,
    q_s,
    k_s,
    v_s,
    tq_s,
    tk_s,
    tr_s,
    context_out,
    shares_s,
    bias_s,
    across_s,
    sems,
):
    row, lane = block_iotas()
    below = lane <= row
    flip = (row + lane == LANES - 1).astype(bf16)
    seg_row = segment[...]
    key_row = jnp.where(live[...] == 1, seg_row, -1)
    for a in range(BLOCKS):
        seg_col = jnp.broadcast_to(
            seg_row[:, a * LANES : (a + 1) * LANES].astype(f32), (LANES, LANES)
        ).T.astype(jnp.int32)
        for b in range(BLOCKS):
            same = seg_col == key_row[:, b * LANES : (b + 1) * LANES]
            if a == b:
                same = same | (row == lane)
            bias_s[a * LANES : (a + 1) * LANES, b * LANES : (b + 1) * LANES] = jnp.where(
                same, 0.0, masked_fill
            )
    for a in range(BLOCKS):
        tr_s[a * LANES : (a + 1) * LANES, :] = dot_nn(
            flip, table[(3 - a) * LANES : (4 - a) * LANES, :]
        ).astype(bf16)

    def project(source, which, target):
        rank_t = dot_nt(left_t[:, which, :], source)
        low_t = (rank_t * column_of(scale[which : which + 1, :])).astype(bf16)
        full = dot_nn(source, mix_weight[which]) + dot_tn(low_t, right[:, which, :])
        for p in range(PAIRS):
            target[p] = full[:, p * LANES : (p + 1) * LANES].astype(bf16)

    project(tokens[...], 0, q_s)
    project(tokens[...], 1, k_s)
    project(tokens[...], 2, v_s)
    project(tr_s[...], 0, tq_s)
    project(tr_s[...], 1, tk_s)

    def pair(p, carry):
        kp = k_s[p]
        tq = tq_s[p]
        tk = tk_s[p]
        context = [None] * BLOCKS
        for which in range(2):
            mask = head_mask(which)
            for b in range(BLOCKS):
                scores = dot_nt(k_s[p, b * LANES : (b + 1) * LANES, :] * mask, tq)
                tiles = pick_tiles(scores, b, below)
                for a in range(BLOCKS):
                    across_s[a * LANES : (a + 1) * LANES, b * LANES : (b + 1) * LANES] = tiles[a].T
            vm = v_s[p] * mask
            for a in range(BLOCKS):
                rows = slice(a * LANES, (a + 1) * LANES)
                qm = q_s[p, rows, :] * mask
                tiles = pick_tiles(dot_nt(qm, tk), a, below)
                total = (
                    dot_nt(qm, kp)
                    + jnp.concatenate(tiles, axis=1)
                    + across_s[rows, :]
                    + bias_s[rows, :]
                )
                peak = jnp.max(total, axis=1, keepdims=True)
                weights = jnp.exp((total - peak) * score_scale)
                inverse = 1.0 / jnp.sum(weights, axis=1, keepdims=True)
                low = (weights * inverse).astype(bf16)
                shares_s[p, which, rows, :] = low
                part = dot_nn(low, vm)
                context[a] = part if which == 0 else context[a] + part
        for a in range(BLOCKS):
            context_out[p, a * LANES : (a + 1) * LANES, :] = context[a].astype(bf16)
        pltpu.make_async_copy(shares_s.at[p], shares_out.at[p], sems.at[p]).start()
        return carry

    lax.fori_loop(0, PAIRS, pair, 0)

    def finish(p, carry):
        pltpu.make_async_copy(shares_s.at[p], shares_out.at[p], sems.at[p]).wait()
        return carry

    lax.fori_loop(0, PAIRS, finish, 0)


def vmem():
    return pl.BlockSpec(memory_space=pltpu.VMEM)


def attend(segment, live, tokens, table, mix_weight, left_t, right, scale):
    piece = jax.ShapeDtypeStruct((PAIRS, ROWS, LANES), bf16)
    return pl.pallas_call(
        attend_kernel,
        out_shape=(
            jax.ShapeDtypeStruct((PAIRS, 2, ROWS, ROWS), bf16),
            piece,
            piece,
            piece,
            piece,
            piece,
            jax.ShapeDtypeStruct((ROWS, WIDTH), bf16),
            piece,
        ),
        in_specs=[vmem()] * 8,
        out_specs=(pl.BlockSpec(memory_space=pl.ANY),) + (vmem(),) * 7,
        scratch_shapes=[
            pltpu.VMEM((PAIRS, 2, ROWS, ROWS), bf16),
            pltpu.VMEM((ROWS, ROWS), f32),
            pltpu.VMEM((ROWS, ROWS), f32),
            pltpu.SemaphoreType.DMA((PAIRS,)),
        ],
        compiler_params=pltpu.CompilerParams(vmem_limit_bytes=56 * 2**20),
        name="attend",
    )(segment, live, tokens, table, mix_weight, left_t, right, scale)


def norm_parts(values):
    center = values - jnp.mean(values, axis=-1, keepdims=True)
    root = lax.rsqrt(jnp.mean(center * center, axis=-1, keepdims=True) + norm_eps)
    return center * root, root


def norm_back(scaled, unit, root):
    return root * (
        scaled
        - jnp.mean(scaled, axis=-1, keepdims=True)
        - unit * jnp.mean(scaled * unit, axis=-1, keepdims=True)
    )


def feed_kernel(
    context,
    tokens,
    cotangent,
    out_weight,
    left_t,
    right,
    scale,
    gain,
    shift,
    expand,
    expand_left_t,
    expand_right,
    shrink,
    shrink_left_t,
    shrink_right,
    feed_scale,
    layer_out,
    grad_first_out,
    grad_context_out,
    out_left_grad,
    out_right_grad,
    expand_left_grad,
    shrink_right_grad,
    expand_right_grad,
    shrink_left_grad,
    scales_out,
    x_s,
    normed_s,
    hidden_s,
    act_s,
    slope_s,
    branch_s,
    context_s,
):
    chunks = expand.shape[0]
    wide = lax.broadcasted_iota(jnp.int32, (RANK, LANES), 1)
    lam_out = column_of(scale[3:4, :])
    lam_one = column_of(feed_scale[0:1, :])
    lam_two = column_of(feed_scale[1:2, :])
    step = LANES
    steps = ROWS // step

    for p in range(PAIRS):
        context_s[:, p * LANES : (p + 1) * LANES] = context[p]
    out_rank = dot_nt(left_t[:, 3, :], context_s[...])
    out_low = (out_rank * lam_out).astype(bf16)
    x_s[...] = dot_nn(context_s[...], out_weight[...]) + dot_tn(out_low, right[:, 3, :])

    def first_norm(i, carry):
        rows = pl.ds(i * step, step)
        values = tokens[rows, :].astype(f32) + x_s[rows, :]
        x_s[rows, :] = values
        unit, root = norm_parts(values)
        normed = unit * gain[0:1, :] + shift[0:1, :]
        normed_s[rows, :] = normed
        hidden_s[rows, :] = normed.astype(bf16)
        return carry

    lax.fori_loop(0, steps, first_norm, 0)

    one_rank = dot_nt(expand_left_t[...], hidden_s[...])
    one_low = (one_rank * lam_one).astype(bf16)
    branch_s[...] = jnp.zeros_like(branch_s)

    def forward(c, two_rank):
        pre = dot_nn(hidden_s[...], expand[c]) + dot_tn(one_low, expand_right[c])
        cdf = 0.5 + 0.5 * lax.erf(pre * inverse_root_two)
        act = (pre * cdf).astype(bf16)
        act_s[c] = act
        slope_s[c] = cdf + pre * jnp.exp(-0.5 * pre * pre) * inverse_root_tau
        branch_s[...] += dot_nn(act, shrink[c])
        return two_rank + dot_nt(shrink_left_t[c], act)

    two_rank = lax.fori_loop(0, chunks, forward, jnp.zeros((RANK, ROWS), f32))
    two_low = (two_rank * lam_two).astype(bf16)
    branch_s[...] += dot_tn(two_low, shrink_right[...])

    def second_norm(i, carry):
        rows = pl.ds(i * step, step)
        unit, root = norm_parts(normed_s[rows, :] + branch_s[rows, :])
        layer_out[rows, :] = (unit * gain[1:2, :] + shift[1:2, :]).astype(bf16)
        grad = norm_back(cotangent[rows, :].astype(f32) * gain[1:2, :], unit, root)
        branch_s[rows, :] = grad
        return carry

    lax.fori_loop(0, steps, second_norm, 0)
    grad_branch = branch_s[...].astype(bf16)
    two_back = dot_nt(shrink_right[...], grad_branch)
    two_small = (two_back * lam_two).astype(bf16)
    shrink_right_grad[...] = dot_nn(two_low, grad_branch)
    two_scale = jnp.sum(two_rank * two_back, axis=1, keepdims=True)

    def backward(c, one_back):
        grad_act = dot_nt(grad_branch, shrink[c]) + dot_tn(two_small, shrink_left_t[c])
        grad_pre = (grad_act * slope_s[c]).astype(bf16)
        shrink_left_grad[c] = dot_nn(two_small, act_s[c])
        expand_right_grad[c] = dot_nn(one_low, grad_pre)
        branch_s[...] += dot_nt(grad_pre, expand[c])
        return one_back + dot_nt(expand_right[c], grad_pre)

    one_back = lax.fori_loop(0, chunks, backward, jnp.zeros((RANK, ROWS), f32))
    one_small = (one_back * lam_one).astype(bf16)
    branch_s[...] += dot_tn(one_small, expand_left_t[...])
    expand_left_grad[...] = dot_nn(one_small, hidden_s[...])
    one_scale = jnp.sum(one_rank * one_back, axis=1, keepdims=True)

    def first_back(i, carry):
        rows = pl.ds(i * step, step)
        unit, root = norm_parts(x_s[rows, :])
        grad_first_out[rows, :] = norm_back(branch_s[rows, :] * gain[0:1, :], unit, root)
        return carry

    lax.fori_loop(0, steps, first_back, 0)
    grad_attended = grad_first_out[...].astype(bf16)
    out_back = dot_nt(right[:, 3, :], grad_attended)
    out_small = (out_back * lam_out).astype(bf16)
    grad_context_out[...] = (
        dot_nt(grad_attended, out_weight[...]) + dot_tn(out_small, left_t[:, 3, :])
    ).astype(bf16)
    out_left_grad[...] = dot_nn(out_small, context_s[...])
    out_right_grad[...] = dot_nn(out_low, grad_attended)
    out_scale = jnp.sum(out_rank * out_back, axis=1, keepdims=True)
    scales_out[...] = jnp.where(
        wide == 3,
        out_scale,
        jnp.where(wide == 4, one_scale, jnp.where(wide == 5, two_scale, 0.0)),
    )


def feed(*args):
    chunks, _, hidden = args[9].shape
    small = jax.ShapeDtypeStruct((RANK, WIDTH), f32)
    parts = jax.ShapeDtypeStruct((chunks, RANK, hidden), f32)
    return pl.pallas_call(
        feed_kernel,
        out_shape=(
            jax.ShapeDtypeStruct((ROWS, WIDTH), bf16),
            jax.ShapeDtypeStruct((ROWS, WIDTH), f32),
            jax.ShapeDtypeStruct((ROWS, WIDTH), bf16),
            small,
            small,
            small,
            small,
            parts,
            parts,
            jax.ShapeDtypeStruct((RANK, LANES), f32),
        ),
        in_specs=[vmem()] * 16,
        out_specs=(vmem(),) * 10,
        scratch_shapes=[
            pltpu.VMEM((ROWS, WIDTH), f32),
            pltpu.VMEM((ROWS, WIDTH), f32),
            pltpu.VMEM((ROWS, WIDTH), bf16),
            pltpu.VMEM((chunks, ROWS, hidden), bf16),
            pltpu.VMEM((chunks, ROWS, hidden), f32),
            pltpu.VMEM((ROWS, WIDTH), f32),
            pltpu.VMEM((ROWS, WIDTH), bf16),
        ],
        compiler_params=pltpu.CompilerParams(vmem_limit_bytes=58 * 2**20),
        name="feed",
    )(*args)


def back_kernel(
    grad_context,
    grad_first,
    shares_in,
    q_s,
    k_s,
    v_s,
    tq_s,
    tk_s,
    tr_s,
    tokens,
    mix_weight,
    left_t,
    right,
    scale,
    grad_tokens,
    left_grad,
    right_grad,
    scales_out,
    shares_s,
    gl_s,
    qf_s,
    kf_s,
    fq_s,
    fk_s,
    gq_s,
    gk_s,
    gv_t,
    gtq_t,
    gtk_t,
    sems,
):
    row, lane = block_iotas()
    below_rev = lane + row <= LANES - 1
    lane_first = lane == 0
    lane_last = lane == LANES - 1
    flip = (row + lane == LANES - 1).astype(bf16)

    def begin(p, carry):
        pltpu.make_async_copy(shares_in.at[p], shares_s.at[p], sems.at[p]).start()
        return carry

    lax.fori_loop(0, PAIRS, begin, 0)

    def flipped(values):
        return jnp.concatenate(
            [
                dot_nn(flip, values[b * LANES : (b + 1) * LANES, :]).astype(bf16)
                for b in range(BLOCKS)
            ],
            axis=0,
        )

    def pair(p, carry):
        pltpu.make_async_copy(shares_in.at[p], shares_s.at[p], sems.at[p]).wait()
        gc = grad_context[p]
        gc_t = gc.T
        q_rev_t = flipped(q_s[p]).T
        k_rev_t = flipped(k_s[p]).T
        vp = v_s[p]
        gq = None
        gk = None
        for which in range(2):
            mask = head_mask(which)
            half = slice(which * 64, which * 64 + 64)
            for a in range(BLOCKS):
                rows = slice(a * LANES, (a + 1) * LANES)
                shares = shares_s[p, which, rows, :].astype(f32)
                grad = dot_nt(gc[rows, :] * mask, vp)
                prod = grad * shares
                inner = jnp.sum(prod, axis=1, keepdims=True)
                gl_s[rows, :] = (prod - shares * inner).astype(bf16)
            for a in range(BLOCKS):
                rows = slice(a * LANES, (a + 1) * LANES)
                along = dot_nn(flip, gl_s[rows, :])
                qf_s[rows, :] = along.astype(bf16)
                fq_s[rows, :] = (
                    fold_rows(along, a, below_rev, lane_first, lane_last) * score_scale
                ).astype(bf16)
                across = dot_nt(flip, gl_s[:, rows])
                kf_s[rows, :] = across.astype(bf16)
                fk_s[rows, :] = (
                    fold_rows(across, a, below_rev, lane_first, lane_last) * score_scale
                ).astype(bf16)
            fq = fq_s[...]
            fk = fk_s[...]
            part_q = dot_nn(qf_s[...], k_s[p] * mask) * score_scale + dot_nn(fq, tk_s[p] * mask)
            part_k = dot_nn(kf_s[...], q_s[p] * mask) * score_scale + dot_nn(fk, tq_s[p] * mask)
            gq = part_q if which == 0 else gq + part_q
            gk = part_k if which == 0 else gk + part_k
            out = pl.ds(pl.multiple_of(p * LANES + which * 64, 64), 64)
            gv_t[out, :] = dot_nn(gc_t[half, :], shares_s[p, which]).astype(bf16)
            gtk_t[out, :] = dot_nn(q_rev_t[half, :], fq).astype(bf16)
            gtq_t[out, :] = dot_nn(k_rev_t[half, :], fk).astype(bf16)
        gq_s[p] = flipped(gq.astype(bf16))
        gk_s[p] = flipped(gk.astype(bf16))
        return carry

    lax.fori_loop(0, PAIRS, pair, 0)

    wide = lax.broadcasted_iota(jnp.int32, (RANK, LANES), 1)
    total = grad_first[...]
    scales = jnp.zeros((RANK, LANES), f32)
    source = tokens[...]
    for which in range(3):
        if which == 2:
            grad = gv_t[...].T
        else:
            grad = jnp.concatenate([(gq_s, gk_s)[which][p] for p in range(PAIRS)], axis=1)
        left = left_t[:, which, :]
        lam = column_of(scale[which : which + 1, :])
        rank = dot_nt(left, source)
        low = (rank * lam).astype(bf16)
        back = dot_nt(right[:, which, :], grad)
        small = (back * lam).astype(bf16)
        total = total + dot_nt(grad, mix_weight[which]) + dot_tn(small, left)
        left_sum = dot_nn(small, source)
        right_sum = dot_nn(low, grad)
        scale_sum = jnp.sum(rank * back, axis=1, keepdims=True)
        if which < 2:
            table_grad = (gtq_t, gtk_t)[which][...]
            rank = dot_nt(left, tr_s[...])
            low = (rank * lam).astype(bf16)
            back = dot_nn(right[:, which, :], table_grad)
            small = (back * lam).astype(bf16)
            left_sum = left_sum + dot_nn(small, tr_s[...])
            right_sum = right_sum + dot_nt(low, table_grad)
            scale_sum = scale_sum + jnp.sum(rank * back, axis=1, keepdims=True)
        left_grad[which] = left_sum
        right_grad[which] = right_sum
        scales = jnp.where(wide == which, scale_sum, scales)
    grad_tokens[...] = total
    scales_out[...] = scales


def back(*args):
    sums = jax.ShapeDtypeStruct((3, RANK, WIDTH), f32)
    return pl.pallas_call(
        back_kernel,
        out_shape=(
            jax.ShapeDtypeStruct((ROWS, WIDTH), f32),
            sums,
            sums,
            jax.ShapeDtypeStruct((RANK, LANES), f32),
        ),
        in_specs=[vmem(), vmem(), pl.BlockSpec(memory_space=pl.ANY)] + [vmem()] * 11,
        out_specs=(vmem(),) * 4,
        scratch_shapes=[
            pltpu.VMEM((PAIRS, 2, ROWS, ROWS), bf16),
            pltpu.VMEM((ROWS, ROWS), bf16),
            pltpu.VMEM((ROWS, ROWS), bf16),
            pltpu.VMEM((ROWS, ROWS), bf16),
            pltpu.VMEM((ROWS, ROWS), bf16),
            pltpu.VMEM((ROWS, ROWS), bf16),
            pltpu.VMEM((PAIRS, ROWS, LANES), bf16),
            pltpu.VMEM((PAIRS, ROWS, LANES), bf16),
            pltpu.VMEM((WIDTH, ROWS), bf16),
            pltpu.VMEM((WIDTH, ROWS), bf16),
            pltpu.VMEM((WIDTH, ROWS), bf16),
            pltpu.SemaphoreType.DMA((PAIRS,)),
        ],
        compiler_params=pltpu.CompilerParams(vmem_limit_bytes=58 * 2**20),
        name="back",
    )(*args)


def body(
    tokens,
    segment,
    live,
    mix_weight,
    out_weight,
    position_table,
    norm_gain,
    norm_bias,
    mix_left,
    mix_scale,
    mix_right,
    expand_weight,
    expand_left,
    expand_right,
    shrink_weight,
    shrink_left,
    feed_scale,
    shrink_right,
    cotangent,
):
    left_t = jnp.transpose(mix_left, (2, 0, 1))
    right = jnp.transpose(mix_right, (1, 0, 2))
    expand_all = lax.all_gather(expand_weight, "tensor")
    shrink_all = lax.all_gather(shrink_weight, "tensor")
    small_all = lax.all_gather(jnp.stack([expand_right, shrink_left.T]), "tensor")
    shares, q, k, v, tq, tk, tr, context = attend(
        segment.reshape(1, ROWS),
        live.reshape(1, ROWS),
        tokens,
        position_table,
        mix_weight,
        left_t,
        right,
        mix_scale,
    )
    (
        layer_out,
        grad_first,
        grad_context,
        out_left_g,
        out_right_g,
        expand_left_g,
        shrink_right_g,
        expand_right_g,
        shrink_left_g,
        feed_scales,
    ) = feed(
        context,
        tokens,
        cotangent,
        out_weight,
        left_t,
        right,
        mix_scale,
        norm_gain,
        norm_bias,
        expand_all,
        expand_left.T,
        small_all[:, 0],
        shrink_all,
        small_all[:, 1],
        shrink_right,
        feed_scale,
    )
    grad_pieces = jnp.transpose(grad_context.reshape(ROWS, PAIRS, LANES), (1, 0, 2))
    grad_tokens, left_g, right_g, mix_scales = back(
        grad_pieces,
        grad_first,
        shares,
        q,
        k,
        v,
        tq,
        tk,
        tr,
        tokens,
        mix_weight,
        left_t,
        right,
        mix_scale,
    )
    left_g = jnp.concatenate([left_g, out_left_g[None]])
    right_g = jnp.concatenate([right_g, out_right_g[None]])
    scales = feed_scales + mix_scales
    left_g, right_g, scales, expand_left_g, shrink_right_g, expand_right_g, shrink_left_g = lax.psum(
        (
            left_g,
            right_g,
            scales,
            expand_left_g,
            shrink_right_g,
            expand_right_g,
            shrink_left_g,
        ),
        ("dp", "tensor"),
    )
    me = lax.axis_index("tensor")
    return (
        layer_out,
        grad_tokens,
        jnp.transpose(left_g, (0, 2, 1)),
        scales[:, :4].T,
        right_g,
        expand_left_g.T,
        lax.dynamic_index_in_dim(expand_right_g, me, 0, keepdims=False),
        lax.dynamic_index_in_dim(shrink_left_g, me, 0, keepdims=False).T,
        scales[:, 4:6].T,
        shrink_right_g,
    )


def solution(mesh):
    rows = P(("dp", "tensor"), None)
    line = P(("dp", "tensor"))
    return jax.shard_map(
        body,
        mesh=mesh,
        in_specs=(
            rows,
            line,
            line,
            P(),
            P(),
            P(),
            P(),
            P(),
            P(),
            P(),
            P(),
            P(None, "tensor"),
            P(),
            P(None, "tensor"),
            P("tensor", None),
            P("tensor", None),
            P(),
            P(),
            rows,
        ),
        out_specs=(
            rows,
            rows,
            P(),
            P(),
            P(),
            P(),
            P(None, "tensor"),
            P("tensor", None),
            P(),
            P(),
        ),
        check_vma=False,
    )
```

```python
import math

import jax
import jax.numpy as jnp
from jax import lax
from jax.experimental import pallas as pl
from jax.experimental.pallas import tpu as pltpu
from jax.sharding import PartitionSpec as P

PAIRS = 6
LANES = 128
ROWS = 512
WIDTH = 768
RANK = 12
BLOCKS = ROWS // LANES
TILE = 16
SPLIT_AT = 25

norm_eps = 1e-07
masked_fill = -1e30
score_scale = 1.0 / math.sqrt(192.0)
inverse_root_two = 1.0 / math.sqrt(2.0)
inverse_root_tau = 1.0 / math.sqrt(2.0 * math.pi)

f32 = jnp.float32
bf16 = jnp.bfloat16


def dot_nn(left, right):
    return jnp.dot(left, right, preferred_element_type=f32)


def dot_nt(left, right):
    return lax.dot_general(left, right, (((1,), (1,)), ((), ())), preferred_element_type=f32)


def dot_tn(left, right):
    return lax.dot_general(left, right, (((0,), (0,)), ((), ())), preferred_element_type=f32)


def column_of(row):
    n = row.shape[1]
    eye = lax.broadcasted_iota(jnp.int32, (n, n), 0) == lax.broadcasted_iota(jnp.int32, (n, n), 1)
    return jnp.sum(jnp.where(eye, row, 0.0), axis=1, keepdims=True)


def block_iotas():
    shape = (LANES, LANES)
    return lax.broadcasted_iota(jnp.int32, shape, 0), lax.broadcasted_iota(jnp.int32, shape, 1)


def head_mask(which):
    lane = lax.broadcasted_iota(jnp.int32, (1, LANES), 1)
    return ((lane >= 64) if which else (lane < 64)).astype(bf16)


def pick_tiles(scores, block, below):
    first = scores[:, :1]
    last = scores[:, ROWS - 1 :]
    rolled = pltpu.roll(scores, 1, 1, stride=1, stride_axis=0)
    tiles = []
    for other in range(BLOCKS):
        v = other - block + 2
        if v < 0:
            tile = jnp.broadcast_to(first, (LANES, LANES))
        elif v == 0:
            tile = jnp.where(below, first, rolled[:, :LANES])
        elif v < 4:
            tile = rolled[:, v * LANES : (v + 1) * LANES]
        elif v == 4:
            tile = jnp.where(below, rolled[:, :LANES], last)
        else:
            tile = jnp.broadcast_to(last, (LANES, LANES))
        tiles.append(tile)
    return tiles


def fold_rows(grads, block, below_rev, lane_first, lane_last):
    zero = jnp.zeros((LANES, LANES), f32)
    tile = [grads[:, b * LANES : (b + 1) * LANES] for b in range(BLOCKS)]
    placed = [zero, zero, zero, zero]
    low = None
    high = None
    for other in range(BLOCKS):
        v = other - block + 2
        if v < 0:
            low = tile[other] if low is None else low + tile[other]
        elif v == 0:
            placed[0] = jnp.where(below_rev, 0.0, tile[other])
            part = jnp.where(below_rev, tile[other], 0.0)
            low = part if low is None else low + part
        elif v < 4:
            placed[v] = tile[other]
        elif v == 4:
            placed[0] = jnp.where(below_rev, tile[other], 0.0)
            part = jnp.where(below_rev, 0.0, tile[other])
            high = part if high is None else high + part
        else:
            high = tile[other] if high is None else high + tile[other]
    rolled = pltpu.roll(
        jnp.concatenate(placed, axis=1), ROWS - LANES, 1, stride=1, stride_axis=0
    )
    out = [rolled[:, b * LANES : (b + 1) * LANES] for b in range(BLOCKS)]
    if low is not None:
        out[0] = out[0] + jnp.where(lane_first, jnp.sum(low, axis=1, keepdims=True), 0.0)
    if high is not None:
        out[3] = out[3] + jnp.where(lane_last, jnp.sum(high, axis=1, keepdims=True), 0.0)
    return jnp.concatenate(out, axis=1)


def attend_kernel(
    segment,
    live,
    tokens,
    table,
    mix_weight,
    left_t,
    right,
    scale,
    expand,
    shrink,
    expand_right,
    shrink_left_t,
    shares_out,
    expand_all,
    shrink_all,
    expand_right_all,
    shrink_left_all,
    q_s,
    k_s,
    v_s,
    tq_s,
    tk_s,
    tr_s,
    context_out,
    shares_s,
    bias_s,
    across_s,
    sems,
    *gather_sems,
):
    gather = Gather(
        expand_all.shape[0],
        (expand, shrink, expand_right, shrink_left_t),
        (expand_all, shrink_all, expand_right_all, shrink_left_all),
        gather_sems,
    )
    gather.start()
    row, lane = block_iotas()
    below = lane <= row
    flip = (row + lane == LANES - 1).astype(bf16)
    seg_row = segment[...]
    key_row = jnp.where(live[...] == 1, seg_row, -1)
    for a in range(BLOCKS):
        seg_col = jnp.broadcast_to(
            seg_row[:, a * LANES : (a + 1) * LANES].astype(f32), (LANES, LANES)
        ).T.astype(jnp.int32)
        for b in range(BLOCKS):
            same = seg_col == key_row[:, b * LANES : (b + 1) * LANES]
            if a == b:
                same = same | (row == lane)
            bias_s[a * LANES : (a + 1) * LANES, b * LANES : (b + 1) * LANES] = jnp.where(
                same, 0.0, masked_fill
            )
    for a in range(BLOCKS):
        tr_s[a * LANES : (a + 1) * LANES, :] = dot_nn(
            flip, table[(3 - a) * LANES : (4 - a) * LANES, :]
        ).astype(bf16)

    def project(source, which, target):
        rank_t = dot_nt(left_t[:, which, :], source)
        low_t = (rank_t * column_of(scale[which : which + 1, :])).astype(bf16)
        full = dot_nn(source, mix_weight[which]) + dot_tn(low_t, right[:, which, :])
        for p in range(PAIRS):
            target[p] = full[:, p * LANES : (p + 1) * LANES].astype(bf16)

    project(tokens[...], 0, q_s)
    project(tokens[...], 1, k_s)
    project(tokens[...], 2, v_s)
    project(tr_s[...], 0, tq_s)
    project(tr_s[...], 1, tk_s)

    def pair(p, carry):
        for k in range(6):

            @pl.when(p == k)
            def _():
                gather.forward_one(k)
                if k:
                    gather.forward_two(k - 1)

        kp = k_s[p]
        tq = tq_s[p]
        tk = tk_s[p]
        context = [None] * BLOCKS
        for which in range(2):
            mask = head_mask(which)
            for b in range(BLOCKS):
                scores = dot_nt(k_s[p, b * LANES : (b + 1) * LANES, :] * mask, tq)
                tiles = pick_tiles(scores, b, below)
                for a in range(BLOCKS):
                    across_s[a * LANES : (a + 1) * LANES, b * LANES : (b + 1) * LANES] = tiles[a].T
            vm = v_s[p] * mask
            for a in range(BLOCKS):
                rows = slice(a * LANES, (a + 1) * LANES)
                qm = q_s[p, rows, :] * mask
                tiles = pick_tiles(dot_nt(qm, tk), a, below)
                total = (
                    dot_nt(qm, kp)
                    + jnp.concatenate(tiles, axis=1)
                    + across_s[rows, :]
                    + bias_s[rows, :]
                )
                peak = jnp.max(total, axis=1, keepdims=True)
                weights = jnp.exp((total - peak) * score_scale)
                inverse = 1.0 / jnp.sum(weights, axis=1, keepdims=True)
                low = (weights * inverse).astype(bf16)
                shares_s[p, which, rows, :] = low
                part = dot_nn(low, vm)
                context[a] = part if which == 0 else context[a] + part
        for a in range(BLOCKS):
            context_out[p, a * LANES : (a + 1) * LANES, :] = context[a].astype(bf16)
        pltpu.make_async_copy(shares_s.at[p], shares_out.at[p], sems.at[p]).start()
        return carry

    lax.fori_loop(0, PAIRS, pair, 0)
    gather.forward_two(5)
    gather.finish()

    def finish(p, carry):
        pltpu.make_async_copy(shares_s.at[p], shares_out.at[p], sems.at[p]).wait()
        return carry

    lax.fori_loop(0, PAIRS, finish, 0)


def vmem():
    return pl.BlockSpec(memory_space=pltpu.VMEM)


def anywhere():
    return pl.BlockSpec(memory_space=pl.ANY)


def remote(source, target, send, recv, device):
    return pltpu.make_async_remote_copy(
        src_ref=source,
        dst_ref=target,
        send_sem=send,
        recv_sem=recv,
        device_id=device,
        device_id_type=pl.DeviceIdType.MESH,
    )


def greet(devices):
    barrier = pltpu.get_barrier_semaphore()
    for device in devices:
        pl.semaphore_signal(
            barrier, inc=1, device_id=device, device_id_type=pl.DeviceIdType.MESH
        )
    pl.semaphore_wait(barrier, len(devices))


class Groups:
    def __init__(self, tensor_size, dp_size):
        self.near_size = tensor_size * 2
        self.far_size = dp_size // 2
        self.tensor = lax.axis_index("tensor")
        self.dp = lax.axis_index("dp")
        self.near = self.tensor * 2 + self.dp % 2
        self.far = self.dp // 2

    def near_index(self, step):
        return (self.near + step) % self.near_size

    def near_device(self, step):
        index = self.near_index(step)
        return {"dp": self.far * 2 + index % 2, "tensor": index // 2}

    def far_device(self, step):
        index = (self.far + step) % self.far_size
        return {"dp": index * 2 + self.dp % 2, "tensor": self.tensor}

    def partners(self):
        return [self.near_device(s) for s in range(1, self.near_size)] + [
            self.far_device(s) for s in range(1, self.far_size)
        ]


class Reduction:
    def __init__(self, groups, pack, arrived, crossed, out, sems):
        self.groups = groups
        self.pack = pack
        self.arrived = arrived
        self.crossed = crossed
        self.out = out
        self.send_one, self.recv_one, self.send_two, self.recv_two, self.send_three, self.recv_three = sems
        self.size = pack.shape[0] // groups.near_size

    def part(self, ref, index):
        return ref.at[pl.ds(index * self.size, self.size)]

    def scatter(self):
        g = self.groups
        return [
            remote(
                self.part(self.pack, g.near_index(s)),
                self.arrived.at[s - 1],
                self.send_one.at[s - 1],
                self.recv_one.at[s - 1],
                g.near_device(s),
            )
            for s in range(1, g.near_size)
        ]

    def cross(self):
        g = self.groups
        return [
            remote(
                self.crossed.at[g.far],
                self.crossed.at[g.far],
                self.send_two.at[s - 1],
                self.recv_two.at[s - 1],
                g.far_device(s),
            )
            for s in range(1, g.far_size)
        ]

    def gather(self):
        g = self.groups
        return [
            remote(
                self.part(self.out, g.near),
                self.part(self.out, g.near),
                self.send_three.at[s - 1],
                self.recv_three.at[s - 1],
                g.near_device(s),
            )
            for s in range(1, g.near_size)
        ]

    def start(self):
        for copy in self.scatter():
            copy.start()

    def middle(self):
        g = self.groups
        for copy in self.scatter():
            copy.wait()
        total = self.pack[pl.ds(g.near * self.size, self.size)].astype(f32)
        for s in range(1, g.near_size):
            total = total + self.arrived[s - 1].astype(f32)
        self.crossed[g.far] = total.astype(self.crossed.dtype)
        for copy in self.cross():
            copy.start()

    def last(self):
        g = self.groups
        for copy in self.cross():
            copy.wait()
        total = self.crossed[0].astype(f32)
        for s in range(1, g.far_size):
            total = total + self.crossed[s].astype(f32)
        self.out[pl.ds(g.near * self.size, self.size)] = total.astype(self.out.dtype)
        for copy in self.gather():
            copy.start()

    def finish(self):
        for copy in self.gather():
            copy.wait()


def reduction_scratch(tiles, near_size, far_size, kind):
    size = tiles // near_size
    near = (near_size - 1,)
    far = (max(far_size - 1, 1),)
    dma = pltpu.SemaphoreType.DMA
    return [
        pltpu.VMEM((near_size - 1, size, TILE, LANES), kind),
        pltpu.VMEM((far_size, size, TILE, LANES), kind),
        dma(near),
        dma(near),
        dma(far),
        dma(far),
        dma(near),
        dma(near),
    ]


class Gather:
    def __init__(self, size, sources, targets, sems):
        self.size = size
        self.far = size // 2
        self.sources = sources
        self.targets = targets
        self.across_s, self.across_r, self.pair_s, self.pair_r, self.one_s, self.one_r, self.two_s, self.two_r = sems[:8]
        self.whole_s, self.whole_r, self.small_s, self.small_r, self.own = sems[8:]
        self.tensor = lax.axis_index("tensor")
        self.dp = lax.axis_index("dp")
        self.bit = self.dp % 2
        self.pair = {"dp": self.dp + 1 - 2 * self.bit, "tensor": self.tensor}
        core = self.tensor % 2
        self.core = {"dp": self.dp, "tensor": self.tensor + 1 - 2 * core}

    def device(self, step):
        return {"dp": self.dp, "tensor": (self.tensor + step) % self.size}

    def partners(self):
        return [self.device(s) for s in range(1, self.size)] + [self.pair]

    def rows(self, which, part, bit):
        count = self.sources[which].shape[0] // 6
        return pl.ds((2 * part + bit) * count, count)

    def across(self, s, k):
        which, part = k // 3, k % 3
        rows = self.rows(which, part, self.bit)
        return remote(
            self.sources[which].at[rows, :],
            self.targets[which].at[self.tensor, rows, :],
            self.across_s.at[s - 1, k],
            self.across_r.at[s - 1, k],
            self.device(2 * s),
        )

    def onward(self, s, k, bit, sends, recvs, device):
        which, part = k // 3, k % 3
        rows = self.rows(which, part, bit)
        slot = (self.tensor + self.size - 2 * s) % self.size
        ref = self.targets[which].at[slot, rows, :]
        return remote(ref, ref, sends.at[s - 1, k], recvs.at[s - 1, k], device)

    def swap(self, s, k):
        return self.onward(s, k, self.bit, self.pair_s, self.pair_r, self.pair)

    def share_one(self, s, k):
        return self.onward(s, k, self.bit, self.one_s, self.one_r, self.core)

    def share_two(self, s, k):
        return self.onward(s, k, 1 - self.bit, self.two_s, self.two_r, self.core)

    def whole(self, which):
        return remote(
            self.sources[which],
            self.targets[which].at[self.tensor],
            self.whole_s.at[which],
            self.whole_r.at[which],
            self.core,
        )

    def small(self, s, which):
        return remote(
            self.sources[which],
            self.targets[which].at[self.tensor],
            self.small_s.at[s - 1, which - 2],
            self.small_r.at[s - 1, which - 2],
            self.device(s),
        )

    def keep(self, which):
        return pltpu.make_async_copy(
            self.sources[which], self.targets[which].at[self.tensor], self.own.at[which - 2]
        )

    def start(self):
        greet(self.partners())
        for k in range(6):
            for s in range(1, self.far):
                self.across(s, k).start()
        for which in range(2):
            self.whole(which).start()
        for s in range(1, self.size):
            for which in (2, 3):
                self.small(s, which).start()
        for which in (2, 3):
            self.keep(which).start()

    def forward_one(self, k):
        for s in range(1, self.far):
            self.across(s, k).wait_recv()
            self.swap(s, k).start()
            self.share_one(s, k).start()

    def forward_two(self, k):
        for s in range(1, self.far):
            self.swap(s, k).wait_recv()
            self.share_two(s, k).start()

    def finish(self):
        for s in range(1, self.far):
            for k in range(6):
                self.across(s, k).wait_send()
                self.swap(s, k).wait_send()
                self.share_one(s, k).wait()
                self.share_two(s, k).wait()
        for which in range(2):
            self.whole(which).wait()
        for s in range(1, self.size):
            for which in (2, 3):
                self.small(s, which).wait()
        for which in (2, 3):
            self.keep(which).wait()


def attend(size, *args):
    piece = jax.ShapeDtypeStruct((PAIRS, ROWS, LANES), bf16)
    dma = pltpu.SemaphoreType.DMA
    steps = (max(size // 2 - 1, 1), 6)
    return pl.pallas_call(
        attend_kernel,
        out_shape=(jax.ShapeDtypeStruct((PAIRS, 2, ROWS, ROWS), bf16),)
        + tuple(jax.ShapeDtypeStruct((size,) + array.shape, bf16) for array in args[8:])
        + (
            piece,
            piece,
            piece,
            piece,
            piece,
            jax.ShapeDtypeStruct((ROWS, WIDTH), bf16),
            piece,
        ),
        in_specs=[vmem()] * 8 + [anywhere()] * 4,
        out_specs=(anywhere(),) * 5 + (vmem(),) * 7,
        scratch_shapes=[
            pltpu.VMEM((PAIRS, 2, ROWS, ROWS), bf16),
            pltpu.VMEM((ROWS, ROWS), f32),
            pltpu.VMEM((ROWS, ROWS), f32),
            dma((PAIRS,)),
        ]
        + [dma(steps)] * 8
        + [dma((2,))] * 2
        + [dma((size - 1, 2))] * 2
        + [dma((2,))],
        compiler_params=pltpu.CompilerParams(
            vmem_limit_bytes=56 * 2**20, collective_id=0, has_side_effects=True
        ),
        name="attend",
    )(*args)


def norm_parts(values):
    center = values - jnp.mean(values, axis=-1, keepdims=True)
    root = lax.rsqrt(jnp.mean(center * center, axis=-1, keepdims=True) + norm_eps)
    return center * root, root


def norm_back(scaled, unit, root):
    return root * (
        scaled
        - jnp.mean(scaled, axis=-1, keepdims=True)
        - unit * jnp.mean(scaled * unit, axis=-1, keepdims=True)
    )


def feed_kernel(
    context,
    tokens,
    cotangent,
    out_weight,
    left_t,
    right,
    scale,
    gain,
    shift,
    expand,
    expand_left_t,
    expand_right,
    shrink,
    shrink_left_t,
    shrink_right,
    feed_scale,
    expand_own,
    shrink_own,
    layer_out,
    grad_first_out,
    grad_context_out,
    pack,
    expand_s,
    shrink_s,
    sems,
    x_s,
    normed_s,
    hidden_s,
    act_s,
    slope_s,
    branch_s,
    context_s,
):
    chunks = expand.shape[0]
    pieces = expand.shape[2] // LANES

    def loads(c):
        return (
            pltpu.make_async_copy(expand.at[c], expand_s.at[c], sems.at[0, c]),
            pltpu.make_async_copy(shrink.at[c], shrink_s.at[c], sems.at[1, c]),
        )

    me = lax.axis_index("tensor")

    def begin(c, carry):
        @pl.when(c == me)
        def _():
            pltpu.make_async_copy(expand_own, expand_s.at[c], sems.at[0, c]).start()
            pltpu.make_async_copy(shrink_own, shrink_s.at[c], sems.at[1, c]).start()

        @pl.when(c != me)
        def _():
            for copy in loads(c):
                copy.start()

        return carry

    lax.fori_loop(0, chunks, begin, 0)
    pack[...] = jnp.zeros_like(pack)

    def keep(first, values):
        for j in range(values.shape[1] // LANES):
            pack[first + j, :RANK, :] = values[:, j * LANES : (j + 1) * LANES]

    wide = lax.broadcasted_iota(jnp.int32, (RANK, LANES), 1)
    lam_out = column_of(scale[3:4, :])
    lam_one = column_of(feed_scale[0:1, :])
    lam_two = column_of(feed_scale[1:2, :])
    step = LANES
    steps = ROWS // step

    for p in range(PAIRS):
        context_s[:, p * LANES : (p + 1) * LANES] = context[p]
    out_rank = dot_nt(left_t[:, 3, :], context_s[...])
    out_low = (out_rank * lam_out).astype(bf16)
    x_s[...] = dot_nn(context_s[...], out_weight[...]) + dot_tn(out_low, right[:, 3, :])

    def first_norm(i, carry):
        rows = pl.ds(i * step, step)
        values = tokens[rows, :].astype(f32) + x_s[rows, :]
        x_s[rows, :] = values
        unit, root = norm_parts(values)
        normed = unit * gain[0:1, :] + shift[0:1, :]
        normed_s[rows, :] = normed
        hidden_s[rows, :] = normed.astype(bf16)
        return carry

    lax.fori_loop(0, steps, first_norm, 0)

    one_rank = dot_nt(expand_left_t[...], hidden_s[...])
    one_low = (one_rank * lam_one).astype(bf16)
    branch_s[...] = jnp.zeros_like(branch_s)

    def forward(c, two_rank):
        for copy in loads(c):
            copy.wait()
        pre = dot_nn(hidden_s[...], expand_s[c]) + dot_tn(one_low, expand_right[c])
        cdf = 0.5 + 0.5 * lax.erf(pre * inverse_root_two)
        act = (pre * cdf).astype(bf16)
        act_s[c] = act
        slope_s[c] = cdf + pre * jnp.exp(-0.5 * pre * pre) * inverse_root_tau
        branch_s[...] += dot_nn(act, shrink_s[c])
        return two_rank + dot_nt(shrink_left_t[c], act)

    two_rank = lax.fori_loop(0, chunks, forward, jnp.zeros((RANK, ROWS), f32))
    two_low = (two_rank * lam_two).astype(bf16)
    branch_s[...] += dot_tn(two_low, shrink_right[...])

    def second_norm(i, carry):
        rows = pl.ds(i * step, step)
        unit, root = norm_parts(normed_s[rows, :] + branch_s[rows, :])
        layer_out[rows, :] = (unit * gain[1:2, :] + shift[1:2, :]).astype(bf16)
        grad = norm_back(cotangent[rows, :].astype(f32) * gain[1:2, :], unit, root)
        branch_s[rows, :] = grad
        return carry

    lax.fori_loop(0, steps, second_norm, 0)
    grad_branch = branch_s[...].astype(bf16)
    two_back = dot_nt(shrink_right[...], grad_branch)
    two_small = (two_back * lam_two).astype(bf16)
    keep(18, dot_nn(two_low, grad_branch))
    two_scale = jnp.sum(two_rank * two_back, axis=1, keepdims=True)

    def backward(c, one_back):
        grad_act = dot_nt(grad_branch, shrink_s[c]) + dot_tn(two_small, shrink_left_t[c])
        grad_pre = (grad_act * slope_s[c]).astype(bf16)
        keep(SPLIT_AT + (chunks + c) * pieces, dot_nn(two_small, act_s[c]))
        keep(SPLIT_AT + c * pieces, dot_nn(one_low, grad_pre))
        branch_s[...] += dot_nt(grad_pre, expand_s[c])
        return one_back + dot_nt(expand_right[c], grad_pre)

    one_back = lax.fori_loop(0, chunks, backward, jnp.zeros((RANK, ROWS), f32))
    one_small = (one_back * lam_one).astype(bf16)
    branch_s[...] += dot_tn(one_small, expand_left_t[...])
    keep(12, dot_nn(one_small, hidden_s[...]))
    one_scale = jnp.sum(one_rank * one_back, axis=1, keepdims=True)

    def first_back(i, carry):
        rows = pl.ds(i * step, step)
        unit, root = norm_parts(x_s[rows, :])
        grad_first_out[rows, :] = norm_back(branch_s[rows, :] * gain[0:1, :], unit, root)
        return carry

    lax.fori_loop(0, steps, first_back, 0)
    grad_attended = grad_first_out[...].astype(bf16)
    out_back = dot_nt(right[:, 3, :], grad_attended)
    out_small = (out_back * lam_out).astype(bf16)
    grad_context = dot_nt(grad_attended, out_weight[...]) + dot_tn(out_small, left_t[:, 3, :])
    for p in range(PAIRS):
        grad_context_out[p] = grad_context[:, p * LANES : (p + 1) * LANES].astype(bf16)
    keep(0, dot_nn(out_small, context_s[...]))
    keep(6, dot_nn(out_low, grad_attended))
    out_scale = jnp.sum(out_rank * out_back, axis=1, keepdims=True)
    keep(
        24,
        jnp.where(
            wide == 3,
            out_scale,
            jnp.where(wide == 4, one_scale, jnp.where(wide == 5, two_scale, 0.0)),
        ),
    )


def feed(tiles, *args):
    chunks, _, hidden = args[9].shape
    return pl.pallas_call(
        feed_kernel,
        out_shape=(
            jax.ShapeDtypeStruct((ROWS, WIDTH), bf16),
            jax.ShapeDtypeStruct((ROWS, WIDTH), f32),
            jax.ShapeDtypeStruct((PAIRS, ROWS, LANES), bf16),
            jax.ShapeDtypeStruct((tiles, TILE, LANES), f32),
        ),
        in_specs=[vmem()] * 9
        + [anywhere(), vmem(), vmem(), anywhere(), vmem(), vmem(), vmem(), anywhere(), anywhere()],
        out_specs=(vmem(),) * 4,
        scratch_shapes=[
            pltpu.VMEM((chunks, WIDTH, hidden), bf16),
            pltpu.VMEM((chunks, hidden, WIDTH), bf16),
            pltpu.SemaphoreType.DMA((2, chunks)),
            pltpu.VMEM((ROWS, WIDTH), f32),
            pltpu.VMEM((ROWS, WIDTH), f32),
            pltpu.VMEM((ROWS, WIDTH), bf16),
            pltpu.VMEM((chunks, ROWS, hidden), bf16),
            pltpu.VMEM((chunks, ROWS, hidden), f32),
            pltpu.VMEM((ROWS, WIDTH), f32),
            pltpu.VMEM((ROWS, WIDTH), bf16),
        ],
        compiler_params=pltpu.CompilerParams(vmem_limit_bytes=58 * 2**20),
        name="feed",
    )(*args)


def back_kernel(
    grad_context,
    grad_first,
    shares_in,
    q_s,
    k_s,
    v_s,
    tq_s,
    tk_s,
    tr_s,
    tokens,
    mix_weight,
    left_t,
    right,
    scale,
    early,
    grad_tokens,
    early_out,
    tail_out,
    shares_s,
    gl_s,
    qf_s,
    kf_s,
    fq_s,
    fk_s,
    gq_s,
    gk_s,
    gv_t,
    gtq_t,
    gtk_t,
    tail,
    sems,
    *reduce_refs,
):
    arrived, crossed = reduce_refs[0], reduce_refs[1]
    groups = Groups(arrived.shape[0] // 2 + 1, crossed.shape[0] * 2)
    first = Reduction(groups, early, arrived, crossed, early_out, reduce_refs[2:8])
    second = Reduction(groups, tail, reduce_refs[8], reduce_refs[9], tail_out, reduce_refs[10:16])
    row, lane = block_iotas()
    below_rev = lane + row <= LANES - 1
    lane_first = lane == 0
    lane_last = lane == LANES - 1
    flip = (row + lane == LANES - 1).astype(bf16)

    def begin(p, carry):
        pltpu.make_async_copy(shares_in.at[p], shares_s.at[p], sems.at[p]).start()
        return carry

    lax.fori_loop(0, PAIRS, begin, 0)
    greet(groups.partners())
    first.start()
    tail[...] = jnp.zeros_like(tail)

    def keep(index, values):
        for j in range(values.shape[1] // LANES):
            tail[index + j, :RANK, :] = values[:, j * LANES : (j + 1) * LANES].astype(bf16)

    def flipped(values):
        return jnp.concatenate(
            [
                dot_nn(flip, values[b * LANES : (b + 1) * LANES, :]).astype(bf16)
                for b in range(BLOCKS)
            ],
            axis=0,
        )

    def pair(p, carry):
        pltpu.make_async_copy(shares_in.at[p], shares_s.at[p], sems.at[p]).wait()

        @pl.when(p == 2)
        def _():
            first.middle()

        @pl.when(p == 4)
        def _():
            first.last()

        gc = grad_context[p]
        gc_t = gc.T
        q_rev_t = flipped(q_s[p]).T
        k_rev_t = flipped(k_s[p]).T
        vp = v_s[p]
        gq = None
        gk = None
        for which in range(2):
            mask = head_mask(which)
            half = slice(which * 64, which * 64 + 64)
            for a in range(BLOCKS):
                rows = slice(a * LANES, (a + 1) * LANES)
                shares = shares_s[p, which, rows, :].astype(f32)
                grad = dot_nt(gc[rows, :] * mask, vp)
                prod = grad * shares
                inner = jnp.sum(prod, axis=1, keepdims=True)
                gl_s[rows, :] = (prod - shares * inner).astype(bf16)
            for a in range(BLOCKS):
                rows = slice(a * LANES, (a + 1) * LANES)
                along = dot_nn(flip, gl_s[rows, :])
                qf_s[rows, :] = along.astype(bf16)
                fq_s[rows, :] = (
                    fold_rows(along, a, below_rev, lane_first, lane_last) * score_scale
                ).astype(bf16)
                across = dot_nt(flip, gl_s[:, rows])
                kf_s[rows, :] = across.astype(bf16)
                fk_s[rows, :] = (
                    fold_rows(across, a, below_rev, lane_first, lane_last) * score_scale
                ).astype(bf16)
            fq = fq_s[...]
            fk = fk_s[...]
            part_q = dot_nn(qf_s[...], k_s[p] * mask) * score_scale + dot_nn(fq, tk_s[p] * mask)
            part_k = dot_nn(kf_s[...], q_s[p] * mask) * score_scale + dot_nn(fk, tq_s[p] * mask)
            gq = part_q if which == 0 else gq + part_q
            gk = part_k if which == 0 else gk + part_k
            out = pl.ds(pl.multiple_of(p * LANES + which * 64, 64), 64)
            gv_t[out, :] = dot_nn(gc_t[half, :], shares_s[p, which]).astype(bf16)
            gtk_t[out, :] = dot_nn(q_rev_t[half, :], fq).astype(bf16)
            gtq_t[out, :] = dot_nn(k_rev_t[half, :], fk).astype(bf16)
        gq_s[p] = flipped(gq.astype(bf16))
        gk_s[p] = flipped(gk.astype(bf16))
        return carry

    lax.fori_loop(0, PAIRS, pair, 0)

    first.finish()
    wide = lax.broadcasted_iota(jnp.int32, (RANK, LANES), 1)
    scales = jnp.zeros((RANK, LANES), f32)
    source = tokens[...]
    grads = []
    smalls = []
    for which in range(3):
        if which == 2:
            grad = gv_t[...].T
        else:
            grad = jnp.concatenate([(gq_s, gk_s)[which][p] for p in range(PAIRS)], axis=1)
        left = left_t[:, which, :]
        lam = column_of(scale[which : which + 1, :])
        rank = dot_nt(left, source)
        low = (rank * lam).astype(bf16)
        back = dot_nt(right[:, which, :], grad)
        small = (back * lam).astype(bf16)
        grads.append(grad)
        smalls.append(small)
        left_sum = dot_nn(small, source)
        right_sum = dot_nn(low, grad)
        scale_sum = jnp.sum(rank * back, axis=1, keepdims=True)
        if which < 2:
            table_grad = (gtq_t, gtk_t)[which][...]
            rank = dot_nt(left, tr_s[...])
            low = (rank * lam).astype(bf16)
            back = dot_nn(right[:, which, :], table_grad)
            small = (back * lam).astype(bf16)
            left_sum = left_sum + dot_nn(small, tr_s[...])
            right_sum = right_sum + dot_nt(low, table_grad)
            scale_sum = scale_sum + jnp.sum(rank * back, axis=1, keepdims=True)
        keep(which * 6, left_sum)
        keep(18 + which * 6, right_sum)
        scales = jnp.where(wide == which, scale_sum, scales)
    keep(36, scales)
    second.start()
    total = grad_first[...]
    for which in range(3):
        if which == 1:
            second.middle()
        if which == 2:
            second.last()
        total = (
            total
            + dot_nt(grads[which], mix_weight[which])
            + dot_tn(smalls[which], left_t[:, which, :])
        )
    grad_tokens[...] = total
    second.finish()


def back(tail_tiles, near_size, far_size, *args):
    early = args[-1]
    return pl.pallas_call(
        back_kernel,
        out_shape=(
            jax.ShapeDtypeStruct((ROWS, WIDTH), f32),
            jax.ShapeDtypeStruct(early.shape, f32),
            jax.ShapeDtypeStruct((tail_tiles, TILE, LANES), bf16),
        ),
        in_specs=[vmem(), vmem(), anywhere()] + [vmem()] * 12,
        out_specs=(vmem(),) * 3,
        scratch_shapes=[
            pltpu.VMEM((PAIRS, 2, ROWS, ROWS), bf16),
            pltpu.VMEM((ROWS, ROWS), bf16),
            pltpu.VMEM((ROWS, ROWS), bf16),
            pltpu.VMEM((ROWS, ROWS), bf16),
            pltpu.VMEM((ROWS, ROWS), bf16),
            pltpu.VMEM((ROWS, ROWS), bf16),
            pltpu.VMEM((PAIRS, ROWS, LANES), bf16),
            pltpu.VMEM((PAIRS, ROWS, LANES), bf16),
            pltpu.VMEM((WIDTH, ROWS), bf16),
            pltpu.VMEM((WIDTH, ROWS), bf16),
            pltpu.VMEM((WIDTH, ROWS), bf16),
            pltpu.VMEM((tail_tiles, TILE, LANES), bf16),
            pltpu.SemaphoreType.DMA((PAIRS,)),
        ]
        + reduction_scratch(early.shape[0], near_size, far_size, f32)
        + reduction_scratch(tail_tiles, near_size, far_size, bf16),
        compiler_params=pltpu.CompilerParams(
            vmem_limit_bytes=58 * 2**20, collective_id=1, has_side_effects=True
        ),
        name="back",
    )(*args)


def unpack_kernel(
    early,
    tail,
    tokens_in,
    tokens_out,
    left,
    scale,
    right,
    expand_left_t,
    expand_right,
    shrink_left_t,
    feed_scale,
    shrink_right,
    sem,
):
    copy = pltpu.make_async_copy(tokens_in, tokens_out, sem)
    copy.start()
    me = lax.axis_index("tensor")
    pieces = expand_right.shape[1] // LANES
    split = SPLIT_AT + me * pieces
    skip = (early.shape[0] - SPLIT_AT) // 2
    for j in range(WIDTH // LANES):
        lanes = slice(j * LANES, (j + 1) * LANES)
        for which in range(3):
            left[:, which, lanes] = tail[which * 6 + j, :RANK, :].astype(f32)
            right[:, which, lanes] = tail[18 + which * 6 + j, :RANK, :].astype(f32)
        left[:, 3, lanes] = early[j, :RANK, :]
        right[:, 3, lanes] = early[6 + j, :RANK, :]
        expand_left_t[:, lanes] = early[12 + j, :RANK, :]
        shrink_right[:, lanes] = early[18 + j, :RANK, :]
    total = lax.axis_size("tensor") * pieces
    for j in range(pieces):
        lanes = slice(j * LANES, (j + 1) * LANES)
        expand_right[:, lanes] = early[split + j, :RANK, :]
        shrink_left_t[:, lanes] = early[split + total + j, :RANK, :]
    wide = lax.broadcasted_iota(jnp.int32, (TILE, LANES), 1)
    both = jnp.where(wide < 3, tail[36].astype(f32), early[24]).T
    scale[...] = both[:4, :RANK]
    feed_scale[...] = both[4:6, :RANK]
    copy.wait()


def unpack(hidden, early, tail, tokens):
    mats = jax.ShapeDtypeStruct((RANK, 4, WIDTH), f32)
    small = jax.ShapeDtypeStruct((RANK, WIDTH), f32)
    split = jax.ShapeDtypeStruct((RANK, hidden), f32)
    return pl.pallas_call(
        unpack_kernel,
        out_shape=(
            jax.ShapeDtypeStruct((ROWS, WIDTH), f32),
            mats,
            jax.ShapeDtypeStruct((4, RANK), f32),
            mats,
            small,
            split,
            split,
            jax.ShapeDtypeStruct((2, RANK), f32),
            small,
        ),
        in_specs=[vmem(), vmem(), vmem()],
        out_specs=(anywhere(),) + (vmem(),) * 8,
        scratch_shapes=[pltpu.SemaphoreType.DMA],
        name="unpack",
    )(early, tail, tokens)


def body(
    tokens,
    segment,
    live,
    mix_weight,
    out_weight,
    position_table,
    norm_gain,
    norm_bias,
    mix_left,
    mix_scale,
    mix_right,
    expand_weight,
    expand_left,
    expand_right,
    shrink_weight,
    shrink_left,
    feed_scale,
    shrink_right,
    cotangent,
):
    tensor_size = lax.axis_size("tensor")
    near_size = tensor_size * 2
    far_size = lax.axis_size("dp") // 2
    hidden = expand_weight.shape[1]
    early_tiles = -(-(SPLIT_AT + 2 * tensor_size * hidden // LANES) // near_size) * near_size
    tail_tiles = -(-37 // near_size) * near_size
    left_t = jnp.transpose(mix_left, (2, 0, 1))
    right = jnp.transpose(mix_right, (1, 0, 2))
    (
        shares,
        expand_all,
        shrink_all,
        expand_right_all,
        shrink_left_all,
        q,
        k,
        v,
        tq,
        tk,
        tr,
        context,
    ) = attend(
        tensor_size,
        segment.reshape(1, ROWS),
        live.reshape(1, ROWS),
        tokens,
        position_table,
        mix_weight,
        left_t,
        right,
        mix_scale,
        expand_weight,
        shrink_weight,
        expand_right,
        shrink_left.T,
    )
    layer_out, grad_first, grad_context, early = feed(
        early_tiles,
        context,
        tokens,
        cotangent,
        out_weight,
        left_t,
        right,
        mix_scale,
        norm_gain,
        norm_bias,
        expand_all,
        expand_left.T,
        expand_right_all,
        shrink_all,
        shrink_left_all,
        shrink_right,
        feed_scale,
        expand_weight,
        shrink_weight,
    )
    grad_tokens, early, tail = back(
        tail_tiles,
        near_size,
        far_size,
        grad_context,
        grad_first,
        shares,
        q,
        k,
        v,
        tq,
        tk,
        tr,
        tokens,
        mix_weight,
        left_t,
        right,
        mix_scale,
        early,
    )
    grad_tokens, left, scale, right, expand_left, expand_right, shrink_left, feed_scale, shrink_right = unpack(
        hidden, early, tail, grad_tokens
    )
    return (
        layer_out,
        grad_tokens,
        jnp.transpose(left, (1, 2, 0)),
        scale,
        jnp.transpose(right, (1, 0, 2)),
        expand_left.T,
        expand_right,
        shrink_left.T,
        feed_scale,
        shrink_right,
    )


def solution(mesh):
    rows = P(("dp", "tensor"), None)
    line = P(("dp", "tensor"))
    return jax.shard_map(
        body,
        mesh=mesh,
        in_specs=(
            rows,
            line,
            line,
            P(),
            P(),
            P(),
            P(),
            P(),
            P(),
            P(),
            P(),
            P(None, "tensor"),
            P(),
            P(None, "tensor"),
            P("tensor", None),
            P("tensor", None),
            P(),
            P(),
            rows,
        ),
        out_specs=(
            rows,
            rows,
            P(),
            P(),
            P(),
            P(),
            P(None, "tensor"),
            P("tensor", None),
            P(),
            P(),
        ),
        check_vma=False,
    )
```

```python
import math

import jax
import jax.numpy as jnp
from jax import lax
from jax.experimental import pallas as pl
from jax.experimental.pallas import tpu as pltpu
from jax.sharding import PartitionSpec as P

PAIRS = 6
LANES = 128
ROWS = 512
WIDTH = 768
RANK = 12
BLOCKS = ROWS // LANES
TILE = 16
GROUP = 2
BACK_GROUP = 4
STACK = 64
SPLIT_AT = 25

norm_eps = 1e-07
masked_fill = -1e30
score_scale = 1.0 / math.sqrt(192.0)
inverse_root_two = 1.0 / math.sqrt(2.0)
log_two_e = math.log2(math.e)
inverse_root_tau = 1.0 / math.sqrt(2.0 * math.pi)

f32 = jnp.float32
bf16 = jnp.bfloat16


def dot_nn(left, right):
    return jnp.dot(left, right, preferred_element_type=f32)


def dot_nt(left, right):
    return lax.dot_general(left, right, (((1,), (1,)), ((), ())), preferred_element_type=f32)


def dot_tn(left, right):
    return lax.dot_general(left, right, (((0,), (0,)), ((), ())), preferred_element_type=f32)


def column_of(row):
    n = row.shape[1]
    eye = lax.broadcasted_iota(jnp.int32, (n, n), 0) == lax.broadcasted_iota(jnp.int32, (n, n), 1)
    return jnp.sum(jnp.where(eye, row, 0.0), axis=1, keepdims=True)


def spread(scale):
    row = lax.broadcasted_iota(jnp.int32, (RANK, STACK), 0)
    lane = lax.broadcasted_iota(jnp.int32, (RANK, STACK), 1)
    total = jnp.zeros((1, STACK), f32)
    for a in range(4):
        column = column_of(scale[a : a + 1, :])
        total = total + jnp.sum(
            jnp.where(lane == row + TILE * a, column, 0.0), axis=0, keepdims=True
        )
    return total


def of_map(which):
    lane = lax.broadcasted_iota(jnp.int32, (1, STACK), 1)
    return (lane // TILE == which).astype(bf16)


def block_iotas():
    shape = (LANES, LANES)
    return lax.broadcasted_iota(jnp.int32, shape, 0), lax.broadcasted_iota(jnp.int32, shape, 1)


def head_mask(which):
    lane = lax.broadcasted_iota(jnp.int32, (1, LANES), 1)
    return ((lane >= 64) if which else (lane < 64)).astype(bf16)


def pick_tiles(scores, block, at_diag):
    first = scores[:, :1]
    last = scores[:, ROWS - 1 :]
    near = {}

    def rolled(u):
        if u not in near:
            near[u] = pltpu.roll(
                scores[:, u * LANES : (u + 1) * LANES], 1, 1, stride=1, stride_axis=0
            )
        return near[u]

    tiles = []
    for other in range(BLOCKS):
        v = other - block + 2
        if v < 0:
            tile = jnp.broadcast_to(first, (LANES, LANES))
        elif v == 0:
            tile = jnp.where(at_diag, first, rolled(0))
        elif v < 4:
            tile = jnp.where(at_diag, rolled(v - 1), rolled(v))
        elif v == 4:
            tile = jnp.where(at_diag, rolled(3), last)
        else:
            tile = jnp.broadcast_to(last, (LANES, LANES))
        tiles.append(tile)
    return tiles


def row_sums(values):
    part = (
        values[:, :LANES]
        + values[:, LANES : 2 * LANES]
        + values[:, 2 * LANES : 3 * LANES]
        + values[:, 3 * LANES :]
    )
    high = part.astype(bf16)
    rest = (part - high.astype(f32)).astype(bf16)
    return dot_nn(jnp.concatenate([high, rest], axis=1), jnp.ones((2 * LANES, LANES), bf16))


def wide4(values):
    return jnp.concatenate([values] * BLOCKS, axis=1)


def fold_rows(grads, block, beyond, inside, pick_first, pick_last):
    zero = jnp.zeros((LANES, LANES), f32)
    near = {}
    low = []
    high = []
    for other in range(BLOCKS):
        v = other - block + 2
        tile = grads[:, other * LANES : (other + 1) * LANES]
        if v < 0:
            low.append(tile.astype(bf16))
        elif v > 4:
            high.append(tile.astype(bf16))
        else:
            near[v] = pltpu.roll(tile, 0, 1, stride=1, stride_axis=0)
        if v == 0:
            low.append(tile.astype(bf16) * inside)
        if v == 4:
            high.append(tile.astype(bf16) * (1 - inside))
    out = []
    for w in range(BLOCKS):
        if w in near or w + 1 in near:
            out.append(jnp.where(beyond, near.get(w + 1, zero), near.get(w, zero)))
        else:
            out.append(zero)
    if low:
        out[0] = out[0] + dot_nn(
            jnp.concatenate(low, axis=1), pick_first[: LANES * len(low), :]
        )
    if high:
        out[3] = out[3] + dot_nn(
            jnp.concatenate(high, axis=1), pick_last[: LANES * len(high), :]
        )
    return jnp.concatenate(out, axis=1)


def attend_part(
    segment,
    live,
    tokens,
    table,
    mix_weight,
    mix_copies,
    left_s,
    right_s,
    scale_row,
    rank_s,
    table_rank_s,
    shares_out,
    q_s,
    k_s,
    v_s,
    tq_s,
    tk_s,
    tr_s,
    context_s,
    shares_s,
    bias_s,
    across_s,
    sems,
    gather,
):
    row, lane = block_iotas()
    below = lane <= row
    flip = (row + lane == LANES - 1).astype(bf16)
    eye = (row == lane).astype(bf16)
    seg_row = segment[...]
    key_row = jnp.where(live[...] == 1, seg_row, -1)
    for a in range(BLOCKS):
        seg_col = jnp.broadcast_to(
            seg_row[:, a * LANES : (a + 1) * LANES].astype(f32), (LANES, LANES)
        ).T.astype(jnp.int32)
        for b in range(BLOCKS):
            same = seg_col == key_row[:, b * LANES : (b + 1) * LANES]
            if a == b:
                same = same | (row == lane)
            bias_s[a * LANES : (a + 1) * LANES, b * LANES : (b + 1) * LANES] = jnp.where(
                same, 0.0, masked_fill
            )
    for a in range(BLOCKS):
        tr_s[a * LANES : (a + 1) * LANES, :] = dot_nn(
            flip, table[(3 - a) * LANES : (4 - a) * LANES, :]
        ).astype(bf16)

    rank_s[...] = dot_nt(tokens[...], left_s[...])
    table_rank_s[...] = dot_nt(tr_s[...], left_s[...])
    low = (rank_s[...] * scale_row).astype(bf16)
    table_low = (table_rank_s[...] * scale_row).astype(bf16)

    def project(source, low, which, target):
        full = dot_nn(source, mix_weight[which]) + dot_nn(low * of_map(which), right_s[...])
        for p in range(PAIRS):
            target[p] = full[:, p * LANES : (p + 1) * LANES].astype(bf16)

    mix_copies[0].wait()
    project(tokens[...], low, 0, q_s)
    project(tr_s[...], table_low, 0, tq_s)
    mix_copies[1].wait()
    project(tokens[...], low, 1, k_s)
    project(tr_s[...], table_low, 1, tk_s)
    gather.forward_one(0)
    mix_copies[2].wait()
    project(tokens[...], low, 2, v_s)

    def key_side(p, which, group):
        top = group * GROUP * LANES
        scores = dot_nt(
            k_s[p, top : top + GROUP * LANES, :] * head_mask(which), tq_s[p]
        )
        for i in range(GROUP):
            tiles = pick_tiles(
                scores[i * LANES : (i + 1) * LANES, :], group * GROUP + i, below
            )
            across_s[which, top + i * LANES : top + (i + 1) * LANES, :] = jnp.concatenate(
                tiles, axis=1
            ).astype(bf16)

    def query_side(p, which, group):
        mask = head_mask(which)
        blocks = range(group * GROUP, (group + 1) * GROUP)
        rows = [slice(a * LANES, (a + 1) * LANES) for a in blocks]
        every = slice(rows[0].start, rows[-1].stop)
        queries = [q_s[p, r, :] * mask for r in rows]
        scores = dot_nt(q_s[p, every, :] * mask, tk_s[p])
        totals = [
            dot_nt(
                jnp.concatenate([q, eye], axis=1),
                jnp.concatenate([k_s[p], across_s[which, :, r]], axis=1),
            )
            for q, r in zip(queries, rows)
        ]
        totals = [
            t
            + jnp.concatenate(
                pick_tiles(scores[i * LANES : (i + 1) * LANES, :], blocks[i], below), axis=1
            )
            + bias_s[rows[i], :]
            for i, t in enumerate(totals)
        ]
        peaks = [jnp.max(t, axis=1, keepdims=True) for t in totals]
        weights = [
            jnp.exp2((t - m) * (score_scale * log_two_e)) for t, m in zip(totals, peaks)
        ]
        inverses = [1.0 / jnp.sum(w, axis=1, keepdims=True) for w in weights]
        for r, w, inverse in zip(rows, weights, inverses):
            shares_s[p, which, r, :] = (w * inverse).astype(bf16)
        return dot_nn(shares_s[p, which, every, :], v_s[p] * mask)

    groups = BLOCKS // GROUP
    for group in range(groups):
        key_side(0, 0, group)

    def pair(p, carry):
        for k in range(6):

            @pl.when(p == k)
            def _():
                if k:
                    gather.forward_one(k)
                if k > 1:
                    gather.forward_two(k - 2)

        later = jnp.minimum(p + 1, PAIRS - 1)
        context = []
        for group in range(groups):
            context.append(query_side(p, 0, group))
            key_side(p, 1, group)
        for group in range(groups):
            part = context[group] + query_side(p, 1, group)
            context_s[
                group * GROUP * LANES : (group + 1) * GROUP * LANES,
                pl.ds(pl.multiple_of(p * LANES, LANES), LANES),
            ] = part.astype(bf16)
            key_side(later, 0, group)
        pltpu.make_async_copy(shares_s.at[p], shares_out.at[p], sems.at[p]).start()
        return carry

    lax.fori_loop(0, PAIRS, pair, 0)
    gather.forward_two(4)


def vmem():
    return pl.BlockSpec(memory_space=pltpu.VMEM)


def anywhere():
    return pl.BlockSpec(memory_space=pl.ANY)


def remote(source, target, send, recv, device):
    return pltpu.make_async_remote_copy(
        src_ref=source,
        dst_ref=target,
        send_sem=send,
        recv_sem=recv,
        device_id=device,
        device_id_type=pl.DeviceIdType.MESH,
    )


def greet(devices):
    barrier = pltpu.get_barrier_semaphore()
    for device in devices:
        pl.semaphore_signal(
            barrier, inc=1, device_id=device, device_id_type=pl.DeviceIdType.MESH
        )
    pl.semaphore_wait(barrier, len(devices))


class Groups:
    def __init__(self, tensor_size, dp_size):
        self.near_size = tensor_size * 2
        self.far_size = dp_size // 2
        self.tensor = lax.axis_index("tensor")
        self.dp = lax.axis_index("dp")
        self.near = self.tensor * 2 + self.dp % 2
        self.far = self.dp // 2

    def near_index(self, step):
        return (self.near + step) % self.near_size

    def near_device(self, step):
        index = self.near_index(step)
        return {"dp": self.far * 2 + index % 2, "tensor": index // 2}

    def far_device(self, step):
        index = (self.far + step) % self.far_size
        return {"dp": index * 2 + self.dp % 2, "tensor": self.tensor}

    def partners(self):
        return [self.near_device(s) for s in range(1, self.near_size)] + [
            self.far_device(s) for s in range(1, self.far_size)
        ]


class Reduction:
    def __init__(self, groups, pack, arrived, crossed, out, sems):
        self.groups = groups
        self.pack = pack
        self.arrived = arrived
        self.crossed = crossed
        self.out = out
        self.send_one, self.recv_one, self.send_two, self.recv_two, self.send_three, self.recv_three = sems
        self.size = pack.shape[0] // groups.near_size

    def part(self, ref, index):
        return ref.at[pl.ds(index * self.size, self.size)]

    def scatter(self):
        g = self.groups
        return [
            remote(
                self.part(self.pack, g.near_index(s)),
                self.arrived.at[s - 1],
                self.send_one.at[s - 1],
                self.recv_one.at[s - 1],
                g.near_device(s),
            )
            for s in range(1, g.near_size)
        ]

    def cross(self):
        g = self.groups
        return [
            remote(
                self.crossed.at[g.far],
                self.crossed.at[g.far],
                self.send_two.at[s - 1],
                self.recv_two.at[s - 1],
                g.far_device(s),
            )
            for s in range(1, g.far_size)
        ]

    def gather(self):
        g = self.groups
        return [
            remote(
                self.part(self.out, g.near),
                self.part(self.out, g.near),
                self.send_three.at[s - 1],
                self.recv_three.at[s - 1],
                g.near_device(s),
            )
            for s in range(1, g.near_size)
        ]

    def start(self):
        for copy in self.scatter():
            copy.start()

    def middle(self):
        g = self.groups
        for copy in self.scatter():
            copy.wait()
        total = self.pack[pl.ds(g.near * self.size, self.size)].astype(f32)
        for s in range(1, g.near_size):
            total = total + self.arrived[s - 1].astype(f32)
        self.crossed[g.far] = total.astype(self.crossed.dtype)
        for copy in self.cross():
            copy.start()

    def last(self):
        g = self.groups
        for copy in self.cross():
            copy.wait()
        total = self.crossed[0].astype(f32)
        for s in range(1, g.far_size):
            total = total + self.crossed[s].astype(f32)
        self.out[pl.ds(g.near * self.size, self.size)] = total.astype(self.out.dtype)
        for copy in self.gather():
            copy.start()

    def finish(self):
        for copy in self.gather():
            copy.wait()


def reduction_scratch(tiles, near_size, far_size, kind):
    size = tiles // near_size
    near = (near_size - 1,)
    far = (max(far_size - 1, 1),)
    dma = pltpu.SemaphoreType.DMA
    return [
        pltpu.VMEM((near_size - 1, size, TILE, LANES), kind),
        pltpu.VMEM((far_size, size, TILE, LANES), kind),
        dma(near),
        dma(near),
        dma(far),
        dma(far),
        dma(near),
        dma(near),
    ]


class Gather:
    def __init__(self, size, sources, targets, sems):
        self.size = size
        self.far = size // 2
        self.sources = sources
        self.targets = targets
        self.across_s, self.across_r, self.pair_s, self.pair_r, self.one_s, self.one_r, self.two_s, self.two_r = sems[:8]
        self.whole_s, self.whole_r, self.small_s, self.small_r, self.own = sems[8:]
        self.tensor = lax.axis_index("tensor")
        self.dp = lax.axis_index("dp")
        self.bit = self.dp % 2
        self.pair = {"dp": self.dp + 1 - 2 * self.bit, "tensor": self.tensor}
        self.near = self.tensor + 1 - 2 * (self.tensor % 2)
        self.core = {"dp": self.dp, "tensor": self.near}

    def device(self, step):
        return {"dp": self.dp, "tensor": (self.tensor + step) % self.size}

    def partners(self):
        return [self.device(s) for s in range(1, self.size)] + [self.pair]

    def slot(self, order):
        first = self.tensor if isinstance(order, int) and order % 2 == 0 else None
        if first is None:
            first = self.tensor + (order % 2) * (self.near - self.tensor)
        return (first + self.size - 2 * (order // 2)) % self.size

    def rows(self, which, part, bit):
        count = self.sources[which].shape[0] // 6
        return pl.ds((2 * part + bit) * count, count)

    def across(self, s, k):
        which, part = k // 3, k % 3
        rows = self.rows(which, part, self.bit)
        return remote(
            self.sources[which].at[rows, :],
            self.targets[which].at[self.tensor, rows, :],
            self.across_s.at[s - 1, k],
            self.across_r.at[s - 1, k],
            self.device(2 * s),
        )

    def onward(self, s, k, bit, sends, recvs, device):
        which, part = k // 3, k % 3
        rows = self.rows(which, part, bit)
        ref = self.targets[which].at[self.slot(2 * s), rows, :]
        return remote(ref, ref, sends.at[s - 1, k], recvs.at[s - 1, k], device)

    def swap(self, s, k):
        return self.onward(s, k, self.bit, self.pair_s, self.pair_r, self.pair)

    def share_one(self, s, k):
        return self.onward(s, k, self.bit, self.one_s, self.one_r, self.core)

    def share_two(self, s, k):
        return self.onward(s, k, 1 - self.bit, self.two_s, self.two_r, self.core)

    def whole(self, which):
        return remote(
            self.sources[which],
            self.targets[which].at[self.tensor],
            self.whole_s.at[which],
            self.whole_r.at[which],
            self.core,
        )

    def small(self, s, which):
        return remote(
            self.sources[which],
            self.targets[which].at[self.tensor],
            self.small_s.at[s - 1, which - 2],
            self.small_r.at[s - 1, which - 2],
            self.device(s),
        )

    def keep(self, which):
        return pltpu.make_async_copy(
            self.sources[which], self.targets[which].at[self.tensor], self.own.at[which]
        )

    def start(self):
        for which in range(4):
            self.keep(which).start()
        greet(self.partners())
        for k in range(6):
            for s in range(1, self.far):
                self.across(s, k).start()
        for which in range(2):
            self.whole(which).start()
        for s in range(1, self.size):
            for which in (2, 3):
                self.small(s, which).start()

    def forward_one(self, k):
        for s in range(1, self.far):
            self.across(s, k).wait_recv()
            self.swap(s, k).start()
            self.share_one(s, k).start()

    def forward_two(self, k):
        for s in range(1, self.far):
            self.swap(s, k).wait_recv()
            self.share_two(s, k).start()

    def arrive(self, order):
        if order == 0:
            for which in range(4):
                self.keep(which).wait()
            for s in range(1, self.size):
                for which in (2, 3):
                    self.small(s, which).wait()
        elif order == 1:
            for which in range(2):
                self.whole(which).wait()
        elif order % 2 == 1:
            for k in range(6):
                self.share_one(order // 2, k).wait_recv()
                self.share_two(order // 2, k).wait_recv()

    def finish(self):
        for s in range(1, self.far):
            for k in range(6):
                self.across(s, k).wait_send()
                self.swap(s, k).wait_send()
                self.share_one(s, k).wait_send()
                self.share_two(s, k).wait_send()


def norm_parts(values):
    center = values - jnp.mean(values, axis=-1, keepdims=True)
    root = lax.rsqrt(jnp.mean(center * center, axis=-1, keepdims=True) + norm_eps)
    return center * root, root


def norm_back(scaled, unit, root):
    return root * (
        scaled
        - jnp.mean(scaled, axis=-1, keepdims=True)
        - unit * jnp.mean(scaled * unit, axis=-1, keepdims=True)
    )


def feed_part(
    tokens,
    cotangent,
    cotangent_copy,
    out_weight,
    out_copy,
    left_s,
    right_s,
    scale_row,
    gain,
    shift,
    expand_left_t,
    expand_right,
    shrink_left_t,
    shrink_right,
    feed_scale,
    layer_out,
    grad_first_out,
    grad_context_out,
    pack,
    expand_s,
    shrink_s,
    x_s,
    normed_s,
    hidden_s,
    act_s,
    slope_s,
    branch_s,
    context_s,
    one_s,
    two_s,
    pre_s,
    gather,
):
    chunks = expand_s.shape[0]
    pieces = expand_s.shape[2] // LANES
    pack[...] = jnp.zeros_like(pack)

    def keep(first, values):
        for j in range(values.shape[1] // LANES):
            pack[first + j, :RANK, :] = values[:, j * LANES : (j + 1) * LANES]

    lam_one = feed_scale[0:1, :]
    lam_two = feed_scale[1:2, :]
    step = LANES
    steps = ROWS // step

    out_copy.wait()
    out_rank = dot_nt(context_s[...], left_s[...])
    out_low = (out_rank * scale_row).astype(bf16) * of_map(3)
    x_s[...] = dot_nn(context_s[...], out_weight[...]) + dot_nn(out_low, right_s[...])

    def first_norm(i, carry):
        rows = pl.ds(i * step, step)
        values = tokens[rows, :].astype(f32) + x_s[rows, :]
        x_s[rows, :] = values
        unit, root = norm_parts(values)
        normed = unit * gain[0:1, :] + shift[0:1, :]
        normed_s[rows, :] = normed
        hidden_s[rows, :] = normed.astype(bf16)
        return carry

    lax.fori_loop(0, steps, first_norm, 0)
    gather.forward_two(5)

    one_rank = dot_nt(hidden_s[...], expand_left_t[...])
    one_low = (one_rank * lam_one).astype(bf16)
    def expanded(order):
        gather.arrive(order)
        c = gather.slot(order)
        pre_s[order % 2] = dot_nn(hidden_s[...], expand_s[c]) + dot_nn(one_low, expand_right[c])

    two_rank = None
    expanded(0)
    for order in range(chunks):
        if order + 1 < chunks:
            expanded(order + 1)
        pre = pre_s[order % 2]
        cdf = 0.5 + 0.5 * lax.erf(pre * inverse_root_two)
        act_s[order] = (pre * cdf).astype(bf16)
        slope_s[order] = cdf + pre * jnp.exp(-0.5 * pre * pre) * inverse_root_tau
        c = gather.slot(order)
        part = dot_nn(act_s[order], shrink_s[c])
        branch_s[...] = part if order == 0 else branch_s[...] + part
        part = dot_nt(act_s[order], shrink_left_t[c])
        two_s[...] = part if order == 0 else two_s[...] + part
    two_rank = two_s[...]
    gather.finish()
    two_low = (two_rank * lam_two).astype(bf16)
    branch_s[...] += dot_nn(two_low, shrink_right[...])

    cotangent_copy.wait()

    def second_norm(i, carry):
        rows = pl.ds(i * step, step)
        unit, root = norm_parts(normed_s[rows, :] + branch_s[rows, :])
        layer_out[rows, :] = (unit * gain[1:2, :] + shift[1:2, :]).astype(bf16)
        grad = norm_back(cotangent[rows, :].astype(f32) * gain[1:2, :], unit, root)
        branch_s[rows, :] = grad
        return carry

    lax.fori_loop(0, steps, second_norm, 0)
    grad_branch = branch_s[...].astype(bf16)
    two_back = dot_nt(grad_branch, shrink_right[...])
    two_small = (two_back * lam_two).astype(bf16)
    two_small_t = two_small.T
    one_low_t = one_low.T
    keep(18, dot_tn(two_low, grad_branch))
    pack[24, 5:6, :RANK] = jnp.sum(two_rank * two_back, axis=0, keepdims=True)

    def shrunk(order):
        c = gather.slot(order)
        pre_s[order % 2] = dot_nt(grad_branch, shrink_s[c]) + dot_nn(two_small, shrink_left_t[c])

    shrunk(0)
    for order in range(chunks):
        if order + 1 < chunks:
            shrunk(order + 1)
        c = gather.slot(order)
        grad_pre = (pre_s[order % 2] * slope_s[order]).astype(bf16)
        keep(SPLIT_AT + (chunks + c) * pieces, dot_nn(two_small_t, act_s[order]))
        keep(SPLIT_AT + c * pieces, dot_nn(one_low_t, grad_pre))
        branch_s[...] += dot_nt(grad_pre, expand_s[c])
        part = dot_nt(grad_pre, expand_right[c])
        one_s[...] = part if order == 0 else one_s[...] + part
    one_back = one_s[...]
    one_small = (one_back * lam_one).astype(bf16)
    branch_s[...] += dot_nn(one_small, expand_left_t[...])
    keep(12, dot_tn(one_small, hidden_s[...]))
    pack[24, 4:5, :RANK] = jnp.sum(one_rank * one_back, axis=0, keepdims=True)

    def first_back(i, carry):
        rows = pl.ds(i * step, step)
        unit, root = norm_parts(x_s[rows, :])
        grad_first_out[rows, :] = norm_back(branch_s[rows, :] * gain[0:1, :], unit, root)
        return carry

    lax.fori_loop(0, steps, first_back, 0)
    grad_attended = grad_first_out[...].astype(bf16)
    out_back = dot_nt(grad_attended, right_s[...])
    out_small = (out_back * scale_row).astype(bf16) * of_map(3)
    grad_context = dot_nt(grad_attended, out_weight[...]) + dot_nn(out_small, left_s[...])
    for p in range(PAIRS):
        grad_context_out[p] = grad_context[:, p * LANES : (p + 1) * LANES].astype(bf16)
    keep(0, dot_tn(out_small, context_s[...])[3 * TILE : 3 * TILE + RANK, :])
    keep(6, dot_tn(out_low, grad_attended)[3 * TILE : 3 * TILE + RANK, :])
    pack[24, 3:4, :STACK] = jnp.sum(out_rank * out_back, axis=0, keepdims=True)


def front_kernel(
    segment,
    live,
    tokens,
    table,
    left_t,
    right,
    scale,
    gain,
    shift,
    expand_left_t,
    shrink_right,
    feed_scale,
    mix_weight,
    cotangent,
    out_weight,
    expand,
    shrink,
    expand_right,
    shrink_left_t,
    layer_out,
    grad_first,
    grad_context,
    pack,
    q_s,
    k_s,
    v_s,
    tq_s,
    tk_s,
    tr_s,
    left_s,
    right_s,
    rank_s,
    table_rank_s,
    shares_out,
    mix_s,
    cotangent_s,
    out_s,
    expand_s,
    shrink_s,
    expand_right_s,
    shrink_left_s,
    shares_s,
    bias_s,
    across_s,
    x_s,
    normed_s,
    hidden_s,
    act_s,
    slope_s,
    branch_s,
    context_s,
    one_s,
    two_s,
    pre_s,
    share_sems,
    load_sems,
    *gather_sems,
):
    mix_copies = [
        pltpu.make_async_copy(mix_weight.at[i], mix_s.at[i], load_sems.at[i]) for i in range(3)
    ]
    cotangent_copy = pltpu.make_async_copy(cotangent, cotangent_s, load_sems.at[3])
    out_copy = pltpu.make_async_copy(out_weight, out_s, load_sems.at[4])
    for copy in mix_copies:
        copy.start()
    gather = Gather(
        expand_s.shape[0],
        (expand, shrink, expand_right, shrink_left_t),
        (expand_s, shrink_s, expand_right_s, shrink_left_s),
        gather_sems,
    )
    gather.start()
    cotangent_copy.start()
    out_copy.start()
    left_s[...] = jnp.zeros_like(left_s)
    right_s[...] = jnp.zeros_like(right_s)
    for a in range(4):
        left_s[a * TILE : a * TILE + RANK, :] = left_t[:, a, :]
        right_s[a * TILE : a * TILE + RANK, :] = right[:, a, :]
    scale_row = spread(scale)
    attend_part(
        segment,
        live,
        tokens,
        table,
        mix_s,
        mix_copies,
        left_s,
        right_s,
        scale_row,
        rank_s,
        table_rank_s,
        shares_out,
        q_s,
        k_s,
        v_s,
        tq_s,
        tk_s,
        tr_s,
        context_s,
        shares_s,
        bias_s,
        across_s,
        share_sems,
        gather,
    )
    feed_part(
        tokens,
        cotangent_s,
        cotangent_copy,
        out_s,
        out_copy,
        left_s,
        right_s,
        scale_row,
        gain,
        shift,
        expand_left_t,
        expand_right_s,
        shrink_left_s,
        shrink_right,
        feed_scale,
        layer_out,
        grad_first,
        grad_context,
        pack,
        expand_s,
        shrink_s,
        x_s,
        normed_s,
        hidden_s,
        act_s,
        slope_s,
        branch_s,
        context_s,
        one_s,
        two_s,
        pre_s,
        gather,
    )

    def finish(p, carry):
        pltpu.make_async_copy(shares_s.at[p], shares_out.at[p], share_sems.at[p]).wait()
        return carry

    lax.fori_loop(0, PAIRS, finish, 0)


def front(size, tiles, *args):
    hidden = args[15].shape[1]
    piece = jax.ShapeDtypeStruct((PAIRS, ROWS, LANES), bf16)
    rows = jax.ShapeDtypeStruct((ROWS, WIDTH), bf16)
    dma = pltpu.SemaphoreType.DMA
    steps = (max(size // 2 - 1, 1), 6)
    return pl.pallas_call(
        front_kernel,
        out_shape=(
            rows,
            jax.ShapeDtypeStruct((ROWS, WIDTH), f32),
            piece,
            jax.ShapeDtypeStruct((tiles, TILE, LANES), f32),
            piece,
            piece,
            piece,
            piece,
            piece,
            rows,
            jax.ShapeDtypeStruct((STACK, WIDTH), bf16),
            jax.ShapeDtypeStruct((STACK, WIDTH), bf16),
            jax.ShapeDtypeStruct((ROWS, STACK), f32),
            jax.ShapeDtypeStruct((ROWS, STACK), f32),
            jax.ShapeDtypeStruct((PAIRS, 2, ROWS, ROWS), bf16),
        ),
        in_specs=[vmem()] * 12 + [anywhere()] * 7,
        out_specs=(vmem(),) * 14 + (anywhere(),),
        scratch_shapes=[
            pltpu.VMEM((3, WIDTH, WIDTH), bf16),
            pltpu.VMEM((ROWS, WIDTH), bf16),
            pltpu.VMEM((WIDTH, WIDTH), bf16),
            pltpu.VMEM((size, WIDTH, hidden), bf16),
            pltpu.VMEM((size, hidden, WIDTH), bf16),
            pltpu.VMEM((size, RANK, hidden), bf16),
            pltpu.VMEM((size, RANK, hidden), bf16),
            pltpu.VMEM((PAIRS, 2, ROWS, ROWS), bf16),
            pltpu.VMEM((ROWS, ROWS), f32),
            pltpu.VMEM((2, ROWS, ROWS), bf16),
            pltpu.VMEM((ROWS, WIDTH), f32),
            pltpu.VMEM((ROWS, WIDTH), f32),
            pltpu.VMEM((ROWS, WIDTH), bf16),
            pltpu.VMEM((size, ROWS, hidden), bf16),
            pltpu.VMEM((size, ROWS, hidden), f32),
            pltpu.VMEM((ROWS, WIDTH), f32),
            pltpu.VMEM((ROWS, WIDTH), bf16),
            pltpu.VMEM((ROWS, RANK), f32),
            pltpu.VMEM((ROWS, RANK), f32),
            pltpu.VMEM((2, ROWS, hidden), f32),
            dma((PAIRS,)),
            dma((5,)),
        ]
        + [dma(steps)] * 8
        + [dma((2,))] * 2
        + [dma((size - 1, 2))] * 2
        + [dma((4,))],
        compiler_params=pltpu.CompilerParams(
            vmem_limit_bytes=60 * 2**20, collective_id=0, has_side_effects=True
        ),
        name="front",
    )(*args)


def back_kernel(
    grad_context,
    q_s,
    k_s,
    v_s,
    tq_s,
    tk_s,
    left_s,
    right_s,
    rank_s,
    table_rank_s,
    scale,
    early,
    tokens_in,
    tr_in,
    mix_in,
    grad_first_in,
    shares_in,
    grad_tokens,
    early_out,
    tail_out,
    tokens,
    tr_s,
    mix_weight,
    grad_first,
    shares_s,
    gl_s,
    qf_s,
    kf_s,
    gq_s,
    gk_s,
    gt_s,
    grads_s,
    tables_s,
    tail,
    sems,
    load_sems,
    *reduce_refs,
):
    arrived, crossed = reduce_refs[0], reduce_refs[1]
    groups = Groups(arrived.shape[0] // 2 + 1, crossed.shape[0] * 2)
    first = Reduction(groups, early, arrived, crossed, early_out, reduce_refs[2:8])
    second = Reduction(groups, tail, reduce_refs[8], reduce_refs[9], tail_out, reduce_refs[10:16])
    row, lane = block_iotas()
    beyond = lane >= row
    inside = (row + lane <= LANES - 1).astype(bf16)
    ends = lax.broadcasted_iota(jnp.int32, (2 * LANES, LANES), 1)
    pick_first = (ends == 0).astype(bf16)
    pick_last = (ends == LANES - 1).astype(bf16)
    flip = (row + lane == LANES - 1).astype(bf16)

    def begin(p, carry):
        pltpu.make_async_copy(shares_in.at[p], shares_s.at[p], sems.at[p]).start()
        return carry

    lax.fori_loop(0, PAIRS, begin, 0)
    loads = [
        pltpu.make_async_copy(source, target, load_sems.at[i])
        for i, (source, target) in enumerate(
            (
                (tokens_in, tokens),
                (tr_in, tr_s),
                (mix_in, mix_weight),
                (grad_first_in, grad_first),
            )
        )
    ]
    greet(groups.partners())
    first.start()
    for copy in loads:
        copy.start()
    tail[...] = jnp.zeros_like(tail)
    scale_row = spread(scale)
    low = (rank_s[...] * scale_row).astype(bf16)
    table_low = (table_rank_s[...] * scale_row).astype(bf16)

    def keep(index, values):
        for j in range(values.shape[1] // LANES):
            tail[index + j] = values[:, j * LANES : (j + 1) * LANES].astype(bf16)

    def flipped(values):
        return jnp.concatenate(
            [
                dot_nn(flip, values[b * LANES : (b + 1) * LANES, :]).astype(bf16)
                for b in range(BLOCKS)
            ],
            axis=0,
        )

    def rows_of(group):
        return [
            slice(a * LANES, (a + 1) * LANES)
            for a in range(group * BACK_GROUP, (group + 1) * BACK_GROUP)
        ]

    def grads(p, which, group):
        rows = rows_of(group)
        every = slice(rows[0].start, rows[-1].stop)
        grad = dot_nt(grad_context[p, every, :] * head_mask(which), v_s[p])
        shares = [shares_s[p, which, r, :].astype(f32) for r in rows]
        prods = [
            grad[i * LANES : (i + 1) * LANES, :] * shares[i] for i in range(BACK_GROUP)
        ]
        inner = [jnp.sum(prod, axis=1, keepdims=True) for prod in prods]
        for i, r in enumerate(rows):
            gl_s[which, r, :] = (prods[i] - shares[i] * inner[i]).astype(bf16)

    def fold(which, group, target, turn):
        rows = rows_of(group)
        turned = [
            dot_nt(flip, gl_s[which, :, r]) if turn else dot_nn(flip, gl_s[which, r, :])
            for r in rows
        ]
        for t, r in zip(turned, rows):
            target[which, r, :ROWS] = t.astype(bf16)
        for i, r in enumerate(rows):
            target[which, r, ROWS:] = fold_rows(
                turned[i], group * BACK_GROUP + i, beyond, inside, pick_first, pick_last
            ).astype(bf16)

    def close(p, which, parts):
        gc_t, k_t, q_t, tk_t, tq_t, q_rev_t, k_rev_t = parts
        half = slice(which * 64, which * 64 + 64)
        gq_t = dot_nt(jnp.concatenate([k_t[half, :], tk_t[half, :]], axis=1), qf_s[which])
        gk_t = dot_nt(jnp.concatenate([q_t[half, :], tq_t[half, :]], axis=1), kf_s[which])
        gq_s[half, :] = (gq_t * score_scale).astype(bf16)
        gk_s[half, :] = (gk_t * score_scale).astype(bf16)
        gtk = dot_nn(q_rev_t[half, :], qf_s[which, :, ROWS:])
        gtq = dot_nn(k_rev_t[half, :], kf_s[which, :, ROWS:])
        gt_s[0, half, :] = (gtq * score_scale).astype(bf16)
        gt_s[1, half, :] = (gtk * score_scale).astype(bf16)
        gt_s[2, half, :] = dot_nn(gc_t[half, :], shares_s[p, which]).astype(bf16)

    sections = BLOCKS // BACK_GROUP
    pltpu.make_async_copy(shares_in.at[0], shares_s.at[0], sems.at[0]).wait()
    for group in range(sections):
        grads(0, 0, group)

    def pair(p, carry):
        later = jnp.minimum(p + 1, PAIRS - 1)

        @pl.when(p < PAIRS - 1)
        def _():
            pltpu.make_async_copy(
                shares_in.at[later], shares_s.at[later], sems.at[later]
            ).wait()

        @pl.when(p == 2)
        def _():
            first.middle()

        @pl.when(p == 4)
        def _():
            first.last()

        parts = (
            grad_context[p].T,
            k_s[p].T,
            q_s[p].T,
            tk_s[p].T,
            tq_s[p].T,
            flipped(q_s[p]).T,
            flipped(k_s[p]).T,
        )
        for group in range(sections):
            fold(0, group, qf_s, False)
            grads(p, 1, group)
            fold(0, group, kf_s, True)
        close(p, 0, parts)
        for group in range(sections):
            fold(1, group, qf_s, False)
            grads(later, 0, group)
            fold(1, group, kf_s, True)
        close(p, 1, parts)
        lanes = pl.ds(pl.multiple_of(p * LANES, LANES), LANES)
        for b in range(BLOCKS):
            rows = slice(b * LANES, (b + 1) * LANES)
            grads_s[0, rows, lanes] = dot_nt(flip, gq_s[:, rows]).astype(bf16)
            grads_s[1, rows, lanes] = dot_nt(flip, gk_s[:, rows]).astype(bf16)
        grads_s[2, :, lanes] = gt_s[2].T
        tables_s[0, :, lanes] = gt_s[0].T
        tables_s[1, :, lanes] = gt_s[1].T
        return carry

    lax.fori_loop(0, PAIRS, pair, 0)

    for copy in loads:
        copy.wait()

    def backs(source, count):
        total = None
        lane = lax.broadcasted_iota(jnp.int32, (1, STACK), 1)
        for which in range(count):
            part = dot_nt(source[which], right_s[...])
            part = jnp.where(lane // TILE == which, part, 0.0)
            total = part if total is None else total + part
        return total

    back = backs(grads_s, 3)
    table_back = backs(tables_s, 2)
    small = (back * scale_row).astype(bf16)
    table_small = (table_back * scale_row).astype(bf16)
    left_sum = dot_tn(small, tokens[...]) + dot_tn(table_small, tr_s[...])
    low_t = low.T
    table_low_t = table_low.T
    for which in range(3):
        rows = slice(which * TILE, (which + 1) * TILE)
        right_sum = dot_nn(low_t[rows, :], grads_s[which])
        if which < 2:
            right_sum = right_sum + dot_nn(table_low_t[rows, :], tables_s[which])
        keep(which * 6, left_sum[rows, :])
        keep(18 + which * 6, right_sum)
    tail[36, :1, :STACK] = jnp.sum(
        rank_s[...] * back + table_rank_s[...] * table_back, axis=0, keepdims=True
    ).astype(bf16)
    first.finish()
    second.start()
    grad_tokens[...] = grad_first[...] + dot_nn(small, left_s[...])
    grad_tokens[...] += dot_nt(grads_s[0], mix_weight[0])
    second.middle()
    grad_tokens[...] += dot_nt(grads_s[1], mix_weight[1])
    second.last()
    grad_tokens[...] += dot_nt(grads_s[2], mix_weight[2])
    second.finish()


def back(tail_tiles, near_size, far_size, *args):
    early = args[11]
    return pl.pallas_call(
        back_kernel,
        out_shape=(
            jax.ShapeDtypeStruct((ROWS, WIDTH), f32),
            jax.ShapeDtypeStruct(early.shape, f32),
            jax.ShapeDtypeStruct((tail_tiles, TILE, LANES), bf16),
        ),
        in_specs=[vmem()] * 12 + [anywhere()] * 5,
        out_specs=(vmem(),) * 3,
        scratch_shapes=[
            pltpu.VMEM((ROWS, WIDTH), bf16),
            pltpu.VMEM((ROWS, WIDTH), bf16),
            pltpu.VMEM((3, WIDTH, WIDTH), bf16),
            pltpu.VMEM((ROWS, WIDTH), f32),
            pltpu.VMEM((PAIRS, 2, ROWS, ROWS), bf16),
            pltpu.VMEM((2, ROWS, ROWS), bf16),
            pltpu.VMEM((2, ROWS, 2 * ROWS), bf16),
            pltpu.VMEM((2, ROWS, 2 * ROWS), bf16),
            pltpu.VMEM((LANES, ROWS), bf16),
            pltpu.VMEM((LANES, ROWS), bf16),
            pltpu.VMEM((3, LANES, ROWS), bf16),
            pltpu.VMEM((3, ROWS, WIDTH), bf16),
            pltpu.VMEM((2, ROWS, WIDTH), bf16),
            pltpu.VMEM((tail_tiles, TILE, LANES), bf16),
            pltpu.SemaphoreType.DMA((PAIRS,)),
            pltpu.SemaphoreType.DMA((4,)),
        ]
        + reduction_scratch(early.shape[0], near_size, far_size, f32)
        + reduction_scratch(tail_tiles, near_size, far_size, bf16),
        compiler_params=pltpu.CompilerParams(
            vmem_limit_bytes=58 * 2**20, collective_id=1, has_side_effects=True
        ),
        name="back",
    )(*args)


def unpack_kernel(
    early,
    tail,
    tokens_in,
    tokens_out,
    left,
    scale,
    right,
    expand_left_t,
    expand_right,
    shrink_left_t,
    feed_scale,
    shrink_right,
    sem,
):
    copy = pltpu.make_async_copy(tokens_in, tokens_out, sem)
    copy.start()
    me = lax.axis_index("tensor")
    pieces = expand_right.shape[1] // LANES
    split = SPLIT_AT + me * pieces
    skip = (early.shape[0] - SPLIT_AT) // 2
    for j in range(WIDTH // LANES):
        lanes = slice(j * LANES, (j + 1) * LANES)
        for which in range(3):
            left[:, which, lanes] = tail[which * 6 + j, :RANK, :].astype(f32)
            right[:, which, lanes] = tail[18 + which * 6 + j, :RANK, :].astype(f32)
        left[:, 3, lanes] = early[j, :RANK, :]
        right[:, 3, lanes] = early[6 + j, :RANK, :]
        expand_left_t[:, lanes] = early[12 + j, :RANK, :]
        shrink_right[:, lanes] = early[18 + j, :RANK, :]
    total = lax.axis_size("tensor") * pieces
    for j in range(pieces):
        lanes = slice(j * LANES, (j + 1) * LANES)
        expand_right[:, lanes] = early[split + j, :RANK, :]
        shrink_left_t[:, lanes] = early[split + total + j, :RANK, :]
    mixed = tail[36].astype(f32)
    for which in range(3):
        scale[which : which + 1, :] = mixed[:1, which * TILE : which * TILE + RANK]
    other = early[24]
    scale[3:4, :] = other[3:4, 3 * TILE : 3 * TILE + RANK]
    feed_scale[...] = other[4:6, :RANK]
    copy.wait()


def unpack(hidden, early, tail, tokens):
    mats = jax.ShapeDtypeStruct((RANK, 4, WIDTH), f32)
    small = jax.ShapeDtypeStruct((RANK, WIDTH), f32)
    split = jax.ShapeDtypeStruct((RANK, hidden), f32)
    return pl.pallas_call(
        unpack_kernel,
        out_shape=(
            jax.ShapeDtypeStruct((ROWS, WIDTH), f32),
            mats,
            jax.ShapeDtypeStruct((4, RANK), f32),
            mats,
            small,
            split,
            split,
            jax.ShapeDtypeStruct((2, RANK), f32),
            small,
        ),
        in_specs=[vmem(), vmem(), vmem()],
        out_specs=(anywhere(),) + (vmem(),) * 8,
        scratch_shapes=[pltpu.SemaphoreType.DMA],
        name="unpack",
    )(early, tail, tokens)


def body(
    tokens,
    segment,
    live,
    mix_weight,
    out_weight,
    position_table,
    norm_gain,
    norm_bias,
    mix_left,
    mix_scale,
    mix_right,
    expand_weight,
    expand_left,
    expand_right,
    shrink_weight,
    shrink_left,
    feed_scale,
    shrink_right,
    cotangent,
):
    tensor_size = lax.axis_size("tensor")
    near_size = tensor_size * 2
    far_size = lax.axis_size("dp") // 2
    hidden = expand_weight.shape[1]
    early_tiles = -(-(SPLIT_AT + 2 * tensor_size * hidden // LANES) // near_size) * near_size
    tail_tiles = -(-37 // near_size) * near_size
    left_t = jnp.transpose(mix_left, (2, 0, 1))
    right = jnp.transpose(mix_right, (1, 0, 2))
    layer_out, grad_first, grad_context, early, q, k, v, tq, tk, tr, *adapters, shares = front(
        tensor_size,
        early_tiles,
        segment.reshape(1, ROWS),
        live.reshape(1, ROWS),
        tokens,
        position_table,
        left_t,
        right,
        mix_scale,
        norm_gain,
        norm_bias,
        expand_left.T,
        shrink_right,
        feed_scale,
        mix_weight,
        cotangent,
        out_weight,
        expand_weight,
        shrink_weight,
        expand_right,
        shrink_left.T,
    )
    grad_tokens, early, tail = back(
        tail_tiles,
        near_size,
        far_size,
        grad_context,
        q,
        k,
        v,
        tq,
        tk,
        *adapters,
        mix_scale,
        early,
        tokens,
        tr,
        mix_weight,
        grad_first,
        shares,
    )
    grad_tokens, left, scale, right, expand_left, expand_right, shrink_left, feed_scale, shrink_right = unpack(
        hidden, early, tail, grad_tokens
    )
    return (
        layer_out,
        grad_tokens,
        jnp.transpose(left, (1, 2, 0)),
        scale,
        jnp.transpose(right, (1, 0, 2)),
        expand_left.T,
        expand_right,
        shrink_left.T,
        feed_scale,
        shrink_right,
    )


def solution(mesh):
    rows = P(("dp", "tensor"), None)
    line = P(("dp", "tensor"))
    return jax.shard_map(
        body,
        mesh=mesh,
        in_specs=(
            rows,
            line,
            line,
            P(),
            P(),
            P(),
            P(),
            P(),
            P(),
            P(),
            P(),
            P(None, "tensor"),
            P(),
            P(None, "tensor"),
            P("tensor", None),
            P("tensor", None),
            P(),
            P(),
            rows,
        ),
        out_specs=(
            rows,
            rows,
            P(),
            P(),
            P(),
            P(),
            P(None, "tensor"),
            P("tensor", None),
            P(),
            P(),
        ),
        check_vma=False,
    )
```

```python
import math

import jax
import jax.numpy as jnp
from jax import lax
from jax.experimental import pallas as pl
from jax.experimental.pallas import tpu as pltpu
from jax.sharding import PartitionSpec as P

PAIRS = 6
LANES = 128
ROWS = 512
WIDTH = 768
RANK = 12
BLOCKS = ROWS // LANES
TILE = 16
GROUP = 2
BACK_GROUP = 4
STACK = 64
SPLIT_AT = 25

norm_eps = 1e-07
masked_fill = -1e30
score_scale = 1.0 / math.sqrt(192.0)
inverse_root_two = 1.0 / math.sqrt(2.0)
log_two_e = math.log2(math.e)
inverse_root_tau = 1.0 / math.sqrt(2.0 * math.pi)

f32 = jnp.float32
bf16 = jnp.bfloat16


def dot_nn(left, right):
    return jnp.dot(left, right, preferred_element_type=f32)


def dot_nt(left, right):
    return lax.dot_general(left, right, (((1,), (1,)), ((), ())), preferred_element_type=f32)


def dot_tn(left, right):
    return lax.dot_general(left, right, (((0,), (0,)), ((), ())), preferred_element_type=f32)


def column_of(row):
    n = row.shape[1]
    eye = lax.broadcasted_iota(jnp.int32, (n, n), 0) == lax.broadcasted_iota(jnp.int32, (n, n), 1)
    return jnp.sum(jnp.where(eye, row, 0.0), axis=1, keepdims=True)


def spread(scale):
    row = lax.broadcasted_iota(jnp.int32, (RANK, STACK), 0)
    lane = lax.broadcasted_iota(jnp.int32, (RANK, STACK), 1)
    total = jnp.zeros((1, STACK), f32)
    for a in range(4):
        column = column_of(scale[a : a + 1, :])
        total = total + jnp.sum(
            jnp.where(lane == row + TILE * a, column, 0.0), axis=0, keepdims=True
        )
    return total


def of_map(which):
    lane = lax.broadcasted_iota(jnp.int32, (1, STACK), 1)
    return (lane // TILE == which).astype(bf16)


def block_iotas():
    shape = (LANES, LANES)
    return lax.broadcasted_iota(jnp.int32, shape, 0), lax.broadcasted_iota(jnp.int32, shape, 1)


def head_mask(which):
    lane = lax.broadcasted_iota(jnp.int32, (1, LANES), 1)
    return ((lane >= 64) if which else (lane < 64)).astype(bf16)


def pick_tiles(scores, block, at_diag):
    first = scores[:, :1]
    last = scores[:, ROWS - 1 :]
    near = {}

    def rolled(u):
        if u not in near:
            near[u] = pltpu.roll(
                scores[:, u * LANES : (u + 1) * LANES], 1, 1, stride=1, stride_axis=0
            )
        return near[u]

    tiles = []
    for other in range(BLOCKS):
        v = other - block + 2
        if v < 0:
            tile = jnp.broadcast_to(first, (LANES, LANES))
        elif v == 0:
            tile = jnp.where(at_diag, first, rolled(0))
        elif v < 4:
            tile = jnp.where(at_diag, rolled(v - 1), rolled(v))
        elif v == 4:
            tile = jnp.where(at_diag, rolled(3), last)
        else:
            tile = jnp.broadcast_to(last, (LANES, LANES))
        tiles.append(tile)
    return jnp.concatenate(tiles, axis=1)


def row_sums(values):
    part = (
        values[:, :LANES]
        + values[:, LANES : 2 * LANES]
        + values[:, 2 * LANES : 3 * LANES]
        + values[:, 3 * LANES :]
    )
    high = part.astype(bf16)
    rest = (part - high.astype(f32)).astype(bf16)
    return dot_nn(jnp.concatenate([high, rest], axis=1), jnp.ones((2 * LANES, LANES), bf16))


def wide4(values):
    return jnp.concatenate([values] * BLOCKS, axis=1)


def fold_rows(grads, block, beyond, inside, pick_first, pick_last):
    zero = jnp.zeros((LANES, LANES), f32)
    near = {}
    low = []
    high = []
    for other in range(BLOCKS):
        v = other - block + 2
        tile = grads[:, other * LANES : (other + 1) * LANES]
        if v < 0:
            low.append(tile.astype(bf16))
        elif v > 4:
            high.append(tile.astype(bf16))
        else:
            near[v] = pltpu.roll(tile, 0, 1, stride=1, stride_axis=0)
        if v == 0:
            low.append(tile.astype(bf16) * inside)
        if v == 4:
            high.append(tile.astype(bf16) * (1 - inside))
    out = []
    for w in range(BLOCKS):
        if w in near or w + 1 in near:
            out.append(jnp.where(beyond, near.get(w + 1, zero), near.get(w, zero)))
        else:
            out.append(zero)
    if low:
        out[0] = out[0] + dot_nn(
            jnp.concatenate(low, axis=1), pick_first[: LANES * len(low), :]
        )
    if high:
        out[3] = out[3] + dot_nn(
            jnp.concatenate(high, axis=1), pick_last[: LANES * len(high), :]
        )
    return jnp.concatenate(out, axis=1)


def attend_part(
    segment,
    live,
    tokens,
    table,
    mix_weight,
    mix_copies,
    left_s,
    right_s,
    scale_row,
    rank_s,
    table_rank_s,
    shares_out,
    q_s,
    k_s,
    v_s,
    tq_s,
    tk_s,
    tr_s,
    context_s,
    shares_s,
    bias_s,
    across_s,
    work,
    sems,
    gather,
):
    row, lane = block_iotas()
    below = lane <= row
    flip = (row + lane == LANES - 1).astype(bf16)
    eye = (row == lane).astype(bf16)
    seg_row = segment[...]
    key_row = jnp.where(live[...] == 1, seg_row, -1)
    for a in range(BLOCKS):
        seg_col = jnp.broadcast_to(
            seg_row[:, a * LANES : (a + 1) * LANES].astype(f32), (LANES, LANES)
        ).T.astype(jnp.int32)
        for b in range(BLOCKS):
            same = seg_col == key_row[:, b * LANES : (b + 1) * LANES]
            if a == b:
                same = same | (row == lane)
            bias_s[a * LANES : (a + 1) * LANES, b * LANES : (b + 1) * LANES] = jnp.where(
                same, 0.0, masked_fill
            )
    for a in range(BLOCKS):
        tr_s[a * LANES : (a + 1) * LANES, :] = dot_nn(
            flip, table[(3 - a) * LANES : (4 - a) * LANES, :]
        ).astype(bf16)

    rank_s[...] = dot_nt(tokens[...], left_s[...])
    table_rank_s[...] = dot_nt(tr_s[...], left_s[...])
    low = (rank_s[...] * scale_row).astype(bf16)
    table_low = (table_rank_s[...] * scale_row).astype(bf16)

    def project(source, low, which, target):
        full = dot_nn(source, mix_weight[which]) + dot_nn(low * of_map(which), right_s[...])
        for p in range(PAIRS):
            target[p] = full[:, p * LANES : (p + 1) * LANES].astype(bf16)

    mix_copies[0].wait()
    project(tokens[...], low, 0, q_s)
    project(tr_s[...], table_low, 0, tq_s)
    mix_copies[1].wait()
    project(tokens[...], low, 1, k_s)
    project(tr_s[...], table_low, 1, tk_s)
    gather.forward_one(0)
    mix_copies[2].wait()
    project(tokens[...], low, 2, v_s)

    blocks = [slice(b * LANES, (b + 1) * LANES) for b in range(BLOCKS)]
    keys_s, queries_s, along_s, both_s = work[:4]
    context_part = work[4]

    def scores(p, which):
        mask = head_mask(which)
        keys_s[which][:, :ROWS] = dot_nt(k_s[p] * mask, tq_s[p])
        queries_s[which][:, :ROWS] = dot_nt(q_s[p] * mask, tk_s[p])

    def pick(p, which):
        for b, r in enumerate(blocks):
            values = pick_tiles(keys_s[which][r, :ROWS], b, below)
            high = values.astype(bf16)
            across_s[which, 0, r, :] = high
            across_s[which, 1, r, :] = (values - high.astype(f32)).astype(bf16)
            along_s[which][r, :ROWS] = pick_tiles(queries_s[which][r, :ROWS], b, below)

    def content(p, which):
        mask = head_mask(which)
        for r in blocks:
            both_s[which][r, :ROWS] = dot_nt(
                jnp.concatenate([q_s[p, r, :] * mask, eye, eye], axis=1),
                jnp.concatenate(
                    [k_s[p], across_s[which, 0, :, r], across_s[which, 1, :, r]], axis=1
                ),
            )

    def softmax(p, which):
        for first in range(0, BLOCKS, GROUP):
            rows = blocks[first : first + GROUP]
            totals = [
                both_s[which][r, :ROWS] + along_s[which][r, :ROWS] + bias_s[r, :] for r in rows
            ]
            peaks = [jnp.max(t, axis=1, keepdims=True) for t in totals]
            weights = [
                jnp.exp2((t - m) * (score_scale * log_two_e)) for t, m in zip(totals, peaks)
            ]
            inverses = [1.0 / jnp.sum(w, axis=1, keepdims=True) for w in weights]
            for r, w, inverse in zip(rows, weights, inverses):
                shares_s[p, which, r, :] = (w * inverse).astype(bf16)

    def mix(p, which):
        part = dot_nn(shares_s[p, which], v_s[p] * head_mask(which))
        if which == 0:
            context_part[:, :LANES] = part
        else:
            lanes = slice(p * LANES, (p + 1) * LANES)
            if not isinstance(p, int):
                lanes = pl.ds(pl.multiple_of(p * LANES, LANES), LANES)
            context_s[:, lanes] = (context_part[:, :LANES] + part).astype(bf16)

    stages = (mix, softmax, content, pick, scores)

    def step(base, extra, first=0, last=4):
        for n in range(first, last + 1):
            head = extra - (4 - n)
            stages[n](base + head // 2, head % 2)

    def give(p):
        pltpu.make_async_copy(shares_s.at[p], shares_out.at[p], sems.at[p]).start()

    for extra in range(4):
        if extra == 2:
            gather.forward_one(1)
        step(0, extra, first=4 - extra)

    def pair(base, carry):
        for at, forward, k in (
            (2, gather.forward_one, 2),
            (3, gather.forward_two, 0),
            (4, gather.forward_one, 3),
            (5, gather.forward_two, 1),
        ):

            @pl.when(base == at)
            def _():
                forward(k)

        step(base, 0)
        step(base, 1)
        give(base - 2)
        return carry

    lax.fori_loop(2, PAIRS, pair, 0)
    gather.forward_one(4)
    step(PAIRS, 0, last=3)
    gather.forward_two(2)
    step(PAIRS, 1, last=2)
    give(PAIRS - 2)
    step(PAIRS, 2, last=1)
    gather.forward_two(3)
    give(PAIRS - 1)
    step(PAIRS, 3, last=0)


def vmem():
    return pl.BlockSpec(memory_space=pltpu.VMEM)


def anywhere():
    return pl.BlockSpec(memory_space=pl.ANY)


def remote(source, target, send, recv, device):
    return pltpu.make_async_remote_copy(
        src_ref=source,
        dst_ref=target,
        send_sem=send,
        recv_sem=recv,
        device_id=device,
        device_id_type=pl.DeviceIdType.MESH,
    )


def greet(devices):
    barrier = pltpu.get_barrier_semaphore()
    for device in devices:
        pl.semaphore_signal(
            barrier, inc=1, device_id=device, device_id_type=pl.DeviceIdType.MESH
        )
    pl.semaphore_wait(barrier, len(devices))


class Groups:
    def __init__(self, tensor_size, dp_size):
        self.near_size = tensor_size * 2
        self.far_size = dp_size // 2
        self.tensor = lax.axis_index("tensor")
        self.dp = lax.axis_index("dp")
        self.near = self.tensor * 2 + self.dp % 2
        self.far = self.dp // 2

    def near_index(self, step):
        return (self.near + step) % self.near_size

    def near_device(self, step):
        index = self.near_index(step)
        return {"dp": self.far * 2 + index % 2, "tensor": index // 2}

    def far_device(self, step):
        index = (self.far + step) % self.far_size
        return {"dp": index * 2 + self.dp % 2, "tensor": self.tensor}

    def partners(self):
        return [self.near_device(s) for s in range(1, self.near_size)] + [
            self.far_device(s) for s in range(1, self.far_size)
        ]


class Reduction:
    def __init__(self, groups, pack, arrived, crossed, out, sems):
        self.groups = groups
        self.pack = pack
        self.arrived = arrived
        self.crossed = crossed
        self.out = out
        self.send_one, self.recv_one, self.send_two, self.recv_two, self.send_three, self.recv_three = sems
        self.size = pack.shape[0] // groups.near_size

    def part(self, ref, index):
        return ref.at[pl.ds(index * self.size, self.size)]

    def scatter(self):
        g = self.groups
        return [
            remote(
                self.part(self.pack, g.near_index(s)),
                self.arrived.at[s - 1],
                self.send_one.at[s - 1],
                self.recv_one.at[s - 1],
                g.near_device(s),
            )
            for s in range(1, g.near_size)
        ]

    def cross(self):
        g = self.groups
        return [
            remote(
                self.crossed.at[g.far],
                self.crossed.at[g.far],
                self.send_two.at[s - 1],
                self.recv_two.at[s - 1],
                g.far_device(s),
            )
            for s in range(1, g.far_size)
        ]

    def gather(self):
        g = self.groups
        return [
            remote(
                self.part(self.out, g.near),
                self.part(self.out, g.near),
                self.send_three.at[s - 1],
                self.recv_three.at[s - 1],
                g.near_device(s),
            )
            for s in range(1, g.near_size)
        ]

    def start(self):
        for copy in self.scatter():
            copy.start()

    def middle(self):
        g = self.groups
        for copy in self.scatter():
            copy.wait()
        total = self.pack[pl.ds(g.near * self.size, self.size)].astype(f32)
        for s in range(1, g.near_size):
            total = total + self.arrived[s - 1].astype(f32)
        self.crossed[g.far] = total.astype(self.crossed.dtype)
        for copy in self.cross():
            copy.start()

    def last(self):
        g = self.groups
        for copy in self.cross():
            copy.wait()
        total = self.crossed[0].astype(f32)
        for s in range(1, g.far_size):
            total = total + self.crossed[s].astype(f32)
        self.out[pl.ds(g.near * self.size, self.size)] = total.astype(self.out.dtype)
        for copy in self.gather():
            copy.start()

    def finish(self):
        for copy in self.gather():
            copy.wait()


def reduction_scratch(tiles, near_size, far_size, kind):
    size = tiles // near_size
    near = (near_size - 1,)
    far = (max(far_size - 1, 1),)
    dma = pltpu.SemaphoreType.DMA
    return [
        pltpu.VMEM((near_size - 1, size, TILE, LANES), kind),
        pltpu.VMEM((far_size, size, TILE, LANES), kind),
        dma(near),
        dma(near),
        dma(far),
        dma(far),
        dma(near),
        dma(near),
    ]


class Gather:
    def __init__(self, size, sources, targets, sems):
        self.size = size
        self.far = size // 2
        self.sources = sources
        self.targets = targets
        self.across_s, self.across_r, self.pair_s, self.pair_r, self.one_s, self.one_r, self.two_s, self.two_r = sems[:8]
        self.whole_s, self.whole_r, self.small_s, self.small_r, self.own = sems[8:]
        self.tensor = lax.axis_index("tensor")
        self.dp = lax.axis_index("dp")
        self.bit = self.dp % 2
        self.pair = {"dp": self.dp + 1 - 2 * self.bit, "tensor": self.tensor}
        self.near = self.tensor + 1 - 2 * (self.tensor % 2)
        self.core = {"dp": self.dp, "tensor": self.near}

    def device(self, step):
        return {"dp": self.dp, "tensor": (self.tensor + step) % self.size}

    def partners(self):
        return [self.device(s) for s in range(1, self.size)] + [self.pair]

    def slot(self, order):
        first = self.tensor if isinstance(order, int) and order % 2 == 0 else None
        if first is None:
            first = self.tensor + (order % 2) * (self.near - self.tensor)
        return (first + self.size - 2 * (order // 2)) % self.size

    def rows(self, which, part, bit):
        count = self.sources[which].shape[0] // 6
        return pl.ds((2 * part + bit) * count, count)

    def across(self, s, k):
        which, part = k // 3, k % 3
        rows = self.rows(which, part, self.bit)
        return remote(
            self.sources[which].at[rows, :],
            self.targets[which].at[self.tensor, rows, :],
            self.across_s.at[s - 1, k],
            self.across_r.at[s - 1, k],
            self.device(2 * s),
        )

    def onward(self, s, k, bit, sends, recvs, device):
        which, part = k // 3, k % 3
        rows = self.rows(which, part, bit)
        ref = self.targets[which].at[self.slot(2 * s), rows, :]
        return remote(ref, ref, sends.at[s - 1, k], recvs.at[s - 1, k], device)

    def swap(self, s, k):
        return self.onward(s, k, self.bit, self.pair_s, self.pair_r, self.pair)

    def share_one(self, s, k):
        return self.onward(s, k, self.bit, self.one_s, self.one_r, self.core)

    def share_two(self, s, k):
        return self.onward(s, k, 1 - self.bit, self.two_s, self.two_r, self.core)

    def whole(self, which):
        return remote(
            self.sources[which],
            self.targets[which].at[self.tensor],
            self.whole_s.at[which],
            self.whole_r.at[which],
            self.core,
        )

    def small(self, s, which):
        return remote(
            self.sources[which],
            self.targets[which].at[self.tensor],
            self.small_s.at[s - 1, which - 2],
            self.small_r.at[s - 1, which - 2],
            self.device(s),
        )

    def keep(self, which):
        return pltpu.make_async_copy(
            self.sources[which], self.targets[which].at[self.tensor], self.own.at[which]
        )

    def start(self):
        for which in range(4):
            self.keep(which).start()
        greet(self.partners())
        for k in range(6):
            for s in range(1, self.far):
                self.across(s, k).start()
        for which in range(2):
            self.whole(which).start()
        for s in range(1, self.size):
            for which in (2, 3):
                self.small(s, which).start()

    def forward_one(self, k):
        for s in range(1, self.far):
            self.across(s, k).wait_recv()
            self.swap(s, k).start()
            self.share_one(s, k).start()

    def forward_two(self, k):
        for s in range(1, self.far):
            self.swap(s, k).wait_recv()
            self.share_two(s, k).start()

    def arrive(self, order):
        if order == 0:
            for which in range(4):
                self.keep(which).wait()
            for s in range(1, self.size):
                for which in (2, 3):
                    self.small(s, which).wait()
        elif order == 1:
            for which in range(2):
                self.whole(which).wait()
        elif order % 2 == 1:
            for k in range(6):
                self.share_one(order // 2, k).wait_recv()
                self.share_two(order // 2, k).wait_recv()

    def finish(self):
        for s in range(1, self.far):
            for k in range(6):
                self.across(s, k).wait_send()
                self.swap(s, k).wait_send()
                self.share_one(s, k).wait_send()
                self.share_two(s, k).wait_send()


def norm_parts(values):
    center = values - jnp.mean(values, axis=-1, keepdims=True)
    root = lax.rsqrt(jnp.mean(center * center, axis=-1, keepdims=True) + norm_eps)
    return center * root, root


def norm_back(scaled, unit, root):
    return root * (
        scaled
        - jnp.mean(scaled, axis=-1, keepdims=True)
        - unit * jnp.mean(scaled * unit, axis=-1, keepdims=True)
    )


def feed_part(
    tokens,
    cotangent,
    cotangent_copy,
    out_weight,
    out_copy,
    left_s,
    right_s,
    scale_row,
    gain,
    shift,
    expand_left_t,
    expand_right,
    shrink_left_t,
    shrink_right,
    feed_scale,
    layer_out,
    layer_copy,
    grad_first_out,
    grad_context_out,
    pack,
    expand_s,
    shrink_s,
    x_s,
    normed_s,
    hidden_s,
    act_s,
    slope_s,
    branch_s,
    context_s,
    one_s,
    two_s,
    pre_s,
    gather,
):
    chunks = expand_s.shape[0]
    pieces = expand_s.shape[2] // LANES
    hidden = expand_s.shape[2]

    def part_of(order):
        place = order * hidden % WIDTH
        return order * hidden // WIDTH, slice(None), slice(place, place + hidden)

    pack[...] = jnp.zeros_like(pack)

    def keep(first, values):
        for j in range(values.shape[1] // LANES):
            pack[first + j, :RANK, :] = values[:, j * LANES : (j + 1) * LANES]

    lam_one = feed_scale[0:1, :]
    lam_two = feed_scale[1:2, :]
    step = LANES
    steps = ROWS // step

    out_copy.wait()
    gather.forward_one(5)
    out_rank = dot_nt(context_s[...], left_s[...])
    out_low = (out_rank * scale_row).astype(bf16) * of_map(3)
    x_s[...] = dot_nn(context_s[...], out_weight[...]) + dot_nn(out_low, right_s[...])

    def first_norm(i, carry):
        rows = pl.ds(i * step, step)
        values = tokens[rows, :].astype(f32) + x_s[rows, :]
        x_s[rows, :] = values
        unit, root = norm_parts(values)
        normed = unit * gain[0:1, :] + shift[0:1, :]
        normed_s[rows, :] = normed
        hidden_s[rows, :] = normed.astype(bf16)
        return carry

    lax.fori_loop(0, steps, first_norm, 0)
    gather.forward_two(4)

    one_rank = dot_nt(hidden_s[...], expand_left_t[...])
    one_low = (one_rank * lam_one).astype(bf16)
    def expanded(order):
        if order == min(2, chunks - 1):
            gather.forward_two(5)
        gather.arrive(order)
        c = gather.slot(order)
        pre_s[order % 2, :, :hidden] = dot_nn(hidden_s[...], expand_s[c]) + dot_nn(one_low, expand_right[c])

    two_rank = None
    expanded(0)
    for order in range(chunks):
        if order + 1 < chunks:
            expanded(order + 1)
        pre = pre_s[order % 2, :, :hidden]
        cdf = 0.5 + 0.5 * lax.erf(pre * inverse_root_two)
        act_s[part_of(order)] = (pre * cdf).astype(bf16)
        slope_s[part_of(order)] = cdf + pre * jnp.exp(-0.5 * pre * pre) * inverse_root_tau
        c = gather.slot(order)
        part = dot_nn(act_s[part_of(order)], shrink_s[c])
        branch_s[...] = part if order == 0 else branch_s[...] + part
        part = dot_nt(act_s[part_of(order)], shrink_left_t[c])
        two_s[...] = part if order == 0 else two_s[...] + part
    two_rank = two_s[...]
    gather.finish()
    two_low = (two_rank * lam_two).astype(bf16)
    branch_s[...] += dot_nn(two_low, shrink_right[...])

    cotangent_copy.wait()

    def second_norm(i, carry):
        rows = pl.ds(i * step, step)
        unit, root = norm_parts(normed_s[rows, :] + branch_s[rows, :])
        layer_out[rows, :] = (unit * gain[1:2, :] + shift[1:2, :]).astype(bf16)
        grad = norm_back(cotangent[rows, :].astype(f32) * gain[1:2, :], unit, root)
        branch_s[rows, :] = grad
        return carry

    lax.fori_loop(0, steps, second_norm, 0)
    layer_copy.start()
    grad_branch = branch_s[...].astype(bf16)
    two_back = dot_nt(grad_branch, shrink_right[...])
    two_small = (two_back * lam_two).astype(bf16)
    two_small_t = two_small.T
    one_low_t = one_low.T
    keep(18, dot_tn(two_low, grad_branch))
    pack[24, 5:6, :RANK] = jnp.sum(two_rank * two_back, axis=0, keepdims=True)

    def shrunk(order):
        c = gather.slot(order)
        pre_s[order % 2, :, :hidden] = dot_nt(grad_branch, shrink_s[c]) + dot_nn(two_small, shrink_left_t[c])

    shrunk(0)
    for order in range(chunks):
        if order + 1 < chunks:
            shrunk(order + 1)
        c = gather.slot(order)
        grad_pre = (pre_s[order % 2, :, :hidden] * slope_s[part_of(order)]).astype(bf16)
        keep(SPLIT_AT + (chunks + c) * pieces, dot_nn(two_small_t, act_s[part_of(order)]))
        keep(SPLIT_AT + c * pieces, dot_nn(one_low_t, grad_pre))
        branch_s[...] += dot_nt(grad_pre, expand_s[c])
        part = dot_nt(grad_pre, expand_right[c])
        one_s[...] = part if order == 0 else one_s[...] + part
    one_back = one_s[...]
    one_small = (one_back * lam_one).astype(bf16)
    branch_s[...] += dot_nn(one_small, expand_left_t[...])
    keep(12, dot_tn(one_small, hidden_s[...]))
    pack[24, 4:5, :RANK] = jnp.sum(one_rank * one_back, axis=0, keepdims=True)

    def first_back(i, carry):
        rows = pl.ds(i * step, step)
        unit, root = norm_parts(x_s[rows, :])
        grad_first_out[rows, :] = norm_back(branch_s[rows, :] * gain[0:1, :], unit, root)
        return carry

    lax.fori_loop(0, steps, first_back, 0)
    grad_attended = grad_first_out[...].astype(bf16)
    out_back = dot_nt(grad_attended, right_s[...])
    out_small = (out_back * scale_row).astype(bf16) * of_map(3)
    grad_context = dot_nt(grad_attended, out_weight[...]) + dot_nn(out_small, left_s[...])
    for p in range(PAIRS):
        grad_context_out[p] = grad_context[:, p * LANES : (p + 1) * LANES].astype(bf16)
    keep(0, dot_tn(out_small, context_s[...])[3 * TILE : 3 * TILE + RANK, :])
    keep(6, dot_tn(out_low, grad_attended)[3 * TILE : 3 * TILE + RANK, :])
    pack[24, 3:4, :STACK] = jnp.sum(out_rank * out_back, axis=0, keepdims=True)


def front_kernel(
    segment,
    live,
    tokens,
    table,
    left_t,
    right,
    scale,
    gain,
    shift,
    expand_left_t,
    shrink_right,
    feed_scale,
    mix_weight,
    cotangent,
    out_weight,
    expand,
    shrink,
    expand_right,
    shrink_left_t,
    grad_first,
    grad_context,
    pack,
    layer_to,
    q_to,
    k_to,
    v_to,
    tq_to,
    tk_to,
    tr_to,
    left_to,
    right_to,
    rank_to,
    table_rank_to,
    shares_out,
    layer_s,
    q_s,
    k_s,
    v_s,
    tq_s,
    tk_s,
    tr_s,
    left_s,
    right_s,
    rank_s,
    table_rank_s,
    mix_s,
    cotangent_s,
    out_s,
    expand_s,
    shrink_s,
    expand_right_s,
    shrink_left_s,
    shares_s,
    bias_s,
    across_s,
    x_s,
    normed_s,
    hidden_s,
    act_s,
    slope_s,
    branch_s,
    context_s,
    one_s,
    two_s,
    pre_s,
    share_sems,
    load_sems,
    keep_sems,
    *gather_sems,
):
    mix_copies = [
        pltpu.make_async_copy(mix_weight.at[i], mix_s.at[i], load_sems.at[i]) for i in range(3)
    ]
    cotangent_copy = pltpu.make_async_copy(cotangent, cotangent_s, load_sems.at[3])
    out_copy = pltpu.make_async_copy(out_weight, out_s, load_sems.at[4])
    for copy in mix_copies:
        copy.start()
    gather = Gather(
        expand_s.shape[0],
        (expand, shrink, expand_right, shrink_left_t),
        (expand_s, shrink_s, expand_right_s, shrink_left_s),
        gather_sems,
    )
    gather.start()
    cotangent_copy.start()
    out_copy.start()
    left_s[...] = jnp.zeros_like(left_s)
    right_s[...] = jnp.zeros_like(right_s)
    for a in range(4):
        left_s[a * TILE : a * TILE + RANK, :] = left_t[:, a, :]
        right_s[a * TILE : a * TILE + RANK, :] = right[:, a, :]
    scale_row = spread(scale)
    attend_part(
        segment,
        live,
        tokens,
        table,
        mix_s,
        mix_copies,
        left_s,
        right_s,
        scale_row,
        rank_s,
        table_rank_s,
        shares_out,
        q_s,
        k_s,
        v_s,
        tq_s,
        tk_s,
        tr_s,
        context_s,
        shares_s,
        bias_s,
        across_s,
        (
            (slope_s.at[0], slope_s.at[1]),
            (slope_s.at[2], slope_s.at[3]),
            (pre_s.at[0], pre_s.at[1]),
            (x_s, normed_s),
            branch_s,
        ),
        share_sems,
        gather,
    )
    kept = [
        pltpu.make_async_copy(source, target, keep_sems.at[i])
        for i, (source, target) in enumerate(
            (
                (layer_s, layer_to),
                (q_s, q_to),
                (k_s, k_to),
                (v_s, v_to),
                (tq_s, tq_to),
                (tk_s, tk_to),
                (tr_s, tr_to),
                (left_s, left_to),
                (right_s, right_to),
                (rank_s, rank_to),
                (table_rank_s, table_rank_to),
            )
        )
    ]
    for copy in kept[1:]:
        copy.start()
    feed_part(
        tokens,
        cotangent_s,
        cotangent_copy,
        out_s,
        out_copy,
        left_s,
        right_s,
        scale_row,
        gain,
        shift,
        expand_left_t,
        expand_right_s,
        shrink_left_s,
        shrink_right,
        feed_scale,
        layer_s,
        kept[0],
        grad_first,
        grad_context,
        pack,
        expand_s,
        shrink_s,
        x_s,
        normed_s,
        hidden_s,
        act_s,
        slope_s,
        branch_s,
        context_s,
        one_s,
        two_s,
        pre_s,
        gather,
    )

    def finish(p, carry):
        pltpu.make_async_copy(shares_s.at[p], shares_out.at[p], share_sems.at[p]).wait()
        return carry

    lax.fori_loop(0, PAIRS, finish, 0)
    for copy in kept:
        copy.wait()


def front(size, tiles, *args):
    hidden = args[15].shape[1]
    wide = size * hidden // WIDTH
    piece = jax.ShapeDtypeStruct((PAIRS, ROWS, LANES), bf16)
    rows = jax.ShapeDtypeStruct((ROWS, WIDTH), bf16)
    dma = pltpu.SemaphoreType.DMA
    steps = (max(size // 2 - 1, 1), 6)
    stack = jax.ShapeDtypeStruct((STACK, WIDTH), bf16)
    rank = jax.ShapeDtypeStruct((ROWS, STACK), f32)
    kept = (rows, piece, piece, piece, piece, piece, rows, stack, stack, rank, rank)
    return pl.pallas_call(
        front_kernel,
        out_shape=(
            jax.ShapeDtypeStruct((ROWS, WIDTH), f32),
            piece,
            jax.ShapeDtypeStruct((tiles, TILE, LANES), f32),
        )
        + kept
        + (jax.ShapeDtypeStruct((PAIRS, 2, ROWS, ROWS), bf16),),
        in_specs=[vmem()] * 12 + [anywhere()] * 7,
        out_specs=(vmem(),) * 3 + (anywhere(),) * 12,
        scratch_shapes=[pltpu.VMEM(array.shape, array.dtype) for array in kept]
        + [
            pltpu.VMEM((3, WIDTH, WIDTH), bf16),
            pltpu.VMEM((ROWS, WIDTH), bf16),
            pltpu.VMEM((WIDTH, WIDTH), bf16),
            pltpu.VMEM((size, WIDTH, hidden), bf16),
            pltpu.VMEM((size, hidden, WIDTH), bf16),
            pltpu.VMEM((size, RANK, hidden), bf16),
            pltpu.VMEM((size, RANK, hidden), bf16),
            pltpu.VMEM((PAIRS, 2, ROWS, ROWS), bf16),
            pltpu.VMEM((ROWS, ROWS), f32),
            pltpu.VMEM((2, 2, ROWS, ROWS), bf16),
            pltpu.VMEM((ROWS, WIDTH), f32),
            pltpu.VMEM((ROWS, WIDTH), f32),
            pltpu.VMEM((ROWS, WIDTH), bf16),
            pltpu.VMEM((wide, ROWS, WIDTH), bf16),
            pltpu.VMEM((wide, ROWS, WIDTH), f32),
            pltpu.VMEM((ROWS, WIDTH), f32),
            pltpu.VMEM((ROWS, WIDTH), bf16),
            pltpu.VMEM((ROWS, RANK), f32),
            pltpu.VMEM((ROWS, RANK), f32),
            pltpu.VMEM((2, ROWS, WIDTH), f32),
            dma((PAIRS,)),
            dma((5,)),
            dma((len(kept),)),
        ]
        + [dma(steps)] * 8
        + [dma((2,))] * 2
        + [dma((size - 1, 2))] * 2
        + [dma((4,))],
        compiler_params=pltpu.CompilerParams(
            vmem_limit_bytes=60 * 2**20, collective_id=0, has_side_effects=True
        ),
        name="front",
    )(*args)


def back_kernel(
    left_s,
    right_s,
    rank_s,
    table_rank_s,
    scale,
    early,
    grad_context_in,
    q_in,
    k_in,
    v_in,
    tq_in,
    tk_in,
    tokens_in,
    tr_in,
    mix_in,
    grad_first_in,
    shares_in,
    grad_tokens,
    early_out,
    tail_out,
    grad_context,
    q_s,
    k_s,
    v_s,
    tq_s,
    tk_s,
    tokens,
    tr_s,
    mix_weight,
    grad_first,
    shares_s,
    gl_s,
    qf_s,
    kf_s,
    gq_s,
    gk_s,
    gt_s,
    grads_s,
    tables_s,
    tail,
    sems,
    load_sems,
    *reduce_refs,
):
    arrived, crossed = reduce_refs[0], reduce_refs[1]
    groups = Groups(arrived.shape[0] // 2 + 1, crossed.shape[0] * 2)
    first = Reduction(groups, early, arrived, crossed, early_out, reduce_refs[2:8])
    second = Reduction(groups, tail, reduce_refs[8], reduce_refs[9], tail_out, reduce_refs[10:16])
    row, lane = block_iotas()
    beyond = lane >= row
    inside = (row + lane <= LANES - 1).astype(bf16)
    ends = lax.broadcasted_iota(jnp.int32, (2 * LANES, LANES), 1)
    pick_first = (ends == 0).astype(bf16)
    pick_last = (ends == LANES - 1).astype(bf16)
    flip = (row + lane == LANES - 1).astype(bf16)

    needed = [
        pltpu.make_async_copy(source, target, load_sems.at[4 + i])
        for i, (source, target) in enumerate(
            (
                (grad_context_in, grad_context),
                (v_in, v_s),
                (q_in, q_s),
                (k_in, k_s),
                (tq_in, tq_s),
                (tk_in, tk_s),
            )
        )
    ]
    for copy in needed:
        copy.start()

    def begin(p, carry):
        pltpu.make_async_copy(shares_in.at[p], shares_s.at[p], sems.at[p]).start()
        return carry

    lax.fori_loop(0, PAIRS, begin, 0)
    loads = [
        pltpu.make_async_copy(source, target, load_sems.at[i])
        for i, (source, target) in enumerate(
            (
                (tokens_in, tokens),
                (tr_in, tr_s),
                (mix_in, mix_weight),
                (grad_first_in, grad_first),
            )
        )
    ]
    greet(groups.partners())
    first.start()
    for copy in loads:
        copy.start()
    for copy in needed:
        copy.wait()
    tail[...] = jnp.zeros_like(tail)
    scale_row = spread(scale)
    low = (rank_s[...] * scale_row).astype(bf16)
    table_low = (table_rank_s[...] * scale_row).astype(bf16)

    def keep(index, values):
        for j in range(values.shape[1] // LANES):
            tail[index + j] = values[:, j * LANES : (j + 1) * LANES].astype(bf16)

    def flipped(values):
        return jnp.concatenate(
            [
                dot_nn(flip, values[b * LANES : (b + 1) * LANES, :]).astype(bf16)
                for b in range(BLOCKS)
            ],
            axis=0,
        )

    def rows_of(group):
        return [
            slice(a * LANES, (a + 1) * LANES)
            for a in range(group * BACK_GROUP, (group + 1) * BACK_GROUP)
        ]

    def grads(p, which, group):
        rows = rows_of(group)
        every = slice(rows[0].start, rows[-1].stop)
        grad = dot_nt(grad_context[p, every, :] * head_mask(which), v_s[p])
        shares = [shares_s[p, which, r, :].astype(f32) for r in rows]
        prods = [
            grad[i * LANES : (i + 1) * LANES, :] * shares[i] for i in range(BACK_GROUP)
        ]
        inner = [jnp.sum(prod, axis=1, keepdims=True) for prod in prods]
        for i, r in enumerate(rows):
            gl_s[which, r, :] = (prods[i] - shares[i] * inner[i]).astype(bf16)

    def fold(which, group, target, turn):
        rows = rows_of(group)
        turned = [
            dot_nt(flip, gl_s[which, :, r]) if turn else dot_nn(flip, gl_s[which, r, :])
            for r in rows
        ]
        for t, r in zip(turned, rows):
            target[which, r, :ROWS] = t.astype(bf16)
        for i, r in enumerate(rows):
            target[which, r, ROWS:] = fold_rows(
                turned[i], group * BACK_GROUP + i, beyond, inside, pick_first, pick_last
            ).astype(bf16)

    def close(p, which, parts):
        gc_t, k_t, q_t, tk_t, tq_t, q_rev_t, k_rev_t = parts
        half = slice(which * 64, which * 64 + 64)
        gq_t = dot_nt(jnp.concatenate([k_t[half, :], tk_t[half, :]], axis=1), qf_s[which])
        gk_t = dot_nt(jnp.concatenate([q_t[half, :], tq_t[half, :]], axis=1), kf_s[which])
        gq_s[half, :] = (gq_t * score_scale).astype(bf16)
        gk_s[half, :] = (gk_t * score_scale).astype(bf16)
        gtk = dot_nn(q_rev_t[half, :], qf_s[which, :, ROWS:])
        gtq = dot_nn(k_rev_t[half, :], kf_s[which, :, ROWS:])
        gt_s[0, half, :] = (gtq * score_scale).astype(bf16)
        gt_s[1, half, :] = (gtk * score_scale).astype(bf16)
        gt_s[2, half, :] = dot_nn(gc_t[half, :], shares_s[p, which]).astype(bf16)

    sections = BLOCKS // BACK_GROUP
    pltpu.make_async_copy(shares_in.at[0], shares_s.at[0], sems.at[0]).wait()
    for group in range(sections):
        grads(0, 0, group)

    def pair(p, carry):
        later = jnp.minimum(p + 1, PAIRS - 1)

        @pl.when(p < PAIRS - 1)
        def _():
            pltpu.make_async_copy(
                shares_in.at[later], shares_s.at[later], sems.at[later]
            ).wait()

        @pl.when(p == 2)
        def _():
            first.middle()

        @pl.when(p == 4)
        def _():
            first.last()

        parts = (
            grad_context[p].T,
            k_s[p].T,
            q_s[p].T,
            tk_s[p].T,
            tq_s[p].T,
            flipped(q_s[p]).T,
            flipped(k_s[p]).T,
        )
        for group in range(sections):
            fold(0, group, qf_s, False)
            grads(p, 1, group)
            fold(0, group, kf_s, True)
        close(p, 0, parts)
        for group in range(sections):
            fold(1, group, qf_s, False)
            grads(later, 0, group)
            fold(1, group, kf_s, True)
        close(p, 1, parts)
        lanes = pl.ds(pl.multiple_of(p * LANES, LANES), LANES)
        for b in range(BLOCKS):
            rows = slice(b * LANES, (b + 1) * LANES)
            grads_s[0, rows, lanes] = dot_nt(flip, gq_s[:, rows]).astype(bf16)
            grads_s[1, rows, lanes] = dot_nt(flip, gk_s[:, rows]).astype(bf16)
        grads_s[2, :, lanes] = gt_s[2].T
        tables_s[0, :, lanes] = gt_s[0].T
        tables_s[1, :, lanes] = gt_s[1].T
        return carry

    lax.fori_loop(0, PAIRS, pair, 0)

    for copy in loads:
        copy.wait()

    def backs(source, count):
        total = None
        lane = lax.broadcasted_iota(jnp.int32, (1, STACK), 1)
        for which in range(count):
            part = dot_nt(source[which], right_s[...])
            part = jnp.where(lane // TILE == which, part, 0.0)
            total = part if total is None else total + part
        return total

    back = backs(grads_s, 3)
    table_back = backs(tables_s, 2)
    small = (back * scale_row).astype(bf16)
    table_small = (table_back * scale_row).astype(bf16)
    left_sum = dot_tn(small, tokens[...]) + dot_tn(table_small, tr_s[...])
    low_t = low.T
    table_low_t = table_low.T
    for which in range(3):
        rows = slice(which * TILE, (which + 1) * TILE)
        right_sum = dot_nn(low_t[rows, :], grads_s[which])
        if which < 2:
            right_sum = right_sum + dot_nn(table_low_t[rows, :], tables_s[which])
        keep(which * 6, left_sum[rows, :])
        keep(18 + which * 6, right_sum)
    tail[36, :1, :STACK] = jnp.sum(
        rank_s[...] * back + table_rank_s[...] * table_back, axis=0, keepdims=True
    ).astype(bf16)
    first.finish()
    second.start()
    grad_tokens[...] = grad_first[...] + dot_nn(small, left_s[...])
    grad_tokens[...] += dot_nt(grads_s[0], mix_weight[0])
    second.middle()
    grad_tokens[...] += dot_nt(grads_s[1], mix_weight[1])
    second.last()
    grad_tokens[...] += dot_nt(grads_s[2], mix_weight[2])
    second.finish()


def back(tail_tiles, near_size, far_size, *args):
    early = args[5]
    piece = pltpu.VMEM((PAIRS, ROWS, LANES), bf16)
    return pl.pallas_call(
        back_kernel,
        out_shape=(
            jax.ShapeDtypeStruct((ROWS, WIDTH), f32),
            jax.ShapeDtypeStruct(early.shape, f32),
            jax.ShapeDtypeStruct((tail_tiles, TILE, LANES), bf16),
        ),
        in_specs=[vmem()] * 6 + [anywhere()] * 11,
        out_specs=(vmem(),) * 3,
        scratch_shapes=[piece] * 6
        + [
            pltpu.VMEM((ROWS, WIDTH), bf16),
            pltpu.VMEM((ROWS, WIDTH), bf16),
            pltpu.VMEM((3, WIDTH, WIDTH), bf16),
            pltpu.VMEM((ROWS, WIDTH), f32),
            pltpu.VMEM((PAIRS, 2, ROWS, ROWS), bf16),
            pltpu.VMEM((2, ROWS, ROWS), bf16),
            pltpu.VMEM((2, ROWS, 2 * ROWS), bf16),
            pltpu.VMEM((2, ROWS, 2 * ROWS), bf16),
            pltpu.VMEM((LANES, ROWS), bf16),
            pltpu.VMEM((LANES, ROWS), bf16),
            pltpu.VMEM((3, LANES, ROWS), bf16),
            pltpu.VMEM((3, ROWS, WIDTH), bf16),
            pltpu.VMEM((2, ROWS, WIDTH), bf16),
            pltpu.VMEM((tail_tiles, TILE, LANES), bf16),
            pltpu.SemaphoreType.DMA((PAIRS,)),
            pltpu.SemaphoreType.DMA((10,)),
        ]
        + reduction_scratch(early.shape[0], near_size, far_size, f32)
        + reduction_scratch(tail_tiles, near_size, far_size, bf16),
        compiler_params=pltpu.CompilerParams(
            vmem_limit_bytes=58 * 2**20, collective_id=1, has_side_effects=True
        ),
        name="back",
    )(*args)


def unpack_kernel(
    early,
    tail,
    tokens_in,
    layer_in,
    tokens_out,
    layer_out,
    left,
    scale,
    right,
    expand_left_t,
    expand_right,
    shrink_left_t,
    feed_scale,
    shrink_right,
    tokens_s,
    layer_s,
    sems,
):
    ins = []
    outs = []
    for i in range(4):
        rows = pl.ds(i * LANES, LANES)
        for n, (source, held, target) in enumerate(
            ((tokens_in, tokens_s, tokens_out), (layer_in, layer_s, layer_out))
        ):
            ins.append(
                pltpu.make_async_copy(source.at[rows, :], held.at[rows, :], sems.at[n, i])
            )
            outs.append(
                pltpu.make_async_copy(held.at[rows, :], target.at[rows, :], sems.at[2 + n, i])
            )
    for copy in ins:
        copy.start()
    for copy, onward in zip(ins, outs):
        copy.wait()
        onward.start()
    me = lax.axis_index("tensor")
    pieces = expand_right.shape[1] // LANES
    split = SPLIT_AT + me * pieces
    skip = (early.shape[0] - SPLIT_AT) // 2
    for j in range(WIDTH // LANES):
        lanes = slice(j * LANES, (j + 1) * LANES)
        for which in range(3):
            left[:, which, lanes] = tail[which * 6 + j, :RANK, :].astype(f32)
            right[:, which, lanes] = tail[18 + which * 6 + j, :RANK, :].astype(f32)
        left[:, 3, lanes] = early[j, :RANK, :]
        right[:, 3, lanes] = early[6 + j, :RANK, :]
        expand_left_t[:, lanes] = early[12 + j, :RANK, :]
        shrink_right[:, lanes] = early[18 + j, :RANK, :]
    total = lax.axis_size("tensor") * pieces
    for j in range(pieces):
        lanes = slice(j * LANES, (j + 1) * LANES)
        expand_right[:, lanes] = early[split + j, :RANK, :]
        shrink_left_t[:, lanes] = early[split + total + j, :RANK, :]
    mixed = tail[36].astype(f32)
    for which in range(3):
        scale[which : which + 1, :] = mixed[:1, which * TILE : which * TILE + RANK]
    other = early[24]
    scale[3:4, :] = other[3:4, 3 * TILE : 3 * TILE + RANK]
    feed_scale[...] = other[4:6, :RANK]
    for copy in outs:
        copy.wait()


def unpack(hidden, early, tail, tokens, layer):
    mats = jax.ShapeDtypeStruct((RANK, 4, WIDTH), f32)
    small = jax.ShapeDtypeStruct((RANK, WIDTH), f32)
    split = jax.ShapeDtypeStruct((RANK, hidden), f32)
    return pl.pallas_call(
        unpack_kernel,
        out_shape=(
            jax.ShapeDtypeStruct((ROWS, WIDTH), f32),
            jax.ShapeDtypeStruct((ROWS, WIDTH), bf16),
            mats,
            jax.ShapeDtypeStruct((4, RANK), f32),
            mats,
            small,
            split,
            split,
            jax.ShapeDtypeStruct((2, RANK), f32),
            small,
        ),
        in_specs=[vmem(), vmem(), anywhere(), anywhere()],
        out_specs=(anywhere(),) * 2 + (vmem(),) * 8,
        scratch_shapes=[
            pltpu.VMEM((ROWS, WIDTH), f32),
            pltpu.VMEM((ROWS, WIDTH), bf16),
            pltpu.SemaphoreType.DMA((4, 4)),
        ],
        name="unpack",
    )(early, tail, tokens, layer)


def body(
    tokens,
    segment,
    live,
    mix_weight,
    out_weight,
    position_table,
    norm_gain,
    norm_bias,
    mix_left,
    mix_scale,
    mix_right,
    expand_weight,
    expand_left,
    expand_right,
    shrink_weight,
    shrink_left,
    feed_scale,
    shrink_right,
    cotangent,
):
    tensor_size = lax.axis_size("tensor")
    near_size = tensor_size * 2
    far_size = lax.axis_size("dp") // 2
    hidden = expand_weight.shape[1]
    early_tiles = -(-(SPLIT_AT + 2 * tensor_size * hidden // LANES) // near_size) * near_size
    tail_tiles = -(-37 // near_size) * near_size
    left_t = jnp.transpose(mix_left, (2, 0, 1))
    right = jnp.transpose(mix_right, (1, 0, 2))
    grad_first, grad_context, early, layer_out, q, k, v, tq, tk, tr, *adapters, shares = front(
        tensor_size,
        early_tiles,
        segment.reshape(1, ROWS),
        live.reshape(1, ROWS),
        tokens,
        position_table,
        left_t,
        right,
        mix_scale,
        norm_gain,
        norm_bias,
        expand_left.T,
        shrink_right,
        feed_scale,
        mix_weight,
        cotangent,
        out_weight,
        expand_weight,
        shrink_weight,
        expand_right,
        shrink_left.T,
    )
    grad_tokens, early, tail = back(
        tail_tiles,
        near_size,
        far_size,
        *adapters,
        mix_scale,
        early,
        grad_context,
        q,
        k,
        v,
        tq,
        tk,
        tokens,
        tr,
        mix_weight,
        grad_first,
        shares,
    )
    (
        grad_tokens,
        layer_out,
        left,
        scale,
        right,
        expand_left,
        expand_right,
        shrink_left,
        feed_scale,
        shrink_right,
    ) = unpack(hidden, early, tail, grad_tokens, layer_out)
    return (
        layer_out,
        grad_tokens,
        jnp.transpose(left, (1, 2, 0)),
        scale,
        jnp.transpose(right, (1, 0, 2)),
        expand_left.T,
        expand_right,
        shrink_left.T,
        feed_scale,
        shrink_right,
    )


def solution(mesh):
    rows = P(("dp", "tensor"), None)
    line = P(("dp", "tensor"))
    return jax.shard_map(
        body,
        mesh=mesh,
        in_specs=(
            rows,
            line,
            line,
            P(),
            P(),
            P(),
            P(),
            P(),
            P(),
            P(),
            P(),
            P(None, "tensor"),
            P(),
            P(None, "tensor"),
            P("tensor", None),
            P("tensor", None),
            P(),
            P(),
            rows,
        ),
        out_specs=(
            rows,
            rows,
            P(),
            P(),
            P(),
            P(),
            P(None, "tensor"),
            P("tensor", None),
            P(),
            P(),
        ),
        check_vma=False,
    )
```

```python
import math

import jax
import jax.numpy as jnp
from jax import lax
from jax.experimental import pallas as pl
from jax.experimental.pallas import tpu as pltpu
from jax.sharding import PartitionSpec as P

PAIRS = 6
LANES = 128
ROWS = 512
WIDTH = 768
RANK = 12
BLOCKS = ROWS // LANES
TILE = 16
GROUP = 2
BACK_GROUP = 4
STACK = 64
SPLIT_AT = 25

norm_eps = 1e-07
masked_fill = -1e30
score_scale = 1.0 / math.sqrt(192.0)
inverse_root_two = 1.0 / math.sqrt(2.0)
log_two_e = math.log2(math.e)
inverse_root_tau = 1.0 / math.sqrt(2.0 * math.pi)

f32 = jnp.float32
bf16 = jnp.bfloat16


def dot_nn(left, right):
    return jnp.dot(left, right, preferred_element_type=f32)


def dot_nt(left, right):
    return lax.dot_general(left, right, (((1,), (1,)), ((), ())), preferred_element_type=f32)


def dot_tn(left, right):
    return lax.dot_general(left, right, (((0,), (0,)), ((), ())), preferred_element_type=f32)


def column_of(row):
    n = row.shape[1]
    eye = lax.broadcasted_iota(jnp.int32, (n, n), 0) == lax.broadcasted_iota(jnp.int32, (n, n), 1)
    return jnp.sum(jnp.where(eye, row, 0.0), axis=1, keepdims=True)


def spread(scale):
    row = lax.broadcasted_iota(jnp.int32, (RANK, STACK), 0)
    lane = lax.broadcasted_iota(jnp.int32, (RANK, STACK), 1)
    total = jnp.zeros((1, STACK), f32)
    for a in range(4):
        column = column_of(scale[a : a + 1, :])
        total = total + jnp.sum(
            jnp.where(lane == row + TILE * a, column, 0.0), axis=0, keepdims=True
        )
    return total


def of_map(which):
    lane = lax.broadcasted_iota(jnp.int32, (1, STACK), 1)
    return (lane // TILE == which).astype(bf16)


def block_iotas():
    shape = (LANES, LANES)
    return lax.broadcasted_iota(jnp.int32, shape, 0), lax.broadcasted_iota(jnp.int32, shape, 1)


def head_mask(which):
    lane = lax.broadcasted_iota(jnp.int32, (1, LANES), 1)
    return ((lane >= 64) if which else (lane < 64)).astype(bf16)


def pick_tiles(scores, block, at_diag):
    first = scores[:, :1]
    last = scores[:, ROWS - 1 :]
    near = {}

    def rolled(u):
        if u not in near:
            near[u] = pltpu.roll(
                scores[:, u * LANES : (u + 1) * LANES], 1, 1, stride=1, stride_axis=0
            )
        return near[u]

    tiles = []
    for other in range(BLOCKS):
        v = other - block + 2
        if v < 0:
            tile = jnp.broadcast_to(first, (LANES, LANES))
        elif v == 0:
            tile = jnp.where(at_diag, first, rolled(0))
        elif v < 4:
            tile = jnp.where(at_diag, rolled(v - 1), rolled(v))
        elif v == 4:
            tile = jnp.where(at_diag, rolled(3), last)
        else:
            tile = jnp.broadcast_to(last, (LANES, LANES))
        tiles.append(tile)
    return jnp.concatenate(tiles, axis=1)


def row_sums(values):
    part = (
        values[:, :LANES]
        + values[:, LANES : 2 * LANES]
        + values[:, 2 * LANES : 3 * LANES]
        + values[:, 3 * LANES :]
    )
    high = part.astype(bf16)
    rest = (part - high.astype(f32)).astype(bf16)
    return dot_nn(jnp.concatenate([high, rest], axis=1), jnp.ones((2 * LANES, LANES), bf16))


def wide4(values):
    return jnp.concatenate([values] * BLOCKS, axis=1)


def fold_rows(grads, block, beyond, inside, pick_first, pick_last):
    zero = jnp.zeros((LANES, LANES), f32)
    near = {}
    low = []
    high = []
    for other in range(BLOCKS):
        v = other - block + 2
        tile = grads[:, other * LANES : (other + 1) * LANES]
        if v < 0:
            low.append(tile.astype(bf16))
        elif v > 4:
            high.append(tile.astype(bf16))
        else:
            near[v] = pltpu.roll(tile, 0, 1, stride=1, stride_axis=0)
        if v == 0:
            low.append(tile.astype(bf16) * inside)
        if v == 4:
            high.append(tile.astype(bf16) * (1 - inside))
    out = []
    for w in range(BLOCKS):
        if w in near or w + 1 in near:
            out.append(jnp.where(beyond, near.get(w + 1, zero), near.get(w, zero)))
        else:
            out.append(zero)
    if low:
        out[0] = out[0] + dot_nn(
            jnp.concatenate(low, axis=1), pick_first[: LANES * len(low), :]
        )
    if high:
        out[3] = out[3] + dot_nn(
            jnp.concatenate(high, axis=1), pick_last[: LANES * len(high), :]
        )
    return jnp.concatenate(out, axis=1)


def attend_part(
    segment,
    live,
    tokens,
    table,
    mix_weight,
    mix_copies,
    left_s,
    right_s,
    scale_row,
    rank_s,
    table_rank_s,
    shares_out,
    q_s,
    k_s,
    v_s,
    tq_s,
    tk_s,
    tr_s,
    context_s,
    shares_s,
    bias_s,
    across_s,
    work,
    sems,
    gather,
):
    row, lane = block_iotas()
    below = lane <= row
    flip = (row + lane == LANES - 1).astype(bf16)
    eye = (row == lane).astype(bf16)
    seg_row = segment[...]
    key_row = jnp.where(live[...] == 1, seg_row, -1)
    for a in range(BLOCKS):
        seg_col = jnp.broadcast_to(
            seg_row[:, a * LANES : (a + 1) * LANES].astype(f32), (LANES, LANES)
        ).T.astype(jnp.int32)
        for b in range(BLOCKS):
            same = seg_col == key_row[:, b * LANES : (b + 1) * LANES]
            if a == b:
                same = same | (row == lane)
            bias_s[a * LANES : (a + 1) * LANES, b * LANES : (b + 1) * LANES] = jnp.where(
                same, 0.0, masked_fill
            )
    for a in range(BLOCKS):
        tr_s[a * LANES : (a + 1) * LANES, :] = dot_nn(
            flip, table[(3 - a) * LANES : (4 - a) * LANES, :]
        ).astype(bf16)

    rank_s[...] = dot_nt(tokens[...], left_s[...])
    table_rank_s[...] = dot_nt(tr_s[...], left_s[...])
    low = (rank_s[...] * scale_row).astype(bf16)
    table_low = (table_rank_s[...] * scale_row).astype(bf16)

    def project(source, low, which, target):
        full = dot_nn(source, mix_weight[which]) + dot_nn(low * of_map(which), right_s[...])
        for p in range(PAIRS):
            target[p] = full[:, p * LANES : (p + 1) * LANES].astype(bf16)

    mix_copies[0].wait()
    project(tokens[...], low, 0, q_s)
    project(tr_s[...], table_low, 0, tq_s)
    mix_copies[1].wait()
    project(tokens[...], low, 1, k_s)
    project(tr_s[...], table_low, 1, tk_s)
    gather.forward_one(0)
    mix_copies[2].wait()
    project(tokens[...], low, 2, v_s)

    blocks = [slice(b * LANES, (b + 1) * LANES) for b in range(BLOCKS)]
    keys_s, queries_s, along_s, both_s = work[:4]
    context_part = work[4]

    def scores(p, which):
        mask = head_mask(which)
        keys_s[which][:, :ROWS] = dot_nt(k_s[p] * mask, tq_s[p])
        queries_s[which][:, :ROWS] = dot_nt(q_s[p] * mask, tk_s[p])

    def pick(p, which):
        for b, r in enumerate(blocks):
            values = pick_tiles(keys_s[which][r, :ROWS], b, below)
            high = values.astype(bf16)
            across_s[which, 0, r, :] = high
            across_s[which, 1, r, :] = (values - high.astype(f32)).astype(bf16)
            along_s[which][r, :ROWS] = pick_tiles(queries_s[which][r, :ROWS], b, below)

    def content(p, which):
        mask = head_mask(which)
        for r in blocks:
            both_s[which][r, :ROWS] = dot_nt(
                jnp.concatenate([q_s[p, r, :] * mask, eye, eye], axis=1),
                jnp.concatenate(
                    [k_s[p], across_s[which, 0, :, r], across_s[which, 1, :, r]], axis=1
                ),
            )

    def softmax(p, which):
        for first in range(0, BLOCKS, GROUP):
            rows = blocks[first : first + GROUP]
            totals = [
                both_s[which][r, :ROWS] + along_s[which][r, :ROWS] + bias_s[r, :] for r in rows
            ]
            peaks = [jnp.max(t, axis=1, keepdims=True) for t in totals]
            weights = [
                jnp.exp2((t - m) * (score_scale * log_two_e)) for t, m in zip(totals, peaks)
            ]
            inverses = [1.0 / jnp.sum(w, axis=1, keepdims=True) for w in weights]
            for r, w, inverse in zip(rows, weights, inverses):
                shares_s[p, which, r, :] = (w * inverse).astype(bf16)

    def mix(p, which):
        part = dot_nn(shares_s[p, which], v_s[p] * head_mask(which))
        if which == 0:
            context_part[:, :LANES] = part
        else:
            lanes = slice(p * LANES, (p + 1) * LANES)
            if not isinstance(p, int):
                lanes = pl.ds(pl.multiple_of(p * LANES, LANES), LANES)
            context_s[:, lanes] = (context_part[:, :LANES] + part).astype(bf16)

    stages = (mix, softmax, content, pick, scores)

    def step(base, extra, first=0, last=4):
        for n in range(first, last + 1):
            head = extra - (4 - n)
            stages[n](base + head // 2, head % 2)

    def give(p):
        pltpu.make_async_copy(shares_s.at[p], shares_out.at[p], sems.at[p]).start()

    for extra in range(4):
        if extra == 2:
            gather.forward_one(1)
        step(0, extra, first=4 - extra)

    def pair(base, carry):
        for at, forward, k in (
            (2, gather.forward_one, 2),
            (3, gather.forward_two, 0),
            (4, gather.forward_one, 3),
            (5, gather.forward_two, 1),
        ):

            @pl.when(base == at)
            def _():
                forward(k)

        step(base, 0)
        step(base, 1)
        give(base - 2)
        return carry

    lax.fori_loop(2, PAIRS, pair, 0)
    gather.forward_one(4)
    step(PAIRS, 0, last=3)
    gather.forward_two(2)
    step(PAIRS, 1, last=2)
    give(PAIRS - 2)
    step(PAIRS, 2, last=1)
    gather.forward_two(3)
    give(PAIRS - 1)
    step(PAIRS, 3, last=0)


def vmem():
    return pl.BlockSpec(memory_space=pltpu.VMEM)


def anywhere():
    return pl.BlockSpec(memory_space=pl.ANY)


def remote(source, target, send, recv, device):
    return pltpu.make_async_remote_copy(
        src_ref=source,
        dst_ref=target,
        send_sem=send,
        recv_sem=recv,
        device_id=device,
        device_id_type=pl.DeviceIdType.MESH,
    )


def greet(devices):
    barrier = pltpu.get_barrier_semaphore()
    for device in devices:
        pl.semaphore_signal(
            barrier, inc=1, device_id=device, device_id_type=pl.DeviceIdType.MESH
        )
    pl.semaphore_wait(barrier, len(devices))


class Groups:
    def __init__(self, tensor_size, dp_size):
        self.near_size = tensor_size * 2
        self.far_size = dp_size // 2
        self.tensor = lax.axis_index("tensor")
        self.dp = lax.axis_index("dp")
        self.near = self.tensor * 2 + self.dp % 2
        self.far = self.dp // 2

    def near_index(self, step):
        return (self.near + step) % self.near_size

    def near_device(self, step):
        index = self.near_index(step)
        return {"dp": self.far * 2 + index % 2, "tensor": index // 2}

    def far_device(self, step):
        index = (self.far + step) % self.far_size
        return {"dp": index * 2 + self.dp % 2, "tensor": self.tensor}

    def partners(self):
        return [self.near_device(s) for s in range(1, self.near_size)] + [
            self.far_device(s) for s in range(1, self.far_size)
        ]


class Reduction:
    def __init__(self, groups, pack, arrived, crossed, out, sems):
        self.groups = groups
        self.pack = pack
        self.arrived = arrived
        self.crossed = crossed
        self.out = out
        self.send_one, self.recv_one, self.send_two, self.recv_two, self.send_three, self.recv_three = sems
        self.size = pack.shape[0] // groups.near_size

    def part(self, ref, index):
        return ref.at[pl.ds(index * self.size, self.size)]

    def scatter(self):
        g = self.groups
        return [
            remote(
                self.part(self.pack, g.near_index(s)),
                self.arrived.at[s - 1],
                self.send_one.at[s - 1],
                self.recv_one.at[s - 1],
                g.near_device(s),
            )
            for s in range(1, g.near_size)
        ]

    def cross(self):
        g = self.groups
        return [
            remote(
                self.crossed.at[g.far],
                self.crossed.at[g.far],
                self.send_two.at[s - 1],
                self.recv_two.at[s - 1],
                g.far_device(s),
            )
            for s in range(1, g.far_size)
        ]

    def gather(self):
        g = self.groups
        return [
            remote(
                self.part(self.out, g.near),
                self.part(self.out, g.near),
                self.send_three.at[s - 1],
                self.recv_three.at[s - 1],
                g.near_device(s),
            )
            for s in range(1, g.near_size)
        ]

    def start(self):
        for copy in self.scatter():
            copy.start()

    def middle(self):
        g = self.groups
        for copy in self.scatter():
            copy.wait()
        total = self.pack[pl.ds(g.near * self.size, self.size)].astype(f32)
        for s in range(1, g.near_size):
            total = total + self.arrived[s - 1].astype(f32)
        self.crossed[g.far] = total.astype(self.crossed.dtype)
        for copy in self.cross():
            copy.start()

    def last(self):
        g = self.groups
        for copy in self.cross():
            copy.wait()
        total = self.crossed[0].astype(f32)
        for s in range(1, g.far_size):
            total = total + self.crossed[s].astype(f32)
        self.out[pl.ds(g.near * self.size, self.size)] = total.astype(self.out.dtype)
        for copy in self.gather():
            copy.start()

    def finish(self):
        for copy in self.gather():
            copy.wait()


def reduction_scratch(tiles, near_size, far_size, kind):
    size = tiles // near_size
    near = (near_size - 1,)
    far = (max(far_size - 1, 1),)
    dma = pltpu.SemaphoreType.DMA
    return [
        pltpu.VMEM((near_size - 1, size, TILE, LANES), kind),
        pltpu.VMEM((far_size, size, TILE, LANES), kind),
        dma(near),
        dma(near),
        dma(far),
        dma(far),
        dma(near),
        dma(near),
    ]


class Gather:
    def __init__(self, size, sources, targets, sems):
        self.size = size
        self.far = size // 2
        self.sources = sources
        self.targets = targets
        self.across_s, self.across_r, self.pair_s, self.pair_r, self.one_s, self.one_r, self.two_s, self.two_r = sems[:8]
        self.whole_s, self.whole_r, self.small_s, self.small_r, self.own = sems[8:]
        self.tensor = lax.axis_index("tensor")
        self.dp = lax.axis_index("dp")
        self.bit = self.dp % 2
        self.pair = {"dp": self.dp + 1 - 2 * self.bit, "tensor": self.tensor}
        self.near = self.tensor + 1 - 2 * (self.tensor % 2)
        self.core = {"dp": self.dp, "tensor": self.near}

    def device(self, step):
        return {"dp": self.dp, "tensor": (self.tensor + step) % self.size}

    def partners(self):
        return [self.device(s) for s in range(1, self.size)] + [self.pair]

    def slot(self, order):
        first = self.tensor if isinstance(order, int) and order % 2 == 0 else None
        if first is None:
            first = self.tensor + (order % 2) * (self.near - self.tensor)
        return (first + self.size - 2 * (order // 2)) % self.size

    def rows(self, which, part, bit):
        count = self.sources[which].shape[0] // 6
        return pl.ds((2 * part + bit) * count, count)

    def across(self, s, k):
        which, part = k // 3, k % 3
        rows = self.rows(which, part, self.bit)
        return remote(
            self.sources[which].at[rows, :],
            self.targets[which].at[self.tensor, rows, :],
            self.across_s.at[s - 1, k],
            self.across_r.at[s - 1, k],
            self.device(2 * s),
        )

    def onward(self, s, k, bit, sends, recvs, device):
        which, part = k // 3, k % 3
        rows = self.rows(which, part, bit)
        ref = self.targets[which].at[self.slot(2 * s), rows, :]
        return remote(ref, ref, sends.at[s - 1, k], recvs.at[s - 1, k], device)

    def swap(self, s, k):
        return self.onward(s, k, self.bit, self.pair_s, self.pair_r, self.pair)

    def share_one(self, s, k):
        return self.onward(s, k, self.bit, self.one_s, self.one_r, self.core)

    def share_two(self, s, k):
        return self.onward(s, k, 1 - self.bit, self.two_s, self.two_r, self.core)

    def whole(self, which):
        return remote(
            self.sources[which],
            self.targets[which].at[self.tensor],
            self.whole_s.at[which],
            self.whole_r.at[which],
            self.core,
        )

    def small(self, s, which):
        return remote(
            self.sources[which],
            self.targets[which].at[self.tensor],
            self.small_s.at[s - 1, which - 2],
            self.small_r.at[s - 1, which - 2],
            self.device(s),
        )

    def keep(self, which):
        return pltpu.make_async_copy(
            self.sources[which], self.targets[which].at[self.tensor], self.own.at[which]
        )

    def start(self):
        for which in range(4):
            self.keep(which).start()
        greet(self.partners())
        for k in range(6):
            for s in range(1, self.far):
                self.across(s, k).start()
        for which in range(2):
            self.whole(which).start()
        for s in range(1, self.size):
            for which in (2, 3):
                self.small(s, which).start()

    def forward_one(self, k):
        for s in range(1, self.far):
            self.across(s, k).wait_recv()
            self.swap(s, k).start()
            self.share_one(s, k).start()

    def forward_two(self, k):
        for s in range(1, self.far):
            self.swap(s, k).wait_recv()
            self.share_two(s, k).start()

    def arrive(self, order):
        if order == 0:
            for which in range(4):
                self.keep(which).wait()
            for s in range(1, self.size):
                for which in (2, 3):
                    self.small(s, which).wait()
        elif order == 1:
            for which in range(2):
                self.whole(which).wait()
        elif order % 2 == 1:
            for k in range(6):
                self.share_one(order // 2, k).wait_recv()
                self.share_two(order // 2, k).wait_recv()

    def finish(self):
        for s in range(1, self.far):
            for k in range(6):
                self.across(s, k).wait_send()
                self.swap(s, k).wait_send()
                self.share_one(s, k).wait_send()
                self.share_two(s, k).wait_send()


def norm_parts(values):
    center = values - jnp.mean(values, axis=-1, keepdims=True)
    root = lax.rsqrt(jnp.mean(center * center, axis=-1, keepdims=True) + norm_eps)
    return center * root, root


def norm_back(scaled, unit, root):
    return root * (
        scaled
        - jnp.mean(scaled, axis=-1, keepdims=True)
        - unit * jnp.mean(scaled * unit, axis=-1, keepdims=True)
    )


def feed_part(
    tokens,
    cotangent,
    cotangent_copy,
    out_weight,
    out_copy,
    left_s,
    right_s,
    scale_row,
    gain,
    shift,
    expand_left_t,
    expand_right,
    shrink_left_t,
    shrink_right,
    feed_scale,
    layer_out,
    layer_copy,
    grad_first_out,
    grad_context_out,
    pack,
    expand_s,
    shrink_s,
    x_s,
    normed_s,
    hidden_s,
    act_s,
    slope_s,
    branch_s,
    context_s,
    one_s,
    two_s,
    pre_s,
    gather,
):
    chunks = expand_s.shape[0]
    pieces = expand_s.shape[2] // LANES
    hidden = expand_s.shape[2]

    def part_of(order):
        if hidden == WIDTH:
            return order, slice(None), slice(None)
        place = order * hidden % WIDTH
        if isinstance(order, int):
            return order * hidden // WIDTH, slice(None), slice(place, place + hidden)
        place = pl.multiple_of(place, LANES)
        return order * hidden // WIDTH, slice(None), pl.ds(place, hidden)

    pack[...] = jnp.zeros_like(pack)

    def keep(first, values):
        for j in range(values.shape[1] // LANES):
            pack[first + j, :RANK, :] = values[:, j * LANES : (j + 1) * LANES]

    lam_one = feed_scale[0:1, :]
    lam_two = feed_scale[1:2, :]
    step = LANES
    steps = ROWS // step

    out_copy.wait()
    gather.forward_one(5)
    out_rank = dot_nt(context_s[...], left_s[...])
    out_low = (out_rank * scale_row).astype(bf16) * of_map(3)
    x_s[...] = dot_nn(context_s[...], out_weight[...]) + dot_nn(out_low, right_s[...])

    def first_norm(i, carry):
        rows = pl.ds(i * step, step)
        values = tokens[rows, :].astype(f32) + x_s[rows, :]
        x_s[rows, :] = values
        unit, root = norm_parts(values)
        normed = unit * gain[0:1, :] + shift[0:1, :]
        normed_s[rows, :] = normed
        hidden_s[rows, :] = normed.astype(bf16)
        return carry

    lax.fori_loop(0, steps, first_norm, 0)
    gather.forward_two(4)

    one_rank = dot_nt(hidden_s[...], expand_left_t[...])
    one_low = (one_rank * lam_one).astype(bf16)
    def expanded(order):
        if order == min(2, chunks - 1):
            gather.forward_two(5)
        gather.arrive(order)
        c = gather.slot(order)
        pre_s[order % 2, :, :hidden] = dot_nn(hidden_s[...], expand_s[c]) + dot_nn(one_low, expand_right[c])

    two_rank = None
    expanded(0)
    for order in range(chunks):
        if order + 1 < chunks:
            expanded(order + 1)
        pre = pre_s[order % 2, :, :hidden]
        cdf = 0.5 + 0.5 * lax.erf(pre * inverse_root_two)
        act_s[part_of(order)] = (pre * cdf).astype(bf16)
        slope_s[part_of(order)] = cdf + pre * jnp.exp(-0.5 * pre * pre) * inverse_root_tau
        c = gather.slot(order)
        part = dot_nn(act_s[part_of(order)], shrink_s[c])
        branch_s[...] = part if order == 0 else branch_s[...] + part
        part = dot_nt(act_s[part_of(order)], shrink_left_t[c])
        two_s[...] = part if order == 0 else two_s[...] + part
    two_rank = two_s[...]
    gather.finish()
    two_low = (two_rank * lam_two).astype(bf16)
    branch_s[...] += dot_nn(two_low, shrink_right[...])

    cotangent_copy.wait()

    def second_norm(i, carry):
        rows = pl.ds(i * step, step)
        unit, root = norm_parts(normed_s[rows, :] + branch_s[rows, :])
        layer_out[rows, :] = (unit * gain[1:2, :] + shift[1:2, :]).astype(bf16)
        grad = norm_back(cotangent[rows, :].astype(f32) * gain[1:2, :], unit, root)
        branch_s[rows, :] = grad
        return carry

    lax.fori_loop(0, steps, second_norm, 0)
    layer_copy.start()
    grad_branch = branch_s[...].astype(bf16)
    two_back = dot_nt(grad_branch, shrink_right[...])
    two_small = (two_back * lam_two).astype(bf16)
    two_small_t = two_small.T
    one_low_t = one_low.T
    keep(18, dot_tn(two_low, grad_branch))
    pack[24, 5:6, :RANK] = jnp.sum(two_rank * two_back, axis=0, keepdims=True)

    one_s[...] = jnp.zeros_like(one_s)

    def backward(order, carry):
        c = gather.slot(order)
        here = part_of(order)
        grad_act = dot_nt(grad_branch, shrink_s[c]) + dot_nn(two_small, shrink_left_t[c])
        grad_pre = (grad_act * slope_s[here]).astype(bf16)
        keep(SPLIT_AT + (chunks + c) * pieces, dot_nn(two_small_t, act_s[here]))
        keep(SPLIT_AT + c * pieces, dot_nn(one_low_t, grad_pre))
        branch_s[...] += dot_nt(grad_pre, expand_s[c])
        one_s[...] += dot_nt(grad_pre, expand_right[c])
        return carry

    lax.fori_loop(0, chunks, backward, 0)
    one_back = one_s[...]
    one_small = (one_back * lam_one).astype(bf16)
    branch_s[...] += dot_nn(one_small, expand_left_t[...])
    keep(12, dot_tn(one_small, hidden_s[...]))
    pack[24, 4:5, :RANK] = jnp.sum(one_rank * one_back, axis=0, keepdims=True)

    def first_back(i, carry):
        rows = pl.ds(i * step, step)
        unit, root = norm_parts(x_s[rows, :])
        grad_first_out[rows, :] = norm_back(branch_s[rows, :] * gain[0:1, :], unit, root)
        return carry

    lax.fori_loop(0, steps, first_back, 0)
    grad_attended = grad_first_out[...].astype(bf16)
    out_back = dot_nt(grad_attended, right_s[...])
    out_small = (out_back * scale_row).astype(bf16) * of_map(3)
    grad_context = dot_nt(grad_attended, out_weight[...]) + dot_nn(out_small, left_s[...])
    for p in range(PAIRS):
        grad_context_out[p] = grad_context[:, p * LANES : (p + 1) * LANES].astype(bf16)
    keep(0, dot_tn(out_small, context_s[...])[3 * TILE : 3 * TILE + RANK, :])
    keep(6, dot_tn(out_low, grad_attended)[3 * TILE : 3 * TILE + RANK, :])
    pack[24, 3:4, :STACK] = jnp.sum(out_rank * out_back, axis=0, keepdims=True)


def front_kernel(
    segment,
    live,
    tokens,
    table,
    left_t,
    right,
    scale,
    gain,
    shift,
    expand_left_t,
    shrink_right,
    feed_scale,
    mix_weight,
    cotangent,
    out_weight,
    expand,
    shrink,
    expand_right,
    shrink_left_t,
    grad_first,
    grad_context,
    pack,
    layer_to,
    q_to,
    k_to,
    v_to,
    tq_to,
    tk_to,
    tr_to,
    left_to,
    right_to,
    rank_to,
    table_rank_to,
    shares_out,
    layer_s,
    q_s,
    k_s,
    v_s,
    tq_s,
    tk_s,
    tr_s,
    left_s,
    right_s,
    rank_s,
    table_rank_s,
    mix_s,
    cotangent_s,
    out_s,
    expand_s,
    shrink_s,
    expand_right_s,
    shrink_left_s,
    shares_s,
    bias_s,
    across_s,
    x_s,
    normed_s,
    hidden_s,
    act_s,
    slope_s,
    branch_s,
    context_s,
    one_s,
    two_s,
    pre_s,
    share_sems,
    load_sems,
    keep_sems,
    *gather_sems,
):
    mix_copies = [
        pltpu.make_async_copy(mix_weight.at[i], mix_s.at[i], load_sems.at[i]) for i in range(3)
    ]
    cotangent_copy = pltpu.make_async_copy(cotangent, cotangent_s, load_sems.at[3])
    out_copy = pltpu.make_async_copy(out_weight, out_s, load_sems.at[4])
    for copy in mix_copies:
        copy.start()
    gather = Gather(
        expand_s.shape[0],
        (expand, shrink, expand_right, shrink_left_t),
        (expand_s, shrink_s, expand_right_s, shrink_left_s),
        gather_sems,
    )
    gather.start()
    cotangent_copy.start()
    out_copy.start()
    left_s[...] = jnp.zeros_like(left_s)
    right_s[...] = jnp.zeros_like(right_s)
    for a in range(4):
        left_s[a * TILE : a * TILE + RANK, :] = left_t[:, a, :]
        right_s[a * TILE : a * TILE + RANK, :] = right[:, a, :]
    scale_row = spread(scale)
    attend_part(
        segment,
        live,
        tokens,
        table,
        mix_s,
        mix_copies,
        left_s,
        right_s,
        scale_row,
        rank_s,
        table_rank_s,
        shares_out,
        q_s,
        k_s,
        v_s,
        tq_s,
        tk_s,
        tr_s,
        context_s,
        shares_s,
        bias_s,
        across_s,
        (
            (slope_s.at[0], slope_s.at[1]),
            (slope_s.at[2], slope_s.at[3]),
            (pre_s.at[0], pre_s.at[1]),
            (x_s, normed_s),
            branch_s,
        ),
        share_sems,
        gather,
    )
    kept = [
        pltpu.make_async_copy(source, target, keep_sems.at[i])
        for i, (source, target) in enumerate(
            (
                (layer_s, layer_to),
                (q_s, q_to),
                (k_s, k_to),
                (v_s, v_to),
                (tq_s, tq_to),
                (tk_s, tk_to),
                (tr_s, tr_to),
                (left_s, left_to),
                (right_s, right_to),
                (rank_s, rank_to),
                (table_rank_s, table_rank_to),
            )
        )
    ]
    for copy in kept[1:]:
        copy.start()
    feed_part(
        tokens,
        cotangent_s,
        cotangent_copy,
        out_s,
        out_copy,
        left_s,
        right_s,
        scale_row,
        gain,
        shift,
        expand_left_t,
        expand_right_s,
        shrink_left_s,
        shrink_right,
        feed_scale,
        layer_s,
        kept[0],
        grad_first,
        grad_context,
        pack,
        expand_s,
        shrink_s,
        x_s,
        normed_s,
        hidden_s,
        act_s,
        slope_s,
        branch_s,
        context_s,
        one_s,
        two_s,
        pre_s,
        gather,
    )

    def finish(p, carry):
        pltpu.make_async_copy(shares_s.at[p], shares_out.at[p], share_sems.at[p]).wait()
        return carry

    lax.fori_loop(0, PAIRS, finish, 0)
    for copy in kept:
        copy.wait()


def front(size, tiles, *args):
    hidden = args[15].shape[1]
    wide = size * hidden // WIDTH
    piece = jax.ShapeDtypeStruct((PAIRS, ROWS, LANES), bf16)
    rows = jax.ShapeDtypeStruct((ROWS, WIDTH), bf16)
    dma = pltpu.SemaphoreType.DMA
    steps = (max(size // 2 - 1, 1), 6)
    stack = jax.ShapeDtypeStruct((STACK, WIDTH), bf16)
    rank = jax.ShapeDtypeStruct((ROWS, STACK), f32)
    kept = (rows, piece, piece, piece, piece, piece, rows, stack, stack, rank, rank)
    return pl.pallas_call(
        front_kernel,
        out_shape=(
            jax.ShapeDtypeStruct((ROWS, WIDTH), f32),
            piece,
            jax.ShapeDtypeStruct((tiles, TILE, LANES), f32),
        )
        + kept
        + (jax.ShapeDtypeStruct((PAIRS, 2, ROWS, ROWS), bf16),),
        in_specs=[vmem()] * 12 + [anywhere()] * 7,
        out_specs=(vmem(),) * 3 + (anywhere(),) * 12,
        scratch_shapes=[pltpu.VMEM(array.shape, array.dtype) for array in kept]
        + [
            pltpu.VMEM((3, WIDTH, WIDTH), bf16),
            pltpu.VMEM((ROWS, WIDTH), bf16),
            pltpu.VMEM((WIDTH, WIDTH), bf16),
            pltpu.VMEM((size, WIDTH, hidden), bf16),
            pltpu.VMEM((size, hidden, WIDTH), bf16),
            pltpu.VMEM((size, RANK, hidden), bf16),
            pltpu.VMEM((size, RANK, hidden), bf16),
            pltpu.VMEM((PAIRS, 2, ROWS, ROWS), bf16),
            pltpu.VMEM((ROWS, ROWS), f32),
            pltpu.VMEM((2, 2, ROWS, ROWS), bf16),
            pltpu.VMEM((ROWS, WIDTH), f32),
            pltpu.VMEM((ROWS, WIDTH), f32),
            pltpu.VMEM((ROWS, WIDTH), bf16),
            pltpu.VMEM((wide, ROWS, WIDTH), bf16),
            pltpu.VMEM((wide, ROWS, WIDTH), f32),
            pltpu.VMEM((ROWS, WIDTH), f32),
            pltpu.VMEM((ROWS, WIDTH), bf16),
            pltpu.VMEM((ROWS, RANK), f32),
            pltpu.VMEM((ROWS, RANK), f32),
            pltpu.VMEM((2, ROWS, WIDTH), f32),
            dma((PAIRS,)),
            dma((5,)),
            dma((len(kept),)),
        ]
        + [dma(steps)] * 8
        + [dma((2,))] * 2
        + [dma((size - 1, 2))] * 2
        + [dma((4,))],
        compiler_params=pltpu.CompilerParams(
            vmem_limit_bytes=60 * 2**20, collective_id=0, has_side_effects=True
        ),
        name="front",
    )(*args)


def back_kernel(
    left_s,
    right_s,
    rank_s,
    table_rank_s,
    scale,
    early,
    grad_context_in,
    q_in,
    k_in,
    v_in,
    tq_in,
    tk_in,
    tokens_in,
    tr_in,
    mix_in,
    grad_first_in,
    shares_in,
    grad_tokens,
    early_out,
    tail_out,
    grad_context,
    q_s,
    k_s,
    v_s,
    tq_s,
    tk_s,
    tokens,
    tr_s,
    mix_weight,
    grad_first,
    shares_s,
    gl_s,
    qf_s,
    kf_s,
    gq_s,
    gk_s,
    gt_s,
    grads_s,
    tables_s,
    tail,
    sems,
    load_sems,
    *reduce_refs,
):
    arrived, crossed = reduce_refs[0], reduce_refs[1]
    groups = Groups(arrived.shape[0] // 2 + 1, crossed.shape[0] * 2)
    first = Reduction(groups, early, arrived, crossed, early_out, reduce_refs[2:8])
    second = Reduction(groups, tail, reduce_refs[8], reduce_refs[9], tail_out, reduce_refs[10:16])
    row, lane = block_iotas()
    beyond = lane >= row
    inside = (row + lane <= LANES - 1).astype(bf16)
    ends = lax.broadcasted_iota(jnp.int32, (2 * LANES, LANES), 1)
    pick_first = (ends == 0).astype(bf16)
    pick_last = (ends == LANES - 1).astype(bf16)
    flip = (row + lane == LANES - 1).astype(bf16)

    needed = [
        pltpu.make_async_copy(source, target, load_sems.at[4 + i])
        for i, (source, target) in enumerate(
            (
                (grad_context_in, grad_context),
                (v_in, v_s),
                (q_in, q_s),
                (k_in, k_s),
                (tq_in, tq_s),
                (tk_in, tk_s),
            )
        )
    ]
    for copy in needed:
        copy.start()

    def begin(p, carry):
        pltpu.make_async_copy(shares_in.at[p], shares_s.at[p], sems.at[p]).start()
        return carry

    lax.fori_loop(0, PAIRS, begin, 0)
    loads = [
        pltpu.make_async_copy(source, target, load_sems.at[i])
        for i, (source, target) in enumerate(
            (
                (tokens_in, tokens),
                (tr_in, tr_s),
                (mix_in, mix_weight),
                (grad_first_in, grad_first),
            )
        )
    ]
    greet(groups.partners())
    first.start()
    for copy in loads:
        copy.start()
    for copy in needed:
        copy.wait()
    tail[...] = jnp.zeros_like(tail)
    scale_row = spread(scale)
    low = (rank_s[...] * scale_row).astype(bf16)
    table_low = (table_rank_s[...] * scale_row).astype(bf16)

    def keep(index, values):
        for j in range(values.shape[1] // LANES):
            tail[index + j] = values[:, j * LANES : (j + 1) * LANES].astype(bf16)

    def flipped(values):
        return jnp.concatenate(
            [
                dot_nn(flip, values[b * LANES : (b + 1) * LANES, :]).astype(bf16)
                for b in range(BLOCKS)
            ],
            axis=0,
        )

    def rows_of(group):
        return [
            slice(a * LANES, (a + 1) * LANES)
            for a in range(group * BACK_GROUP, (group + 1) * BACK_GROUP)
        ]

    def grads(p, which, group):
        rows = rows_of(group)
        every = slice(rows[0].start, rows[-1].stop)
        grad = dot_nt(grad_context[p, every, :] * head_mask(which), v_s[p])
        shares = [shares_s[p, which, r, :].astype(f32) for r in rows]
        prods = [
            grad[i * LANES : (i + 1) * LANES, :] * shares[i] for i in range(BACK_GROUP)
        ]
        inner = [jnp.sum(prod, axis=1, keepdims=True) for prod in prods]
        for i, r in enumerate(rows):
            gl_s[which, r, :] = (prods[i] - shares[i] * inner[i]).astype(bf16)

    def fold(which, group, target, turn):
        rows = rows_of(group)
        turned = [
            dot_nt(flip, gl_s[which, :, r]) if turn else dot_nn(flip, gl_s[which, r, :])
            for r in rows
        ]
        for t, r in zip(turned, rows):
            target[which, r, :ROWS] = t.astype(bf16)
        for i, r in enumerate(rows):
            target[which, r, ROWS:] = fold_rows(
                turned[i], group * BACK_GROUP + i, beyond, inside, pick_first, pick_last
            ).astype(bf16)

    def close(p, which, parts):
        gc_t, k_t, q_t, tk_t, tq_t, q_rev_t, k_rev_t = parts
        half = slice(which * 64, which * 64 + 64)
        gq_t = dot_nt(jnp.concatenate([k_t[half, :], tk_t[half, :]], axis=1), qf_s[which])
        gk_t = dot_nt(jnp.concatenate([q_t[half, :], tq_t[half, :]], axis=1), kf_s[which])
        gq_s[half, :] = (gq_t * score_scale).astype(bf16)
        gk_s[half, :] = (gk_t * score_scale).astype(bf16)
        gtk = dot_nn(q_rev_t[half, :], qf_s[which, :, ROWS:])
        gtq = dot_nn(k_rev_t[half, :], kf_s[which, :, ROWS:])
        gt_s[0, half, :] = (gtq * score_scale).astype(bf16)
        gt_s[1, half, :] = (gtk * score_scale).astype(bf16)
        gt_s[2, half, :] = dot_nn(gc_t[half, :], shares_s[p, which]).astype(bf16)

    sections = BLOCKS // BACK_GROUP
    pltpu.make_async_copy(shares_in.at[0], shares_s.at[0], sems.at[0]).wait()
    for group in range(sections):
        grads(0, 0, group)

    def pair(p, carry):
        later = jnp.minimum(p + 1, PAIRS - 1)

        @pl.when(p < PAIRS - 1)
        def _():
            pltpu.make_async_copy(
                shares_in.at[later], shares_s.at[later], sems.at[later]
            ).wait()

        @pl.when(p == 2)
        def _():
            first.middle()

        @pl.when(p == 4)
        def _():
            first.last()

        parts = (
            grad_context[p].T,
            k_s[p].T,
            q_s[p].T,
            tk_s[p].T,
            tq_s[p].T,
            flipped(q_s[p]).T,
            flipped(k_s[p]).T,
        )
        for group in range(sections):
            fold(0, group, qf_s, False)
            grads(p, 1, group)
            fold(0, group, kf_s, True)
        close(p, 0, parts)
        for group in range(sections):
            fold(1, group, qf_s, False)
            grads(later, 0, group)
            fold(1, group, kf_s, True)
        close(p, 1, parts)
        lanes = pl.ds(pl.multiple_of(p * LANES, LANES), LANES)
        for b in range(BLOCKS):
            rows = slice(b * LANES, (b + 1) * LANES)
            grads_s[0, rows, lanes] = dot_nt(flip, gq_s[:, rows]).astype(bf16)
            grads_s[1, rows, lanes] = dot_nt(flip, gk_s[:, rows]).astype(bf16)
        grads_s[2, :, lanes] = gt_s[2].T
        tables_s[0, :, lanes] = gt_s[0].T
        tables_s[1, :, lanes] = gt_s[1].T
        return carry

    lax.fori_loop(0, PAIRS, pair, 0)

    for copy in loads:
        copy.wait()

    def backs(source, count):
        total = None
        lane = lax.broadcasted_iota(jnp.int32, (1, STACK), 1)
        for which in range(count):
            part = dot_nt(source[which], right_s[...])
            part = jnp.where(lane // TILE == which, part, 0.0)
            total = part if total is None else total + part
        return total

    back = backs(grads_s, 3)
    table_back = backs(tables_s, 2)
    small = (back * scale_row).astype(bf16)
    table_small = (table_back * scale_row).astype(bf16)
    left_sum = dot_tn(small, tokens[...]) + dot_tn(table_small, tr_s[...])
    low_t = low.T
    table_low_t = table_low.T
    for which in range(3):
        rows = slice(which * TILE, (which + 1) * TILE)
        right_sum = dot_nn(low_t[rows, :], grads_s[which])
        if which < 2:
            right_sum = right_sum + dot_nn(table_low_t[rows, :], tables_s[which])
        keep(which * 6, left_sum[rows, :])
        keep(18 + which * 6, right_sum)
    tail[36, :1, :STACK] = jnp.sum(
        rank_s[...] * back + table_rank_s[...] * table_back, axis=0, keepdims=True
    ).astype(bf16)
    first.finish()
    second.start()
    grad_tokens[...] = grad_first[...] + dot_nn(small, left_s[...])
    grad_tokens[...] += dot_nt(grads_s[0], mix_weight[0])
    second.middle()
    grad_tokens[...] += dot_nt(grads_s[1], mix_weight[1])
    second.last()
    grad_tokens[...] += dot_nt(grads_s[2], mix_weight[2])
    second.finish()


def back(tail_tiles, near_size, far_size, *args):
    early = args[5]
    piece = pltpu.VMEM((PAIRS, ROWS, LANES), bf16)
    return pl.pallas_call(
        back_kernel,
        out_shape=(
            jax.ShapeDtypeStruct((ROWS, WIDTH), f32),
            jax.ShapeDtypeStruct(early.shape, f32),
            jax.ShapeDtypeStruct((tail_tiles, TILE, LANES), bf16),
        ),
        in_specs=[vmem()] * 6 + [anywhere()] * 11,
        out_specs=(vmem(),) * 3,
        scratch_shapes=[piece] * 6
        + [
            pltpu.VMEM((ROWS, WIDTH), bf16),
            pltpu.VMEM((ROWS, WIDTH), bf16),
            pltpu.VMEM((3, WIDTH, WIDTH), bf16),
            pltpu.VMEM((ROWS, WIDTH), f32),
            pltpu.VMEM((PAIRS, 2, ROWS, ROWS), bf16),
            pltpu.VMEM((2, ROWS, ROWS), bf16),
            pltpu.VMEM((2, ROWS, 2 * ROWS), bf16),
            pltpu.VMEM((2, ROWS, 2 * ROWS), bf16),
            pltpu.VMEM((LANES, ROWS), bf16),
            pltpu.VMEM((LANES, ROWS), bf16),
            pltpu.VMEM((3, LANES, ROWS), bf16),
            pltpu.VMEM((3, ROWS, WIDTH), bf16),
            pltpu.VMEM((2, ROWS, WIDTH), bf16),
            pltpu.VMEM((tail_tiles, TILE, LANES), bf16),
            pltpu.SemaphoreType.DMA((PAIRS,)),
            pltpu.SemaphoreType.DMA((10,)),
        ]
        + reduction_scratch(early.shape[0], near_size, far_size, f32)
        + reduction_scratch(tail_tiles, near_size, far_size, bf16),
        compiler_params=pltpu.CompilerParams(
            vmem_limit_bytes=58 * 2**20, collective_id=1, has_side_effects=True
        ),
        name="back",
    )(*args)


def unpack_kernel(
    early,
    tail,
    tokens_in,
    layer_in,
    tokens_out,
    layer_out,
    left,
    scale,
    right,
    expand_left_t,
    expand_right,
    shrink_left_t,
    feed_scale,
    shrink_right,
    tokens_s,
    layer_s,
    sems,
):
    ins = []
    outs = []
    for i in range(4):
        rows = pl.ds(i * LANES, LANES)
        for n, (source, held, target) in enumerate(
            ((tokens_in, tokens_s, tokens_out), (layer_in, layer_s, layer_out))
        ):
            ins.append(
                pltpu.make_async_copy(source.at[rows, :], held.at[rows, :], sems.at[n, i])
            )
            outs.append(
                pltpu.make_async_copy(held.at[rows, :], target.at[rows, :], sems.at[2 + n, i])
            )
    for copy in ins:
        copy.start()
    for copy, onward in zip(ins, outs):
        copy.wait()
        onward.start()
    me = lax.axis_index("tensor")
    pieces = expand_right.shape[1] // LANES
    split = SPLIT_AT + me * pieces
    skip = (early.shape[0] - SPLIT_AT) // 2
    for j in range(WIDTH // LANES):
        lanes = slice(j * LANES, (j + 1) * LANES)
        for which in range(3):
            left[:, which, lanes] = tail[which * 6 + j, :RANK, :].astype(f32)
            right[:, which, lanes] = tail[18 + which * 6 + j, :RANK, :].astype(f32)
        left[:, 3, lanes] = early[j, :RANK, :]
        right[:, 3, lanes] = early[6 + j, :RANK, :]
        expand_left_t[:, lanes] = early[12 + j, :RANK, :]
        shrink_right[:, lanes] = early[18 + j, :RANK, :]
    total = lax.axis_size("tensor") * pieces
    for j in range(pieces):
        lanes = slice(j * LANES, (j + 1) * LANES)
        expand_right[:, lanes] = early[split + j, :RANK, :]
        shrink_left_t[:, lanes] = early[split + total + j, :RANK, :]
    mixed = tail[36].astype(f32)
    for which in range(3):
        scale[which : which + 1, :] = mixed[:1, which * TILE : which * TILE + RANK]
    other = early[24]
    scale[3:4, :] = other[3:4, 3 * TILE : 3 * TILE + RANK]
    feed_scale[...] = other[4:6, :RANK]
    for copy in outs:
        copy.wait()


def unpack(hidden, early, tail, tokens, layer):
    mats = jax.ShapeDtypeStruct((RANK, 4, WIDTH), f32)
    small = jax.ShapeDtypeStruct((RANK, WIDTH), f32)
    split = jax.ShapeDtypeStruct((RANK, hidden), f32)
    return pl.pallas_call(
        unpack_kernel,
        out_shape=(
            jax.ShapeDtypeStruct((ROWS, WIDTH), f32),
            jax.ShapeDtypeStruct((ROWS, WIDTH), bf16),
            mats,
            jax.ShapeDtypeStruct((4, RANK), f32),
            mats,
            small,
            split,
            split,
            jax.ShapeDtypeStruct((2, RANK), f32),
            small,
        ),
        in_specs=[vmem(), vmem(), anywhere(), anywhere()],
        out_specs=(anywhere(),) * 2 + (vmem(),) * 8,
        scratch_shapes=[
            pltpu.VMEM((ROWS, WIDTH), f32),
            pltpu.VMEM((ROWS, WIDTH), bf16),
            pltpu.SemaphoreType.DMA((4, 4)),
        ],
        name="unpack",
    )(early, tail, tokens, layer)


def body(
    tokens,
    segment,
    live,
    mix_weight,
    out_weight,
    position_table,
    norm_gain,
    norm_bias,
    mix_left,
    mix_scale,
    mix_right,
    expand_weight,
    expand_left,
    expand_right,
    shrink_weight,
    shrink_left,
    feed_scale,
    shrink_right,
    cotangent,
):
    tensor_size = lax.axis_size("tensor")
    near_size = tensor_size * 2
    far_size = lax.axis_size("dp") // 2
    hidden = expand_weight.shape[1]
    early_tiles = -(-(SPLIT_AT + 2 * tensor_size * hidden // LANES) // near_size) * near_size
    tail_tiles = -(-37 // near_size) * near_size
    left_t = jnp.transpose(mix_left, (2, 0, 1))
    right = jnp.transpose(mix_right, (1, 0, 2))
    grad_first, grad_context, early, layer_out, q, k, v, tq, tk, tr, *adapters, shares = front(
        tensor_size,
        early_tiles,
        segment.reshape(1, ROWS),
        live.reshape(1, ROWS),
        tokens,
        position_table,
        left_t,
        right,
        mix_scale,
        norm_gain,
        norm_bias,
        expand_left.T,
        shrink_right,
        feed_scale,
        mix_weight,
        cotangent,
        out_weight,
        expand_weight,
        shrink_weight,
        expand_right,
        shrink_left.T,
    )
    grad_tokens, early, tail = back(
        tail_tiles,
        near_size,
        far_size,
        *adapters,
        mix_scale,
        early,
        grad_context,
        q,
        k,
        v,
        tq,
        tk,
        tokens,
        tr,
        mix_weight,
        grad_first,
        shares,
    )
    (
        grad_tokens,
        layer_out,
        left,
        scale,
        right,
        expand_left,
        expand_right,
        shrink_left,
        feed_scale,
        shrink_right,
    ) = unpack(hidden, early, tail, grad_tokens, layer_out)
    return (
        layer_out,
        grad_tokens,
        jnp.transpose(left, (1, 2, 0)),
        scale,
        jnp.transpose(right, (1, 0, 2)),
        expand_left.T,
        expand_right,
        shrink_left.T,
        feed_scale,
        shrink_right,
    )


def solution(mesh):
    rows = P(("dp", "tensor"), None)
    line = P(("dp", "tensor"))
    return jax.shard_map(
        body,
        mesh=mesh,
        in_specs=(
            rows,
            line,
            line,
            P(),
            P(),
            P(),
            P(),
            P(),
            P(),
            P(),
            P(),
            P(None, "tensor"),
            P(),
            P(None, "tensor"),
            P("tensor", None),
            P("tensor", None),
            P(),
            P(),
            rows,
        ),
        out_specs=(
            rows,
            rows,
            P(),
            P(),
            P(),
            P(),
            P(None, "tensor"),
            P("tensor", None),
            P(),
            P(),
        ),
        check_vma=False,
    )
```

```python
import math

import jax
import jax.numpy as jnp
from jax import lax
from jax.experimental import pallas as pl
from jax.experimental.pallas import tpu as pltpu
from jax.sharding import PartitionSpec as P

PAIRS = 6
LANES = 128
ROWS = 512
WIDTH = 768
RANK = 12
BLOCKS = ROWS // LANES
TILE = 16
GROUP = 2
BACK_GROUP = 4
STACK = 64
SPLIT_AT = 25

norm_eps = 1e-07
masked_fill = -1e30
score_scale = 1.0 / math.sqrt(192.0)
inverse_root_two = 1.0 / math.sqrt(2.0)
log_two_e = math.log2(math.e)
inverse_root_tau = 1.0 / math.sqrt(2.0 * math.pi)

f32 = jnp.float32
bf16 = jnp.bfloat16


def dot_nn(left, right):
    return jnp.dot(left, right, preferred_element_type=f32)


def dot_nt(left, right):
    return lax.dot_general(left, right, (((1,), (1,)), ((), ())), preferred_element_type=f32)


def dot_tn(left, right):
    return lax.dot_general(left, right, (((0,), (0,)), ((), ())), preferred_element_type=f32)


def column_of(row):
    n = row.shape[1]
    eye = lax.broadcasted_iota(jnp.int32, (n, n), 0) == lax.broadcasted_iota(jnp.int32, (n, n), 1)
    return jnp.sum(jnp.where(eye, row, 0.0), axis=1, keepdims=True)


def spread(scale):
    row = lax.broadcasted_iota(jnp.int32, (RANK, STACK), 0)
    lane = lax.broadcasted_iota(jnp.int32, (RANK, STACK), 1)
    total = jnp.zeros((1, STACK), f32)
    for a in range(4):
        column = column_of(scale[a : a + 1, :])
        total = total + jnp.sum(
            jnp.where(lane == row + TILE * a, column, 0.0), axis=0, keepdims=True
        )
    return total


def of_map(which):
    lane = lax.broadcasted_iota(jnp.int32, (1, STACK), 1)
    return (lane // TILE == which).astype(bf16)


def block_iotas():
    shape = (LANES, LANES)
    return lax.broadcasted_iota(jnp.int32, shape, 0), lax.broadcasted_iota(jnp.int32, shape, 1)


def head_mask(which):
    lane = lax.broadcasted_iota(jnp.int32, (1, LANES), 1)
    return ((lane >= 64) if which else (lane < 64)).astype(bf16)


def pick_tiles(scores, block, at_diag):
    first = scores[:, :1]
    last = scores[:, ROWS - 1 :]
    near = {}

    def rolled(u):
        if u not in near:
            near[u] = pltpu.roll(
                scores[:, u * LANES : (u + 1) * LANES], 1, 1, stride=1, stride_axis=0
            )
        return near[u]

    tiles = []
    for other in range(BLOCKS):
        v = other - block + 2
        if v < 0:
            tile = jnp.broadcast_to(first, (LANES, LANES))
        elif v == 0:
            tile = jnp.where(at_diag, first, rolled(0))
        elif v < 4:
            tile = jnp.where(at_diag, rolled(v - 1), rolled(v))
        elif v == 4:
            tile = jnp.where(at_diag, rolled(3), last)
        else:
            tile = jnp.broadcast_to(last, (LANES, LANES))
        tiles.append(tile)
    return jnp.concatenate(tiles, axis=1)


def row_sums(values):
    part = (
        values[:, :LANES]
        + values[:, LANES : 2 * LANES]
        + values[:, 2 * LANES : 3 * LANES]
        + values[:, 3 * LANES :]
    )
    high = part.astype(bf16)
    rest = (part - high.astype(f32)).astype(bf16)
    return dot_nn(jnp.concatenate([high, rest], axis=1), jnp.ones((2 * LANES, LANES), bf16))


def wide4(values):
    return jnp.concatenate([values] * BLOCKS, axis=1)


def fold_rows(grads, block, beyond, inside, pick_first, pick_last):
    zero = jnp.zeros((LANES, LANES), f32)
    near = {}
    low = []
    high = []
    for other in range(BLOCKS):
        v = other - block + 2
        tile = grads[:, other * LANES : (other + 1) * LANES]
        if v < 0:
            low.append(tile.astype(bf16))
        elif v > 4:
            high.append(tile.astype(bf16))
        else:
            near[v] = pltpu.roll(tile, 0, 1, stride=1, stride_axis=0)
        if v == 0:
            low.append(tile.astype(bf16) * inside)
        if v == 4:
            high.append(tile.astype(bf16) * (1 - inside))
    out = []
    for w in range(BLOCKS):
        if w in near or w + 1 in near:
            out.append(jnp.where(beyond, near.get(w + 1, zero), near.get(w, zero)))
        else:
            out.append(zero)
    if low:
        out[0] = out[0] + dot_nn(
            jnp.concatenate(low, axis=1), pick_first[: LANES * len(low), :]
        )
    if high:
        out[3] = out[3] + dot_nn(
            jnp.concatenate(high, axis=1), pick_last[: LANES * len(high), :]
        )
    return jnp.concatenate(out, axis=1)


def attend_part(
    segment,
    live,
    tokens,
    table,
    mix_weight,
    mix_copies,
    left_s,
    right_s,
    scale_row,
    rank_s,
    table_rank_s,
    shares_out,
    q_s,
    k_s,
    v_s,
    tq_s,
    tk_s,
    tr_s,
    context_s,
    shares_s,
    bias_s,
    across_s,
    work,
    sems,
    gather,
):
    row, lane = block_iotas()
    below = lane <= row
    flip = (row + lane == LANES - 1).astype(bf16)
    eye = (row == lane).astype(bf16)
    seg_row = segment[...]
    key_row = jnp.where(live[...] == 1, seg_row, -1)
    for a in range(BLOCKS):
        seg_col = jnp.broadcast_to(
            seg_row[:, a * LANES : (a + 1) * LANES].astype(f32), (LANES, LANES)
        ).T.astype(jnp.int32)
        for b in range(BLOCKS):
            same = seg_col == key_row[:, b * LANES : (b + 1) * LANES]
            if a == b:
                same = same | (row == lane)
            bias_s[a * LANES : (a + 1) * LANES, b * LANES : (b + 1) * LANES] = jnp.where(
                same, 0.0, masked_fill
            )
    for a in range(BLOCKS):
        tr_s[a * LANES : (a + 1) * LANES, :] = dot_nn(
            flip, table[(3 - a) * LANES : (4 - a) * LANES, :]
        ).astype(bf16)

    rank_s[...] = dot_nt(tokens[...], left_s[...])
    table_rank_s[...] = dot_nt(tr_s[...], left_s[...])
    low = (rank_s[...] * scale_row).astype(bf16)
    table_low = (table_rank_s[...] * scale_row).astype(bf16)

    def project(source, low, which, target):
        full = dot_nn(source, mix_weight[which]) + dot_nn(low * of_map(which), right_s[...])
        for p in range(PAIRS):
            target[p] = full[:, p * LANES : (p + 1) * LANES].astype(bf16)

    mix_copies[0].wait()
    project(tokens[...], low, 0, q_s)
    project(tr_s[...], table_low, 0, tq_s)
    mix_copies[1].wait()
    project(tokens[...], low, 1, k_s)
    project(tr_s[...], table_low, 1, tk_s)
    gather.forward_one(0)
    mix_copies[2].wait()
    project(tokens[...], low, 2, v_s)

    blocks = [slice(b * LANES, (b + 1) * LANES) for b in range(BLOCKS)]
    keys_s, queries_s, along_s, both_s = work[:4]
    context_part = work[4]

    def scores(p, which):
        mask = head_mask(which)
        keys_s[which][:, :ROWS] = dot_nt(k_s[p] * mask, tq_s[p])
        queries_s[which][:, :ROWS] = dot_nt(q_s[p] * mask, tk_s[p])

    def pick(p, which):
        for b, r in enumerate(blocks):
            values = pick_tiles(keys_s[which][r, :ROWS], b, below)
            high = values.astype(bf16)
            across_s[which, 0, r, :] = high
            across_s[which, 1, r, :] = (values - high.astype(f32)).astype(bf16)
            along_s[which][r, :ROWS] = pick_tiles(queries_s[which][r, :ROWS], b, below)

    def content(p, which):
        mask = head_mask(which)
        for r in blocks:
            both_s[which][r, :ROWS] = dot_nt(
                jnp.concatenate([q_s[p, r, :] * mask, eye, eye], axis=1),
                jnp.concatenate(
                    [k_s[p], across_s[which, 0, :, r], across_s[which, 1, :, r]], axis=1
                ),
            )

    def softmax(p, which):
        for first in range(0, BLOCKS, GROUP):
            rows = blocks[first : first + GROUP]
            totals = [
                both_s[which][r, :ROWS] + along_s[which][r, :ROWS] + bias_s[r, :] for r in rows
            ]
            peaks = [jnp.max(t, axis=1, keepdims=True) for t in totals]
            weights = [
                jnp.exp2((t - m) * (score_scale * log_two_e)) for t, m in zip(totals, peaks)
            ]
            inverses = [1.0 / jnp.sum(w, axis=1, keepdims=True) for w in weights]
            for r, w, inverse in zip(rows, weights, inverses):
                shares_s[p, which, r, :] = (w * inverse).astype(bf16)

    def mix(p, which):
        part = dot_nn(shares_s[p, which], v_s[p] * head_mask(which))
        if which == 0:
            context_part[:, :LANES] = part
        else:
            lanes = slice(p * LANES, (p + 1) * LANES)
            if not isinstance(p, int):
                lanes = pl.ds(pl.multiple_of(p * LANES, LANES), LANES)
            context_s[:, lanes] = (context_part[:, :LANES] + part).astype(bf16)

    stages = (mix, softmax, content, pick, scores)

    def step(base, extra, first=0, last=4):
        for n in range(first, last + 1):
            head = extra - (4 - n)
            stages[n](base + head // 2, head % 2)

    def give(p):
        pltpu.make_async_copy(shares_s.at[p], shares_out.at[p], sems.at[p]).start()

    for extra in range(4):
        if extra == 2:
            gather.forward_one(1)
        step(0, extra, first=4 - extra)

    def pair(base, carry):
        for at, forward, k in (
            (2, gather.forward_one, 2),
            (3, gather.forward_two, 0),
            (4, gather.forward_one, 3),
            (5, gather.forward_two, 1),
        ):

            @pl.when(base == at)
            def _():
                forward(k)

        step(base, 0)
        step(base, 1)
        give(base - 2)
        return carry

    lax.fori_loop(2, PAIRS, pair, 0)
    gather.forward_one(4)
    step(PAIRS, 0, last=3)
    gather.forward_two(2)
    step(PAIRS, 1, last=2)
    give(PAIRS - 2)
    step(PAIRS, 2, last=1)
    gather.forward_two(3)
    give(PAIRS - 1)
    step(PAIRS, 3, last=0)


def vmem():
    return pl.BlockSpec(memory_space=pltpu.VMEM)


def anywhere():
    return pl.BlockSpec(memory_space=pl.ANY)


def remote(source, target, send, recv, device):
    return pltpu.make_async_remote_copy(
        src_ref=source,
        dst_ref=target,
        send_sem=send,
        recv_sem=recv,
        device_id=device,
        device_id_type=pl.DeviceIdType.MESH,
    )


def hail(devices):
    barrier = pltpu.get_barrier_semaphore()
    for device in devices:
        pl.semaphore_signal(
            barrier, inc=1, device_id=device, device_id_type=pl.DeviceIdType.MESH
        )


def heard(devices):
    pl.semaphore_wait(pltpu.get_barrier_semaphore(), len(devices))


def greet(devices):
    hail(devices)
    heard(devices)


class Groups:
    def __init__(self, tensor_size, dp_size):
        self.near_size = tensor_size * 2
        self.far_size = dp_size // 2
        self.tensor = lax.axis_index("tensor")
        self.dp = lax.axis_index("dp")
        self.near = self.tensor * 2 + self.dp % 2
        self.far = self.dp // 2

    def near_index(self, step):
        return (self.near + step) % self.near_size

    def near_device(self, step):
        index = self.near_index(step)
        return {"dp": self.far * 2 + index % 2, "tensor": index // 2}

    def far_device(self, step):
        index = (self.far + step) % self.far_size
        return {"dp": index * 2 + self.dp % 2, "tensor": self.tensor}

    def partners(self):
        return [self.near_device(s) for s in range(1, self.near_size)] + [
            self.far_device(s) for s in range(1, self.far_size)
        ]


class Reduction:
    def __init__(self, groups, pack, arrived, crossed, out, sems):
        self.groups = groups
        self.pack = pack
        self.arrived = arrived
        self.crossed = crossed
        self.out = out
        self.send_one, self.recv_one, self.send_two, self.recv_two, self.send_three, self.recv_three = sems
        self.size = pack.shape[0] // groups.near_size

    def part(self, ref, index):
        return ref.at[pl.ds(index * self.size, self.size)]

    def scatter(self):
        g = self.groups
        return [
            remote(
                self.part(self.pack, g.near_index(s)),
                self.arrived.at[s - 1],
                self.send_one.at[s - 1],
                self.recv_one.at[s - 1],
                g.near_device(s),
            )
            for s in range(1, g.near_size)
        ]

    def cross(self):
        g = self.groups
        return [
            remote(
                self.crossed.at[g.far],
                self.crossed.at[g.far],
                self.send_two.at[s - 1],
                self.recv_two.at[s - 1],
                g.far_device(s),
            )
            for s in range(1, g.far_size)
        ]

    def gather(self):
        g = self.groups
        return [
            remote(
                self.part(self.out, g.near),
                self.part(self.out, g.near),
                self.send_three.at[s - 1],
                self.recv_three.at[s - 1],
                g.near_device(s),
            )
            for s in range(1, g.near_size)
        ]

    def start(self):
        for copy in self.scatter():
            copy.start()

    def middle(self):
        g = self.groups
        for copy in self.scatter():
            copy.wait_recv()
        total = self.pack[pl.ds(g.near * self.size, self.size)].astype(f32)
        for s in range(1, g.near_size):
            total = total + self.arrived[s - 1].astype(f32)
        self.crossed[g.far] = total.astype(self.crossed.dtype)
        for copy in self.cross():
            copy.start()

    def last(self):
        g = self.groups
        for copy in self.cross():
            copy.wait_recv()
        total = self.crossed[0].astype(f32)
        for s in range(1, g.far_size):
            total = total + self.crossed[s].astype(f32)
        self.out[pl.ds(g.near * self.size, self.size)] = total.astype(self.out.dtype)
        for copy in self.gather():
            copy.start()

    def finish(self):
        for copy in self.gather():
            copy.wait()
        for copy in self.scatter() + self.cross():
            copy.wait_send()


def reduction_scratch(tiles, near_size, far_size, kind):
    size = tiles // near_size
    near = (near_size - 1,)
    far = (max(far_size - 1, 1),)
    dma = pltpu.SemaphoreType.DMA
    return [
        pltpu.VMEM((near_size - 1, size, TILE, LANES), kind),
        pltpu.VMEM((far_size, size, TILE, LANES), kind),
        dma(near),
        dma(near),
        dma(far),
        dma(far),
        dma(near),
        dma(near),
    ]


class Gather:
    def __init__(self, size, sources, targets, sems):
        self.size = size
        self.far = size // 2
        self.sources = sources
        self.targets = targets
        self.across_s, self.across_r, self.pair_s, self.pair_r, self.one_s, self.one_r, self.two_s, self.two_r = sems[:8]
        self.whole_s, self.whole_r, self.small_s, self.small_r, self.own = sems[8:]
        self.tensor = lax.axis_index("tensor")
        self.dp = lax.axis_index("dp")
        self.bit = self.dp % 2
        self.pair = {"dp": self.dp + 1 - 2 * self.bit, "tensor": self.tensor}
        self.near = self.tensor + 1 - 2 * (self.tensor % 2)
        self.core = {"dp": self.dp, "tensor": self.near}

    def device(self, step):
        return {"dp": self.dp, "tensor": (self.tensor + step) % self.size}

    def partners(self):
        return [self.device(s) for s in range(1, self.size)] + [self.pair]

    def slot(self, order):
        first = self.tensor if isinstance(order, int) and order % 2 == 0 else None
        if first is None:
            first = self.tensor + (order % 2) * (self.near - self.tensor)
        return (first + self.size - 2 * (order // 2)) % self.size

    def rows(self, which, part, bit):
        count = self.sources[which].shape[0] // 6
        return pl.ds((2 * part + bit) * count, count)

    def across(self, s, k):
        which, part = k // 3, k % 3
        rows = self.rows(which, part, self.bit)
        return remote(
            self.sources[which].at[rows, :],
            self.targets[which].at[self.tensor, rows, :],
            self.across_s.at[s - 1, k],
            self.across_r.at[s - 1, k],
            self.device(2 * s),
        )

    def onward(self, s, k, bit, sends, recvs, device):
        which, part = k // 3, k % 3
        rows = self.rows(which, part, bit)
        ref = self.targets[which].at[self.slot(2 * s), rows, :]
        return remote(ref, ref, sends.at[s - 1, k], recvs.at[s - 1, k], device)

    def swap(self, s, k):
        return self.onward(s, k, self.bit, self.pair_s, self.pair_r, self.pair)

    def share_one(self, s, k):
        return self.onward(s, k, self.bit, self.one_s, self.one_r, self.core)

    def share_two(self, s, k):
        return self.onward(s, k, 1 - self.bit, self.two_s, self.two_r, self.core)

    def whole(self, which):
        return remote(
            self.sources[which],
            self.targets[which].at[self.tensor],
            self.whole_s.at[which],
            self.whole_r.at[which],
            self.core,
        )

    def small(self, s, which):
        return remote(
            self.sources[which],
            self.targets[which].at[self.tensor],
            self.small_s.at[s - 1, which - 2],
            self.small_r.at[s - 1, which - 2],
            self.device(s),
        )

    def keep(self, which):
        return pltpu.make_async_copy(
            self.sources[which], self.targets[which].at[self.tensor], self.own.at[which]
        )

    def start(self):
        for which in range(4):
            self.keep(which).start()
        greet(self.partners())
        for k in range(6):
            for s in range(1, self.far):
                self.across(s, k).start()
        for which in range(2):
            self.whole(which).start()
        for s in range(1, self.size):
            for which in (2, 3):
                self.small(s, which).start()

    def forward_one(self, k):
        for s in range(1, self.far):
            self.across(s, k).wait_recv()
            self.swap(s, k).start()
            self.share_one(s, k).start()

    def forward_two(self, k):
        for s in range(1, self.far):
            self.swap(s, k).wait_recv()
            self.share_two(s, k).start()

    def arrive(self, order):
        if order == 0:
            for which in range(4):
                self.keep(which).wait()
            for s in range(1, self.size):
                for which in (2, 3):
                    self.small(s, which).wait()
        elif order == 1:
            for which in range(2):
                self.whole(which).wait()
        elif order % 2 == 1:
            for k in range(6):
                self.share_one(order // 2, k).wait_recv()
                self.share_two(order // 2, k).wait_recv()

    def finish(self):
        for s in range(1, self.far):
            for k in range(6):
                self.across(s, k).wait_send()
                self.swap(s, k).wait_send()
                self.share_one(s, k).wait_send()
                self.share_two(s, k).wait_send()


def norm_parts(values):
    center = values - jnp.mean(values, axis=-1, keepdims=True)
    root = lax.rsqrt(jnp.mean(center * center, axis=-1, keepdims=True) + norm_eps)
    return center * root, root


def norm_back(scaled, unit, root):
    return root * (
        scaled
        - jnp.mean(scaled, axis=-1, keepdims=True)
        - unit * jnp.mean(scaled * unit, axis=-1, keepdims=True)
    )


def feed_part(
    tokens,
    cotangent,
    cotangent_copy,
    out_weight,
    out_copy,
    left_s,
    right_s,
    scale_row,
    gain,
    shift,
    expand_left_t,
    expand_right,
    shrink_left_t,
    shrink_right,
    feed_scale,
    layer_out,
    layer_copy,
    grad_first_out,
    grad_context_out,
    pack,
    expand_s,
    shrink_s,
    x_s,
    normed_s,
    hidden_s,
    act_s,
    slope_s,
    branch_s,
    context_s,
    one_s,
    two_s,
    pre_s,
    gather,
):
    chunks = expand_s.shape[0]
    pieces = expand_s.shape[2] // LANES
    hidden = expand_s.shape[2]

    def part_of(order):
        if hidden == WIDTH:
            return order, slice(None), slice(None)
        place = order * hidden % WIDTH
        if isinstance(order, int):
            return order * hidden // WIDTH, slice(None), slice(place, place + hidden)
        place = pl.multiple_of(place, LANES)
        return order * hidden // WIDTH, slice(None), pl.ds(place, hidden)

    pack[...] = jnp.zeros_like(pack)

    def keep(first, values):
        for j in range(values.shape[1] // LANES):
            pack[first + j, :RANK, :] = values[:, j * LANES : (j + 1) * LANES]

    lam_one = feed_scale[0:1, :]
    lam_two = feed_scale[1:2, :]
    step = LANES
    steps = ROWS // step

    out_copy.wait()
    gather.forward_one(5)
    out_rank = dot_nt(context_s[...], left_s[...])
    out_low = (out_rank * scale_row).astype(bf16) * of_map(3)
    x_s[...] = dot_nn(context_s[...], out_weight[...]) + dot_nn(out_low, right_s[...])

    def first_norm(i, carry):
        rows = pl.ds(i * step, step)
        values = tokens[rows, :].astype(f32) + x_s[rows, :]
        x_s[rows, :] = values
        unit, root = norm_parts(values)
        normed = unit * gain[0:1, :] + shift[0:1, :]
        normed_s[rows, :] = normed
        hidden_s[rows, :] = normed.astype(bf16)
        return carry

    lax.fori_loop(0, steps, first_norm, 0)
    gather.forward_two(4)

    one_rank = dot_nt(hidden_s[...], expand_left_t[...])
    one_low = (one_rank * lam_one).astype(bf16)
    def expanded(order):
        if order == min(2, chunks - 1):
            gather.forward_two(5)
        gather.arrive(order)
        c = gather.slot(order)
        pre_s[order % 2, :, :hidden] = dot_nn(hidden_s[...], expand_s[c]) + dot_nn(one_low, expand_right[c])

    two_rank = None
    expanded(0)
    for order in range(chunks):
        if order + 1 < chunks:
            expanded(order + 1)
        pre = pre_s[order % 2, :, :hidden]
        cdf = 0.5 + 0.5 * lax.erf(pre * inverse_root_two)
        act_s[part_of(order)] = (pre * cdf).astype(bf16)
        slope_s[part_of(order)] = cdf + pre * jnp.exp(-0.5 * pre * pre) * inverse_root_tau
        c = gather.slot(order)
        part = dot_nn(act_s[part_of(order)], shrink_s[c])
        branch_s[...] = part if order == 0 else branch_s[...] + part
        part = dot_nt(act_s[part_of(order)], shrink_left_t[c])
        two_s[...] = part if order == 0 else two_s[...] + part
    two_rank = two_s[...]
    gather.finish()
    two_low = (two_rank * lam_two).astype(bf16)
    branch_s[...] += dot_nn(two_low, shrink_right[...])

    cotangent_copy.wait()

    def second_norm(i, carry):
        rows = pl.ds(i * step, step)
        unit, root = norm_parts(normed_s[rows, :] + branch_s[rows, :])
        layer_out[rows, :] = (unit * gain[1:2, :] + shift[1:2, :]).astype(bf16)
        grad = norm_back(cotangent[rows, :].astype(f32) * gain[1:2, :], unit, root)
        branch_s[rows, :] = grad
        return carry

    lax.fori_loop(0, steps, second_norm, 0)
    layer_copy.start()
    grad_branch = branch_s[...].astype(bf16)
    two_back = dot_nt(grad_branch, shrink_right[...])
    two_small = (two_back * lam_two).astype(bf16)
    two_small_t = two_small.T
    one_low_t = one_low.T
    keep(18, dot_tn(two_low, grad_branch))
    pack[24, 5:6, :RANK] = jnp.sum(two_rank * two_back, axis=0, keepdims=True)

    one_s[...] = jnp.zeros_like(one_s)

    def backward(order, carry):
        c = gather.slot(order)
        here = part_of(order)
        grad_act = dot_nt(grad_branch, shrink_s[c]) + dot_nn(two_small, shrink_left_t[c])
        grad_pre = (grad_act * slope_s[here]).astype(bf16)
        keep(SPLIT_AT + (chunks + c) * pieces, dot_nn(two_small_t, act_s[here]))
        keep(SPLIT_AT + c * pieces, dot_nn(one_low_t, grad_pre))
        branch_s[...] += dot_nt(grad_pre, expand_s[c])
        one_s[...] += dot_nt(grad_pre, expand_right[c])
        return carry

    lax.fori_loop(0, chunks, backward, 0)
    one_back = one_s[...]
    one_small = (one_back * lam_one).astype(bf16)
    branch_s[...] += dot_nn(one_small, expand_left_t[...])
    keep(12, dot_tn(one_small, hidden_s[...]))
    pack[24, 4:5, :RANK] = jnp.sum(one_rank * one_back, axis=0, keepdims=True)

    def first_back(i, carry):
        rows = pl.ds(i * step, step)
        unit, root = norm_parts(x_s[rows, :])
        grad_first_out[rows, :] = norm_back(branch_s[rows, :] * gain[0:1, :], unit, root)
        return carry

    lax.fori_loop(0, steps, first_back, 0)
    grad_attended = grad_first_out[...].astype(bf16)
    out_back = dot_nt(grad_attended, right_s[...])
    out_small = (out_back * scale_row).astype(bf16) * of_map(3)
    grad_context = dot_nt(grad_attended, out_weight[...]) + dot_nn(out_small, left_s[...])
    for p in range(PAIRS):
        grad_context_out[p] = grad_context[:, p * LANES : (p + 1) * LANES].astype(bf16)
    keep(0, dot_tn(out_small, context_s[...])[3 * TILE : 3 * TILE + RANK, :])
    keep(6, dot_tn(out_low, grad_attended)[3 * TILE : 3 * TILE + RANK, :])
    pack[24, 3:4, :STACK] = jnp.sum(out_rank * out_back, axis=0, keepdims=True)


def front_kernel(
    segment,
    live,
    tokens,
    table,
    left_t,
    right,
    scale,
    gain,
    shift,
    expand_left_t,
    shrink_right,
    feed_scale,
    mix_weight,
    cotangent,
    out_weight,
    expand,
    shrink,
    expand_right,
    shrink_left_t,
    grad_first,
    grad_context,
    pack,
    layer_to,
    q_to,
    k_to,
    v_to,
    tq_to,
    tk_to,
    tr_to,
    left_to,
    right_to,
    rank_to,
    table_rank_to,
    shares_out,
    layer_s,
    q_s,
    k_s,
    v_s,
    tq_s,
    tk_s,
    tr_s,
    left_s,
    right_s,
    rank_s,
    table_rank_s,
    mix_s,
    cotangent_s,
    out_s,
    expand_s,
    shrink_s,
    expand_right_s,
    shrink_left_s,
    shares_s,
    bias_s,
    across_s,
    x_s,
    normed_s,
    hidden_s,
    act_s,
    slope_s,
    branch_s,
    context_s,
    one_s,
    two_s,
    pre_s,
    share_sems,
    load_sems,
    keep_sems,
    *gather_sems,
):
    mix_copies = [
        pltpu.make_async_copy(mix_weight.at[i], mix_s.at[i], load_sems.at[i]) for i in range(3)
    ]
    cotangent_copy = pltpu.make_async_copy(cotangent, cotangent_s, load_sems.at[3])
    out_copy = pltpu.make_async_copy(out_weight, out_s, load_sems.at[4])
    for copy in mix_copies:
        copy.start()
    gather = Gather(
        expand_s.shape[0],
        (expand, shrink, expand_right, shrink_left_t),
        (expand_s, shrink_s, expand_right_s, shrink_left_s),
        gather_sems,
    )
    gather.start()
    cotangent_copy.start()
    out_copy.start()
    left_s[...] = jnp.zeros_like(left_s)
    right_s[...] = jnp.zeros_like(right_s)
    for a in range(4):
        left_s[a * TILE : a * TILE + RANK, :] = left_t[:, a, :]
        right_s[a * TILE : a * TILE + RANK, :] = right[:, a, :]
    scale_row = spread(scale)
    attend_part(
        segment,
        live,
        tokens,
        table,
        mix_s,
        mix_copies,
        left_s,
        right_s,
        scale_row,
        rank_s,
        table_rank_s,
        shares_out,
        q_s,
        k_s,
        v_s,
        tq_s,
        tk_s,
        tr_s,
        context_s,
        shares_s,
        bias_s,
        across_s,
        (
            (slope_s.at[0], slope_s.at[1]),
            (slope_s.at[2], slope_s.at[3]),
            (pre_s.at[0], pre_s.at[1]),
            (x_s, normed_s),
            branch_s,
        ),
        share_sems,
        gather,
    )
    kept = [
        pltpu.make_async_copy(source, target, keep_sems.at[i])
        for i, (source, target) in enumerate(
            (
                (layer_s, layer_to),
                (q_s, q_to),
                (k_s, k_to),
                (v_s, v_to),
                (tq_s, tq_to),
                (tk_s, tk_to),
                (tr_s, tr_to),
                (left_s, left_to),
                (right_s, right_to),
                (rank_s, rank_to),
                (table_rank_s, table_rank_to),
            )
        )
    ]
    for copy in kept[1:]:
        copy.start()
    feed_part(
        tokens,
        cotangent_s,
        cotangent_copy,
        out_s,
        out_copy,
        left_s,
        right_s,
        scale_row,
        gain,
        shift,
        expand_left_t,
        expand_right_s,
        shrink_left_s,
        shrink_right,
        feed_scale,
        layer_s,
        kept[0],
        grad_first,
        grad_context,
        pack,
        expand_s,
        shrink_s,
        x_s,
        normed_s,
        hidden_s,
        act_s,
        slope_s,
        branch_s,
        context_s,
        one_s,
        two_s,
        pre_s,
        gather,
    )

    def finish(p, carry):
        pltpu.make_async_copy(shares_s.at[p], shares_out.at[p], share_sems.at[p]).wait()
        return carry

    lax.fori_loop(0, PAIRS, finish, 0)
    for copy in kept:
        copy.wait()


def front(size, tiles, *args):
    hidden = args[15].shape[1]
    wide = size * hidden // WIDTH
    piece = jax.ShapeDtypeStruct((PAIRS, ROWS, LANES), bf16)
    rows = jax.ShapeDtypeStruct((ROWS, WIDTH), bf16)
    dma = pltpu.SemaphoreType.DMA
    steps = (max(size // 2 - 1, 1), 6)
    stack = jax.ShapeDtypeStruct((STACK, WIDTH), bf16)
    rank = jax.ShapeDtypeStruct((ROWS, STACK), f32)
    kept = (rows, piece, piece, piece, piece, piece, rows, stack, stack, rank, rank)
    return pl.pallas_call(
        front_kernel,
        out_shape=(
            jax.ShapeDtypeStruct((ROWS, WIDTH), f32),
            piece,
            jax.ShapeDtypeStruct((tiles, TILE, LANES), f32),
        )
        + kept
        + (jax.ShapeDtypeStruct((PAIRS, 2, ROWS, ROWS), bf16),),
        in_specs=[vmem()] * 12 + [anywhere()] * 7,
        out_specs=(vmem(),) * 3 + (anywhere(),) * 12,
        scratch_shapes=[pltpu.VMEM(array.shape, array.dtype) for array in kept]
        + [
            pltpu.VMEM((3, WIDTH, WIDTH), bf16),
            pltpu.VMEM((ROWS, WIDTH), bf16),
            pltpu.VMEM((WIDTH, WIDTH), bf16),
            pltpu.VMEM((size, WIDTH, hidden), bf16),
            pltpu.VMEM((size, hidden, WIDTH), bf16),
            pltpu.VMEM((size, RANK, hidden), bf16),
            pltpu.VMEM((size, RANK, hidden), bf16),
            pltpu.VMEM((PAIRS, 2, ROWS, ROWS), bf16),
            pltpu.VMEM((ROWS, ROWS), f32),
            pltpu.VMEM((2, 2, ROWS, ROWS), bf16),
            pltpu.VMEM((ROWS, WIDTH), f32),
            pltpu.VMEM((ROWS, WIDTH), f32),
            pltpu.VMEM((ROWS, WIDTH), bf16),
            pltpu.VMEM((wide, ROWS, WIDTH), bf16),
            pltpu.VMEM((wide, ROWS, WIDTH), f32),
            pltpu.VMEM((ROWS, WIDTH), f32),
            pltpu.VMEM((ROWS, WIDTH), bf16),
            pltpu.VMEM((ROWS, RANK), f32),
            pltpu.VMEM((ROWS, RANK), f32),
            pltpu.VMEM((2, ROWS, WIDTH), f32),
            dma((PAIRS,)),
            dma((5,)),
            dma((len(kept),)),
        ]
        + [dma(steps)] * 8
        + [dma((2,))] * 2
        + [dma((size - 1, 2))] * 2
        + [dma((4,))],
        compiler_params=pltpu.CompilerParams(
            vmem_limit_bytes=60 * 2**20, collective_id=0, has_side_effects=True
        ),
        name="front",
    )(*args)


def back_kernel(
    left_s,
    right_s,
    rank_s,
    table_rank_s,
    scale,
    early,
    grad_context_in,
    q_in,
    k_in,
    v_in,
    tq_in,
    tk_in,
    tokens_in,
    tr_in,
    mix_in,
    grad_first_in,
    shares_in,
    grad_tokens,
    early_out,
    tail_out,
    grad_context,
    q_s,
    k_s,
    v_s,
    tq_s,
    tk_s,
    tokens,
    tr_s,
    mix_weight,
    grad_first,
    shares_s,
    gl_s,
    qf_s,
    kf_s,
    gq_s,
    gk_s,
    gt_s,
    grads_s,
    tables_s,
    tail,
    sems,
    load_sems,
    *reduce_refs,
):
    arrived, crossed = reduce_refs[0], reduce_refs[1]
    groups = Groups(arrived.shape[0] // 2 + 1, crossed.shape[0] * 2)
    first = Reduction(groups, early, arrived, crossed, early_out, reduce_refs[2:8])
    second = Reduction(groups, tail, reduce_refs[8], reduce_refs[9], tail_out, reduce_refs[10:16])
    row, lane = block_iotas()
    beyond = lane >= row
    inside = (row + lane <= LANES - 1).astype(bf16)
    ends = lax.broadcasted_iota(jnp.int32, (2 * LANES, LANES), 1)
    pick_first = (ends == 0).astype(bf16)
    pick_last = (ends == LANES - 1).astype(bf16)
    flip = (row + lane == LANES - 1).astype(bf16)

    needed = [
        pltpu.make_async_copy(source, target, load_sems.at[4 + i])
        for i, (source, target) in enumerate(
            (
                (grad_context_in, grad_context),
                (v_in, v_s),
                (q_in, q_s),
                (k_in, k_s),
                (tq_in, tq_s),
                (tk_in, tk_s),
            )
        )
    ]
    for copy in needed:
        copy.start()

    def begin(p, carry):
        pltpu.make_async_copy(shares_in.at[p], shares_s.at[p], sems.at[p]).start()
        return carry

    lax.fori_loop(0, PAIRS, begin, 0)
    loads = [
        pltpu.make_async_copy(source, target, load_sems.at[i])
        for i, (source, target) in enumerate(
            (
                (tokens_in, tokens),
                (tr_in, tr_s),
                (mix_in, mix_weight),
                (grad_first_in, grad_first),
            )
        )
    ]
    hail(groups.partners())
    for copy in loads:
        copy.start()
    for copy in needed:
        copy.wait()
    tail[...] = jnp.zeros_like(tail)
    scale_row = spread(scale)
    low = (rank_s[...] * scale_row).astype(bf16)
    table_low = (table_rank_s[...] * scale_row).astype(bf16)

    def keep(index, values):
        for j in range(values.shape[1] // LANES):
            tail[index + j] = values[:, j * LANES : (j + 1) * LANES].astype(bf16)

    def flipped(values):
        return jnp.concatenate(
            [
                dot_nn(flip, values[b * LANES : (b + 1) * LANES, :]).astype(bf16)
                for b in range(BLOCKS)
            ],
            axis=0,
        )

    def rows_of(group):
        return [
            slice(a * LANES, (a + 1) * LANES)
            for a in range(group * BACK_GROUP, (group + 1) * BACK_GROUP)
        ]

    def grads(p, which, group):
        rows = rows_of(group)
        every = slice(rows[0].start, rows[-1].stop)
        grad = dot_nt(grad_context[p, every, :] * head_mask(which), v_s[p])
        shares = [shares_s[p, which, r, :].astype(f32) for r in rows]
        prods = [
            grad[i * LANES : (i + 1) * LANES, :] * shares[i] for i in range(BACK_GROUP)
        ]
        inner = [jnp.sum(prod, axis=1, keepdims=True) for prod in prods]
        for i, r in enumerate(rows):
            gl_s[which, r, :] = (prods[i] - shares[i] * inner[i]).astype(bf16)

    def fold(which, group, target, turn):
        rows = rows_of(group)
        turned = [
            dot_nt(flip, gl_s[which, :, r]) if turn else dot_nn(flip, gl_s[which, r, :])
            for r in rows
        ]
        for t, r in zip(turned, rows):
            target[which, r, :ROWS] = t.astype(bf16)
        for i, r in enumerate(rows):
            target[which, r, ROWS:] = fold_rows(
                turned[i], group * BACK_GROUP + i, beyond, inside, pick_first, pick_last
            ).astype(bf16)

    def close(p, which, parts):
        gc_t, k_t, q_t, tk_t, tq_t, q_rev_t, k_rev_t = parts
        half = slice(which * 64, which * 64 + 64)
        gq_t = dot_nt(jnp.concatenate([k_t[half, :], tk_t[half, :]], axis=1), qf_s[which])
        gk_t = dot_nt(jnp.concatenate([q_t[half, :], tq_t[half, :]], axis=1), kf_s[which])
        gq_s[half, :] = (gq_t * score_scale).astype(bf16)
        gk_s[half, :] = (gk_t * score_scale).astype(bf16)
        gtk = dot_nn(q_rev_t[half, :], qf_s[which, :, ROWS:])
        gtq = dot_nn(k_rev_t[half, :], kf_s[which, :, ROWS:])
        gt_s[0, half, :] = (gtq * score_scale).astype(bf16)
        gt_s[1, half, :] = (gtk * score_scale).astype(bf16)
        gt_s[2, half, :] = dot_nn(gc_t[half, :], shares_s[p, which]).astype(bf16)

    sections = BLOCKS // BACK_GROUP
    pltpu.make_async_copy(shares_in.at[0], shares_s.at[0], sems.at[0]).wait()
    for group in range(sections):
        grads(0, 0, group)
    heard(groups.partners())
    first.start()

    def pair(p, carry):
        later = jnp.minimum(p + 1, PAIRS - 1)

        @pl.when(p < PAIRS - 1)
        def _():
            pltpu.make_async_copy(
                shares_in.at[later], shares_s.at[later], sems.at[later]
            ).wait()

        @pl.when(p == 2)
        def _():
            first.middle()

        @pl.when(p == 4)
        def _():
            first.last()

        parts = (
            grad_context[p].T,
            k_s[p].T,
            q_s[p].T,
            tk_s[p].T,
            tq_s[p].T,
            flipped(q_s[p]).T,
            flipped(k_s[p]).T,
        )
        for group in range(sections):
            fold(0, group, qf_s, False)
            grads(p, 1, group)
            fold(0, group, kf_s, True)
        close(p, 0, parts)
        for group in range(sections):
            fold(1, group, qf_s, False)
            grads(later, 0, group)
            fold(1, group, kf_s, True)
        close(p, 1, parts)
        lanes = pl.ds(pl.multiple_of(p * LANES, LANES), LANES)
        for b in range(BLOCKS):
            rows = slice(b * LANES, (b + 1) * LANES)
            grads_s[0, rows, lanes] = dot_nt(flip, gq_s[:, rows]).astype(bf16)
            grads_s[1, rows, lanes] = dot_nt(flip, gk_s[:, rows]).astype(bf16)
        grads_s[2, :, lanes] = gt_s[2].T
        tables_s[0, :, lanes] = gt_s[0].T
        tables_s[1, :, lanes] = gt_s[1].T
        return carry

    lax.fori_loop(0, PAIRS, pair, 0)

    for copy in loads:
        copy.wait()

    def backs(source, count):
        total = None
        lane = lax.broadcasted_iota(jnp.int32, (1, STACK), 1)
        for which in range(count):
            part = dot_nt(source[which], right_s[...])
            part = jnp.where(lane // TILE == which, part, 0.0)
            total = part if total is None else total + part
        return total

    back = backs(grads_s, 3)
    table_back = backs(tables_s, 2)
    small = (back * scale_row).astype(bf16)
    table_small = (table_back * scale_row).astype(bf16)
    left_sum = dot_tn(small, tokens[...]) + dot_tn(table_small, tr_s[...])
    low_t = low.T
    table_low_t = table_low.T
    for which in range(3):
        rows = slice(which * TILE, (which + 1) * TILE)
        right_sum = dot_nn(low_t[rows, :], grads_s[which])
        if which < 2:
            right_sum = right_sum + dot_nn(table_low_t[rows, :], tables_s[which])
        keep(which * 6, left_sum[rows, :])
        keep(18 + which * 6, right_sum)
    tail[36, :1, :STACK] = jnp.sum(
        rank_s[...] * back + table_rank_s[...] * table_back, axis=0, keepdims=True
    ).astype(bf16)
    first.finish()
    second.start()
    grad_tokens[...] = grad_first[...] + dot_nn(small, left_s[...])
    grad_tokens[...] += dot_nt(grads_s[0], mix_weight[0])
    second.middle()
    grad_tokens[...] += dot_nt(grads_s[1], mix_weight[1])
    second.last()
    grad_tokens[...] += dot_nt(grads_s[2], mix_weight[2])
    second.finish()


def back(tail_tiles, near_size, far_size, *args):
    early = args[5]
    piece = pltpu.VMEM((PAIRS, ROWS, LANES), bf16)
    return pl.pallas_call(
        back_kernel,
        out_shape=(
            jax.ShapeDtypeStruct((ROWS, WIDTH), f32),
            jax.ShapeDtypeStruct(early.shape, f32),
            jax.ShapeDtypeStruct((tail_tiles, TILE, LANES), bf16),
        ),
        in_specs=[vmem()] * 6 + [anywhere()] * 11,
        out_specs=(vmem(),) * 3,
        scratch_shapes=[piece] * 6
        + [
            pltpu.VMEM((ROWS, WIDTH), bf16),
            pltpu.VMEM((ROWS, WIDTH), bf16),
            pltpu.VMEM((3, WIDTH, WIDTH), bf16),
            pltpu.VMEM((ROWS, WIDTH), f32),
            pltpu.VMEM((PAIRS, 2, ROWS, ROWS), bf16),
            pltpu.VMEM((2, ROWS, ROWS), bf16),
            pltpu.VMEM((2, ROWS, 2 * ROWS), bf16),
            pltpu.VMEM((2, ROWS, 2 * ROWS), bf16),
            pltpu.VMEM((LANES, ROWS), bf16),
            pltpu.VMEM((LANES, ROWS), bf16),
            pltpu.VMEM((3, LANES, ROWS), bf16),
            pltpu.VMEM((3, ROWS, WIDTH), bf16),
            pltpu.VMEM((2, ROWS, WIDTH), bf16),
            pltpu.VMEM((tail_tiles, TILE, LANES), bf16),
            pltpu.SemaphoreType.DMA((PAIRS,)),
            pltpu.SemaphoreType.DMA((10,)),
        ]
        + reduction_scratch(early.shape[0], near_size, far_size, f32)
        + reduction_scratch(tail_tiles, near_size, far_size, bf16),
        compiler_params=pltpu.CompilerParams(
            vmem_limit_bytes=58 * 2**20, collective_id=1, has_side_effects=True
        ),
        name="back",
    )(*args)


def unpack_kernel(
    early,
    tail,
    tokens_in,
    layer_in,
    tokens_out,
    layer_out,
    left,
    scale,
    right,
    expand_left_t,
    expand_right,
    shrink_left_t,
    feed_scale,
    shrink_right,
    tokens_s,
    layer_s,
    sems,
):
    ins = []
    outs = []
    for i in range(4):
        rows = pl.ds(i * LANES, LANES)
        for n, (source, held, target) in enumerate(
            ((tokens_in, tokens_s, tokens_out), (layer_in, layer_s, layer_out))
        ):
            ins.append(
                pltpu.make_async_copy(source.at[rows, :], held.at[rows, :], sems.at[n, i])
            )
            outs.append(
                pltpu.make_async_copy(held.at[rows, :], target.at[rows, :], sems.at[2 + n, i])
            )
    for copy in ins:
        copy.start()
    for copy, onward in zip(ins, outs):
        copy.wait()
        onward.start()
    me = lax.axis_index("tensor")
    pieces = expand_right.shape[1] // LANES
    split = SPLIT_AT + me * pieces
    skip = (early.shape[0] - SPLIT_AT) // 2
    for j in range(WIDTH // LANES):
        lanes = slice(j * LANES, (j + 1) * LANES)
        for which in range(3):
            left[:, which, lanes] = tail[which * 6 + j, :RANK, :].astype(f32)
            right[:, which, lanes] = tail[18 + which * 6 + j, :RANK, :].astype(f32)
        left[:, 3, lanes] = early[j, :RANK, :]
        right[:, 3, lanes] = early[6 + j, :RANK, :]
        expand_left_t[:, lanes] = early[12 + j, :RANK, :]
        shrink_right[:, lanes] = early[18 + j, :RANK, :]
    total = lax.axis_size("tensor") * pieces
    for j in range(pieces):
        lanes = slice(j * LANES, (j + 1) * LANES)
        expand_right[:, lanes] = early[split + j, :RANK, :]
        shrink_left_t[:, lanes] = early[split + total + j, :RANK, :]
    mixed = tail[36].astype(f32)
    for which in range(3):
        scale[which : which + 1, :] = mixed[:1, which * TILE : which * TILE + RANK]
    other = early[24]
    scale[3:4, :] = other[3:4, 3 * TILE : 3 * TILE + RANK]
    feed_scale[...] = other[4:6, :RANK]
    for copy in outs:
        copy.wait()


def unpack(hidden, early, tail, tokens, layer):
    mats = jax.ShapeDtypeStruct((RANK, 4, WIDTH), f32)
    small = jax.ShapeDtypeStruct((RANK, WIDTH), f32)
    split = jax.ShapeDtypeStruct((RANK, hidden), f32)
    return pl.pallas_call(
        unpack_kernel,
        out_shape=(
            jax.ShapeDtypeStruct((ROWS, WIDTH), f32),
            jax.ShapeDtypeStruct((ROWS, WIDTH), bf16),
            mats,
            jax.ShapeDtypeStruct((4, RANK), f32),
            mats,
            small,
            split,
            split,
            jax.ShapeDtypeStruct((2, RANK), f32),
            small,
        ),
        in_specs=[vmem(), vmem(), anywhere(), anywhere()],
        out_specs=(anywhere(),) * 2 + (vmem(),) * 8,
        scratch_shapes=[
            pltpu.VMEM((ROWS, WIDTH), f32),
            pltpu.VMEM((ROWS, WIDTH), bf16),
            pltpu.SemaphoreType.DMA((4, 4)),
        ],
        name="unpack",
    )(early, tail, tokens, layer)


def body(
    tokens,
    segment,
    live,
    mix_weight,
    out_weight,
    position_table,
    norm_gain,
    norm_bias,
    mix_left,
    mix_scale,
    mix_right,
    expand_weight,
    expand_left,
    expand_right,
    shrink_weight,
    shrink_left,
    feed_scale,
    shrink_right,
    cotangent,
):
    tensor_size = lax.axis_size("tensor")
    near_size = tensor_size * 2
    far_size = lax.axis_size("dp") // 2
    hidden = expand_weight.shape[1]
    early_tiles = -(-(SPLIT_AT + 2 * tensor_size * hidden // LANES) // near_size) * near_size
    tail_tiles = -(-37 // near_size) * near_size
    left_t = jnp.transpose(mix_left, (2, 0, 1))
    right = jnp.transpose(mix_right, (1, 0, 2))
    grad_first, grad_context, early, layer_out, q, k, v, tq, tk, tr, *adapters, shares = front(
        tensor_size,
        early_tiles,
        segment.reshape(1, ROWS),
        live.reshape(1, ROWS),
        tokens,
        position_table,
        left_t,
        right,
        mix_scale,
        norm_gain,
        norm_bias,
        expand_left.T,
        shrink_right,
        feed_scale,
        mix_weight,
        cotangent,
        out_weight,
        expand_weight,
        shrink_weight,
        expand_right,
        shrink_left.T,
    )
    grad_tokens, early, tail = back(
        tail_tiles,
        near_size,
        far_size,
        *adapters,
        mix_scale,
        early,
        grad_context,
        q,
        k,
        v,
        tq,
        tk,
        tokens,
        tr,
        mix_weight,
        grad_first,
        shares,
    )
    (
        grad_tokens,
        layer_out,
        left,
        scale,
        right,
        expand_left,
        expand_right,
        shrink_left,
        feed_scale,
        shrink_right,
    ) = unpack(hidden, early, tail, grad_tokens, layer_out)
    return (
        layer_out,
        grad_tokens,
        jnp.transpose(left, (1, 2, 0)),
        scale,
        jnp.transpose(right, (1, 0, 2)),
        expand_left.T,
        expand_right,
        shrink_left.T,
        feed_scale,
        shrink_right,
    )


def solution(mesh):
    rows = P(("dp", "tensor"), None)
    line = P(("dp", "tensor"))
    return jax.shard_map(
        body,
        mesh=mesh,
        in_specs=(
            rows,
            line,
            line,
            P(),
            P(),
            P(),
            P(),
            P(),
            P(),
            P(),
            P(),
            P(None, "tensor"),
            P(),
            P(None, "tensor"),
            P("tensor", None),
            P("tensor", None),
            P(),
            P(),
            rows,
        ),
        out_specs=(
            rows,
            rows,
            P(),
            P(),
            P(),
            P(),
            P(None, "tensor"),
            P("tensor", None),
            P(),
            P(),
        ),
        check_vma=False,
    )
```
